128 devices in a mesh: ctx: 16 (over y, x_hi, core), tp: 8 (over x_lo, z).
Axes of the slice: x: 4 (x_hi: 2, x_lo: 2; x = x_hi * 2 + x_lo), y: 4, z: 4, core: 2. Of those that a mesh axis runs over, the one named last changes fastest.
Arguments:
- inputs: bfloat16 [2048, 4096], P('ctx', 'tp'), may hold values from -6 to 6
- residue: float32 [4096, 16], P('tp'), may hold values from -1.5 to 1.5
- log_rate: float32 [4096, 16], P('tp'), may hold values from -1 to 6.5
- skip: float32 [4096], P('tp'), may hold values from 0.5 to 1.5
- out_weight: bfloat16 [4096, 8192], P('tp'), may hold values from -0.09375 to 0.09375
- out_grad: bfloat16 [2048, 8192], P(('ctx', 'tp')), may hold values from -6 to 6
Outputs:
- out: bfloat16 [2048, 8192], P(('ctx', 'tp'))
- grad_input: bfloat16 [2048, 4096], P('ctx', 'tp')
- grad_residue: float32 [4096, 16], P('tp')
- grad_log_rate: float32 [4096, 16], P('tp')
- grad_skip: float32 [4096], P('tp')
The draws below stay inside these ranges and needn't reach their ends.
All inputs are finite; a program needn't handle non-finite values.
Results may differ from the reference program's by a relative error of at most 0.02.
Values may be sent and summed in bfloat16 or wider, within the bound.
A program may use at most 128 MiB of HBM per device.

```python
import math
import jax
import jax.numpy as jnp
from jax import lax

CH_DEV = 512
DIM = 8192
MODES = 16
SEQ = 2048
CHANNELS = 4096


def draw_log_rate(key, part):
    key = jax.random.fold_in(key, 7)
    first = jax.random.fold_in(key, 0)
    return jax.random.uniform(first, (CHANNELS, MODES), jnp.float32, -1.0, 6.5)


def block_scale(own_key, shape, shards, smallest, high):
    def one(axis_at, parts):
        steps = jax.random.uniform(jax.random.fold_in(jax.random.fold_in(own_key, 6), axis_at), (parts,), jnp.float32, smallest / len(shards), high / len(shards))
        return jnp.repeat(jnp.exp(steps), shape[axis_at] // parts).reshape((-1,) + (1,) * (len(shape) - axis_at - 1))

    factor_of = one(*shards[0])
    for cut in shards[1:]:
        factor_of = factor_of * one(*cut)
    return factor_of


def normal_values(key, shape, scale, most, shards=(), held_as=jnp.bfloat16):
    values = scale * jax.random.normal(key, shape, jnp.float32)
    if shards:
        values = values * block_scale(key, shape, shards, -0.22, 0.18)
    return jnp.clip(values, -most, most).astype(held_as)


def setup_inputs(seed: int = 0) -> dict:
    key_of = jax.random.split(jax.random.key(seed), 7)
    inputs = normal_values(key_of[0], (SEQ, CHANNELS), 1.0, 6.0, ((0, 16), (1, 8)))
    residue = normal_values(key_of[1], (CHANNELS, MODES), 0.25, 1.5, ((0, 8),), jnp.float32)
    log_rate = draw_log_rate(jax.random.fold_in(key_of[6], 71), 0)
    skip = jnp.clip(1.0 + 0.1 * jax.random.normal(key_of[3], (CHANNELS,), jnp.float32), 0.5, 1.5)
    out_weight = normal_values(key_of[4], (CHANNELS, DIM), CHANNELS ** -0.5, 0.09375, ((0, 8),))
    out_grad = normal_values(key_of[5], (SEQ, DIM), 1.0, 6.0, ((0, 128),))
    return {"inputs": inputs, "residue": residue, "log_rate": log_rate, "skip": skip, "out_weight": out_weight, "out_grad": out_grad}


def reference(inputs, residue, log_rate, skip, out_weight, out_grad):
    x = inputs.astype(jnp.float32)
    places = jnp.arange(SEQ).astype(jnp.float32)
    rate = jnp.exp(log_rate) / SEQ
    filt = jnp.zeros(x.shape, jnp.float32)
    for mode in range(MODES):
        rate_n = rate[:, mode][None, :]
        basis_n = jnp.sqrt(2.0 * rate_n) * jnp.exp(-(rate_n * places[:, None]))
        filt = filt + residue[:, mode][None, :] * basis_n
    length = 2 * SEQ
    spec_x = jnp.fft.rfft(x, n=length, axis=0)
    spec_f = jnp.fft.rfft(filt, n=length, axis=0)
    conv = jnp.fft.irfft(spec_x * spec_f, n=length, axis=0)[:SEQ]
    merged = (conv + skip[None, :] * x).astype(jnp.bfloat16)
    total = jnp.zeros((SEQ, DIM), jnp.float32)
    for group in range(CHANNELS // CH_DEV):
        block = merged[:, group * CH_DEV:(group + 1) * CH_DEV]
        weights = out_weight[group * CH_DEV:(group + 1) * CH_DEV]
        partial_sum = jnp.dot(block, weights, preferred_element_type=jnp.float32).astype(jnp.bfloat16)
        total = total + lax.optimization_barrier(partial_sum).astype(jnp.float32)
    out = total.astype(jnp.bfloat16)
    grad_merged = lax.dot_general(out_grad, out_weight, (((1,), (1,)), ((), ())), preferred_element_type=jnp.float32).astype(jnp.bfloat16)
    g = grad_merged.astype(jnp.float32)
    spec_g = jnp.fft.rfft(g, n=length, axis=0)
    back_conv = jnp.fft.irfft(spec_g * jnp.conj(spec_f), n=length, axis=0)[:SEQ]
    grad_input = (back_conv + skip[None, :] * g).astype(jnp.bfloat16)
    filt_grad = jnp.fft.irfft(spec_g * jnp.conj(spec_x), n=length, axis=0)[:SEQ]
    res_cols = []
    log_cols = []
    for mode in range(MODES):
        rate_n = rate[:, mode][None, :]
        basis_n = jnp.sqrt(2.0 * rate_n) * jnp.exp(-(rate_n * places[:, None]))
        weighted = filt_grad * basis_n
        res_cols.append(lax.optimization_barrier(jnp.sum(weighted, axis=0)))
        log_cols.append(lax.optimization_barrier(jnp.sum(weighted * residue[:, mode][None, :] * (0.5 - rate_n * places[:, None]), axis=0)))
    scale = math.sqrt(SEQ)
    grad_residue = jnp.stack(res_cols, axis=1) / scale
    grad_log_rate = jnp.stack(log_cols, axis=1) / scale
    grad_skip = lax.optimization_barrier(jnp.sum(g * x, axis=0)) / scale
    return (out, grad_input, grad_residue, grad_log_rate, grad_skip)
```

```python
import functools
import math

import jax
import jax.numpy as jnp
from jax import lax
from jax.experimental import pallas as pl
from jax.experimental.pallas import tpu as pltpu
from jax.sharding import PartitionSpec as P

MESH = pl.DeviceIdType.MESH
F32 = jnp.float32
BF16 = jnp.bfloat16
SUB = 8
LANE = 128
NX, NZ = 2, 4


def kernel(
    seq,
    n_ctx,
    x_ref,
    res_ref,
    lr_ref,
    skip_ref,
    w_hbm,
    og_hbm,
    out_ref,
    gi_ref,
    gres_ref,
    glog_ref,
    gskip_ref,
    w_v,
    og,
    part,
    hall,
    x32,
    y32,
    g32,
    gacc,
    mb,
    rate_t,
    c_t,
    rate8,
    a8,
    c8,
    ex8,
    in8,
    st_t,
    s_send,
    s_recv,
    r_send,
    r_recv,
    g8,
    m8,
    k8,
    red,
    rr,
    fin,
    bx1,
    bl1,
    br1,
    bl2,
    br2,
    bx3,
    al1,
    ar1,
    al2,
    ar2,
    w_sem,
    own_sem,
    ag_s,
    ag_r,
    rs_s,
    rs_r,
    s_ss,
    s_rs,
    r_ss,
    r_rs,
    p_ss,
    p_rs,
    q_ss,
    q_rs,
):
    tok, chans = x_ref.shape
    modes = res_ref.shape[1]
    dim = w_v.shape[1]
    rows = tok // (NX * NZ)
    steps = tok // SUB
    lanes = chans // LANE
    half, quarter = dim // 2, dim // 4
    col_block = min(1024, half)
    n_blocks = dim // col_block

    me = lax.axis_index("ctx")
    tp = lax.axis_index("tp")
    xl, z = tp // NZ, lax.rem(tp, NZ)
    ox = 1 - xl
    zr, zl, zo = lax.rem(z + 1, NZ), lax.rem(z + 3, NZ), lax.rem(z + 2, NZ)
    to_x = {"tp": ox * NZ + z}
    to_r = {"tp": xl * NZ + zr}
    to_l = {"tp": xl * NZ + zl}

    def cols(block):
        return pl.ds(pl.multiple_of(block * col_block, col_block), col_block)

    def w_copy(block):
        return pltpu.make_async_copy(
            w_hbm.at[:, cols(block)], w_v.at[:, cols(block)], w_sem.at[block]
        )

    own = pltpu.make_async_copy(og_hbm, og.at[xl, z], own_sem)
    own.start()

    @pl.loop(0, n_blocks)
    def _(block):
        w_copy(block).start()

    barrier = pltpu.get_barrier_semaphore()
    for peer in (to_x, to_r, to_l):
        pl.semaphore_signal(barrier, inc=1, device_id=peer, device_id_type=MESH)

    @pl.loop(1, n_ctx)
    def _(k):
        pl.semaphore_signal(
            barrier, inc=1, device_id={"ctx": lax.rem(me + k, n_ctx)}, device_id_type=MESH
        )

    pl.semaphore_wait(barrier, n_ctx + 2)

    def ag(index, src, dst, peer):
        return pltpu.make_async_remote_copy(
            src_ref=src,
            dst_ref=dst,
            send_sem=ag_s.at[index],
            recv_sem=ag_r.at[index],
            device_id=peer,
            device_id_type=MESH,
        )

    def relay(index, shard_x, shard_z, columns, peer):
        piece = og.at[shard_x, shard_z, :, columns]
        return ag(index, piece, piece, peer)

    all_a, all_b = pl.ds(0, half), pl.ds(half, half)
    a1, a2 = pl.ds(0, quarter), pl.ds(quarter, quarter)
    b1, b2 = pl.ds(half, quarter), pl.ds(half + quarter, quarter)

    first = [ag(i, og_hbm, og.at[xl, z], p) for i, p in enumerate((to_x, to_r, to_l))]
    for copy in first:
        copy.start()
    second = [
        relay(3, ox, z, all_a, to_r),
        relay(4, ox, z, all_a, to_l),
        relay(5, xl, zl, b1, to_r),
        relay(6, xl, zr, b2, to_l),
        relay(7, xl, zl, all_b, to_x),
        relay(8, xl, zr, all_b, to_x),
        relay(9, xl, zl, a1, to_r),
        relay(10, xl, zr, a2, to_l),
    ]
    third = [
        relay(11, xl, zo, all_b, to_x),
        relay(12, ox, zl, a1, to_r),
        relay(13, ox, zr, a2, to_l),
    ]

    lr_t = jnp.transpose(lr_ref[...])
    rate = jnp.exp(lr_t) / seq
    rate_t[...] = rate
    c_t[...] = jnp.transpose(res_ref[...]) * jnp.sqrt(2.0 * rate)
    for n in range(modes):
        row = pl.ds(n, 1)
        rate8[n] = jnp.broadcast_to(rate_t[row, :], (SUB, chans))
        c8[n] = jnp.broadcast_to(c_t[row, :], (SUB, chans))
    a8[...] = jnp.exp(-rate8[...])

    def lane(k):
        return pl.ds(k * LANE, LANE)

    for k in range(lanes):
        x32[k] = x_ref[:, lane(k)].astype(F32)

    place = lax.broadcasted_iota(jnp.int32, (modes, SUB, LANE), 1)
    place_f = place.astype(F32)
    span = float(steps)

    def at_step(ref, i, k):
        return ref[k, pl.ds(i, SUB, stride=steps), :]

    for k in range(lanes):
        a = a8[:, :, lane(k)]

        def grow(i, h, a=a, k=k):
            return a * h + at_step(x32, i, k)[None]

        end = lax.fori_loop(0, steps, grow, jnp.zeros((modes, SUB, LANE), F32), unroll=4)
        rk = rate8[:, :, lane(k)]
        for s in (1, 2, 4):
            moved = jnp.where(place >= s, pltpu.roll(end, s, 1), 0.0)
            end = end + jnp.exp(-(span * s) * rk) * moved
        ex8[:, :, lane(k)] = jnp.where(place >= 1, pltpu.roll(end, 1, 1), 0.0)
        s_send[:, lane(k)] = jnp.sum(jnp.where(place == SUB - 1, end, 0.0), axis=1)

    def ctx_copy(src, dst, sends, recvs, peer, sender):
        return pltpu.make_async_remote_copy(
            src_ref=src,
            dst_ref=dst,
            send_sem=sends.at[peer],
            recv_sem=recvs.at[sender],
            device_id={"ctx": peer},
            device_id_type=MESH,
        )

    def s_copy(peer, sender):
        return ctx_copy(s_send, s_recv.at[sender], s_ss, s_rs, peer, sender)

    def r_copy(peer, sender):
        return ctx_copy(r_send, r_recv.at[sender], r_ss, r_rs, peer, sender)

    @pl.loop(me + 1, n_ctx)
    def _(peer):
        s_copy(peer, me).start()

    for copy in first:
        copy.wait_recv()
    for copy in second:
        copy.start()

    far = jnp.exp(-float(tok) * rate_t[...])

    def join(sender, total):
        s_copy(0, sender).wait_recv()
        return far * total + s_recv[sender]

    st_t[...] = lax.fori_loop(0, me, join, jnp.zeros((modes, chans), F32))
    for n in range(modes):
        in8[n] = jnp.broadcast_to(st_t[pl.ds(n, 1), :], (SUB, chans))

    for k in range(lanes):
        a, c = a8[:, :, lane(k)], c8[:, :, lane(k)]
        skip = skip_ref[:, lane(k)]
        start = ex8[:, :, lane(k)] + jnp.exp(-span * place_f * rate8[:, :, lane(k)]) * in8[
            :, :, lane(k)
        ]

        def emit(i, h, a=a, c=c, skip=skip, k=k):
            now = at_step(x32, i, k)
            h = a * h + now[None]
            hall[i, :, :, lane(k)] = h
            y32[k, pl.ds(i, SUB, stride=steps), :] = jnp.sum(c * h, axis=0) + skip * now
            return h

        lax.fori_loop(0, steps, emit, start, unroll=2)
        mb[:, lane(k)] = y32[k].astype(BF16)

    for copy in second[:4]:
        copy.wait_recv()
    for copy in third:
        copy.start()

    def rs(index, src, dst, peer):
        return pltpu.make_async_remote_copy(
            src_ref=src,
            dst_ref=dst,
            send_sem=rs_s.at[index],
            recv_sem=rs_r.at[index],
            device_id=peer,
            device_id_type=MESH,
        )

    def project(block):
        w_copy(block).wait()
        p = jnp.dot(mb[...], w_v[:, cols(block)], preferred_element_type=F32)
        part[:, :, :, cols(block)] = p.astype(BF16).reshape(NX, NZ, rows, col_block)

    pl.loop(0, n_blocks // 2)(project)
    rs_x1 = rs(0, part.at[ox, :, :, all_a], bx1, to_x)
    rs_x1.start()
    pl.loop(n_blocks // 2, n_blocks)(project)
    rs_l1 = rs(1, part.at[:, zo, :, b1], bl1, to_r)
    rs_r1 = rs(2, part.at[:, zo, :, b2], br1, to_l)
    rs_l1.start()
    rs_r1.start()

    for copy in second[4:] + third:
        copy.wait_recv()
    own.wait()

    gacc[...] = jnp.zeros_like(gacc)

    @pl.loop(0, n_blocks)
    def _(block):
        gacc[...] += lax.dot_general(
            og[:, :, :, cols(block)].reshape(tok, col_block),
            w_v[:, cols(block)],
            (((1,), (1,)), ((), ())),
            preferred_element_type=F32,
        )

    for k in range(lanes):
        g32[k] = gacc[:, lane(k)].astype(BF16).astype(F32)
        a = a8[:, :, lane(k)]

        def back(i, h, a=a, k=k):
            return a * h + at_step(g32, steps - 1 - i, k)[None]

        end = lax.fori_loop(0, steps, back, jnp.zeros((modes, SUB, LANE), F32), unroll=4)
        rk = rate8[:, :, lane(k)]
        for s in (1, 2, 4):
            moved = jnp.where(place < SUB - s, pltpu.roll(end, SUB - s, 1), 0.0)
            end = end + jnp.exp(-(span * s) * rk) * moved
        ex8[:, :, lane(k)] = jnp.where(place < SUB - 1, pltpu.roll(end, SUB - 1, 1), 0.0)
        r_send[:, lane(k)] = jnp.sum(jnp.where(place == 0, end, 0.0), axis=1)

    @pl.loop(0, me)
    def _(peer):
        r_copy(peer, me).start()

    def merge(ref, got):
        ref[...] = (ref[...].astype(F32) + got[...].astype(F32)).astype(BF16)

    rs_x1.wait_recv()
    merge(part.at[xl, zo, :, all_a], bx1.at[zo])
    rs_al1 = rs(3, part.at[xl, zo, :, a1], al1, to_r)
    rs_ar1 = rs(4, part.at[xl, zo, :, a2], ar1, to_l)
    rs_al1.start()
    rs_ar1.start()
    rs_l1.wait_recv()
    merge(part.at[:, zr, :, b1], bl1)
    rs_l2 = rs(5, part.at[:, zr, :, all_b], bl2, to_r)
    rs_l2.start()
    rs_r1.wait_recv()
    merge(part.at[:, zl, :, b2], br1)
    rs_r2 = rs(6, part.at[:, zl, :, all_b], br2, to_l)
    rs_r2.start()
    merge(part.at[xl, zr, :, all_a], bx1.at[zr])
    merge(part.at[xl, zl, :, all_a], bx1.at[zl])

    def join_back(j, total):
        sender = n_ctx - 1 - j
        r_copy(0, sender).wait_recv()
        return far * total + r_recv[sender]

    st_t[...] = lax.fori_loop(
        0, n_ctx - 1 - me, join_back, jnp.zeros((modes, chans), F32)
    )
    for n in range(modes):
        in8[n] = jnp.broadcast_to(st_t[pl.ds(n, 1), :], (SUB, chans))

    rs_al1.wait_recv()
    merge(part.at[xl, zr, :, a1], al1)
    rs_al2 = rs(7, part.at[xl, zr, :, all_a], al2, to_r)
    rs_al2.start()
    rs_ar1.wait_recv()
    merge(part.at[xl, zl, :, a2], ar1)
    rs_ar2 = rs(8, part.at[xl, zl, :, all_a], ar2, to_l)
    rs_ar2.start()

    for k in range(lanes):
        a, c = a8[:, :, lane(k)], c8[:, :, lane(k)]
        skip = skip_ref[:, lane(k)]
        start = ex8[:, :, lane(k)] + jnp.exp(
            -span * (SUB - 1.0 - place_f) * rate8[:, :, lane(k)]
        ) * in8[:, :, lane(k)]
        g8[:, :, lane(k)] = jnp.zeros((modes, SUB, LANE), F32)
        m8[:, :, lane(k)] = jnp.zeros((modes, SUB, LANE), F32)

        def emit_back(j, carry, a=a, c=c, skip=skip, k=k):
            h, sk = carry
            i = steps - 1 - j
            now = at_step(g32, i, k)
            h = a * h + now[None]
            y32[k, pl.ds(i, SUB, stride=steps), :] = jnp.sum(c * h, axis=0) + skip * now
            held = hall[i, :, :, lane(k)]
            g8[:, :, lane(k)] += now[None] * held
            m8[:, :, lane(k)] += h * held
            return h, sk + now * at_step(x32, i, k)

        _, sk = lax.fori_loop(
            0, steps, emit_back, (start, jnp.zeros((SUB, LANE), F32)), unroll=2
        )
        red[:, pl.ds(k, 1), :] = jnp.sum(g8[:, :, lane(k)], axis=1, keepdims=True)
        red[:, pl.ds(lanes + k, 1), :] = jnp.sum(m8[:, :, lane(k)], axis=1, keepdims=True)
        sk = jnp.sum(sk, axis=0, keepdims=True)
        red[:, pl.ds(2 * lanes + k, 1), :] = jnp.broadcast_to(sk[None], (modes, 1, LANE))

    def p_copy(peer, sender):
        return ctx_copy(red.at[peer], rr.at[sender], p_ss, p_rs, peer, sender)

    def q_copy(peer, sender):
        return ctx_copy(fin.at[sender], fin.at[sender], q_ss, q_rs, peer, sender)

    def others(step):
        pl.loop(1, n_ctx)(lambda k: step(lax.rem(me + k, n_ctx)))

    others(lambda peer: p_copy(peer, me).start())
    for k in range(lanes):
        gi_ref[:, lane(k)] = y32[k].astype(BF16)
    rr[me] = red[me]

    rs_l2.wait_recv()
    rs_r2.wait_recv()

    def total3(ref, left, right):
        return ref[...].astype(F32) + left[...].astype(F32) + right[...].astype(F32)

    far_part = part.at[ox, z, :, all_b]
    far_part[...] = total3(far_part, bl2.at[ox], br2.at[ox]).astype(BF16)
    rs_x3 = rs(9, far_part, bx3, to_x)
    rs_x3.start()

    others(lambda peer: p_copy(0, peer).wait_recv())
    total = lax.fori_loop(1, n_ctx, lambda c, t: t + rr[c], rr[0])
    fin[me] = total[: 2 * lanes]
    others(lambda peer: q_copy(peer, me).start())
    scale = 1.0 / math.sqrt(seq)
    gskip_ref[...] = total[2 * lanes : 3 * lanes] * scale

    rs_al2.wait_recv()
    rs_ar2.wait_recv()
    out_ref[:, all_a] = (
        total3(part.at[xl, z, :, all_a], al2, ar2) + bx1[z].astype(F32)
    ).astype(BF16)
    rs_x3.wait_recv()
    out_ref[:, all_b] = (
        total3(part.at[xl, z, :, all_b], bl2.at[xl], br2.at[xl]) + bx3[...].astype(F32)
    ).astype(BF16)

    others(lambda peer: q_copy(0, peer).wait_recv())
    for k in range(lanes):
        rate = rate_t[:, lane(k)]
        gr = jnp.sum(fin[:, pl.ds(k, 1), :], axis=1)
        ml = jnp.sum(fin[:, pl.ds(lanes + k, 1), :], axis=1)
        here = pl.ds(k * LANE, LANE)
        gres_ref[here, :] = jnp.transpose(gr * (jnp.sqrt(2.0 * rate) * scale))
        glog_ref[here, :] = jnp.transpose(
            c_t[:, lane(k)] * ((0.5 + rate) * gr - rate * ml) * scale
        )

    for copy in first + second + third:
        copy.wait_send()
    for copy in (rs_x1, rs_l1, rs_r1, rs_al1, rs_ar1, rs_l2, rs_r2, rs_al2, rs_ar2, rs_x3):
        copy.wait_send()

    @pl.loop(me + 1, n_ctx)
    def _(peer):
        s_copy(peer, me).wait_send()

    @pl.loop(0, me)
    def _(peer):
        r_copy(peer, me).wait_send()

    others(lambda peer: p_copy(peer, me).wait_send())
    others(lambda peer: q_copy(peer, me).wait_send())


def per_device(inputs, residue, log_rate, skip, out_weight, out_grad):
    n_ctx = lax.axis_size("ctx")
    tok, chans = inputs.shape
    modes = residue.shape[1]
    dim = out_weight.shape[1]
    rows = tok // (NX * NZ)
    steps = tok // SUB
    lanes = chans // LANE
    half, quarter = dim // 2, dim // 4
    n_blocks = dim // min(1024, half)
    wide = (modes, SUB, chans)
    flat = (modes, chans)
    packed = -(-3 * lanes // SUB) * SUB
    vmem = pl.BlockSpec(memory_space=pltpu.VMEM)
    hbm = pl.BlockSpec(memory_space=pl.ANY)
    dma = pltpu.SemaphoreType.DMA
    out, gi, gres, glog, gskip = pl.pallas_call(
        functools.partial(kernel, tok * n_ctx, n_ctx),
        out_shape=(
            jax.ShapeDtypeStruct((rows, dim), BF16),
            jax.ShapeDtypeStruct((tok, chans), BF16),
            jax.ShapeDtypeStruct((chans, modes), F32),
            jax.ShapeDtypeStruct((chans, modes), F32),
            jax.ShapeDtypeStruct((lanes, LANE), F32),
        ),
        in_specs=[vmem, vmem, vmem, vmem, hbm, hbm],
        out_specs=(vmem,) * 5,
        scratch_shapes=[
            pltpu.VMEM((chans, dim), BF16),
            pltpu.VMEM((NX, NZ, rows, dim), BF16),
            pltpu.VMEM((NX, NZ, rows, dim), BF16),
            pltpu.VMEM((steps, *wide), F32),
            pltpu.VMEM((lanes, tok, LANE), F32),
            pltpu.VMEM((lanes, tok, LANE), F32),
            pltpu.VMEM((lanes, tok, LANE), F32),
            pltpu.VMEM((tok, chans), F32),
            pltpu.VMEM((tok, chans), BF16),
            pltpu.VMEM(flat, F32),
            pltpu.VMEM(flat, F32),
            pltpu.VMEM(wide, F32),
            pltpu.VMEM(wide, F32),
            pltpu.VMEM(wide, F32),
            pltpu.VMEM(wide, F32),
            pltpu.VMEM(wide, F32),
            pltpu.VMEM(flat, F32),
            pltpu.VMEM(flat, F32),
            pltpu.VMEM((n_ctx, *flat), F32),
            pltpu.VMEM(flat, F32),
            pltpu.VMEM((n_ctx, *flat), F32),
            pltpu.VMEM(wide, F32),
            pltpu.VMEM(wide, F32),
            pltpu.VMEM((SUB, chans), F32),
            pltpu.VMEM((modes, packed, LANE), F32),
            pltpu.VMEM((n_ctx, packed, LANE), F32),
            pltpu.VMEM((n_ctx, 2 * lanes, LANE), F32),
            pltpu.VMEM((NZ, rows, half), BF16),
            pltpu.VMEM((NX, rows, quarter), BF16),
            pltpu.VMEM((NX, rows, quarter), BF16),
            pltpu.VMEM((NX, rows, half), BF16),
            pltpu.VMEM((NX, rows, half), BF16),
            pltpu.VMEM((rows, half), BF16),
            pltpu.VMEM((rows, quarter), BF16),
            pltpu.VMEM((rows, quarter), BF16),
            pltpu.VMEM((rows, half), BF16),
            pltpu.VMEM((rows, half), BF16),
            dma((n_blocks,)),
            dma,
            dma((14,)),
            dma((14,)),
            dma((10,)),
            dma((10,)),
            *[dma((n_ctx,)) for _ in range(8)],
        ],
        compiler_params=pltpu.CompilerParams(
            collective_id=0, has_side_effects=True, vmem_limit_bytes=48 * 1024 * 1024
        ),
    )(inputs, residue, log_rate, skip.reshape(1, chans), out_weight, out_grad)
    return out, gi, gres, glog, gskip.reshape(chans)


def solution(mesh):
    return jax.shard_map(
        per_device,
        mesh=mesh,
        in_specs=(
            P("ctx", "tp"),
            P("tp", None),
            P("tp", None),
            P("tp"),
            P("tp", None),
            P(("ctx", "tp"), None),
        ),
        out_specs=(P(("ctx", "tp"), None), P("ctx", "tp"), P("tp", None), P("tp", None), P("tp")),
        check_vma=False,
    )
```

```python
import functools
import math

import jax
import jax.numpy as jnp
from jax import lax
from jax.experimental import pallas as pl
from jax.experimental.pallas import tpu as pltpu
from jax.sharding import PartitionSpec as P

MESH = pl.DeviceIdType.MESH
F32 = jnp.float32
BF16 = jnp.bfloat16
SUB = 8
LANE = 128
NX, NZ = 2, 4
A_PIECES, B_PIECES = 4, 2


def kernel(
    seq,
    n_ctx,
    x_hbm,
    res_hbm,
    lr_hbm,
    skip_hbm,
    w_hbm,
    og_hbm,
    out_ref,
    gi_ref,
    gres_ref,
    glog_ref,
    gskip_ref,
    x_ref,
    res_ref,
    lr_ref,
    skip_ref,
    w_v,
    og,
    part,
    hall,
    x32,
    y32,
    g32,
    gacc,
    mb,
    rate_t,
    c_t,
    far4,
    rate8,
    a8,
    c8,
    ex8,
    in8,
    v8,
    st_t,
    s_send,
    s_recv,
    r_send,
    r_recv,
    red,
    rr,
    fin,
    bx1,
    al1,
    ar1,
    al2,
    ar2,
    bl1,
    br1,
    bl2,
    br2,
    bx3,
    in_sem,
    w_sem,
    ag_s,
    ag_r,
    rs_s,
    rs_r,
    s_ss,
    s_rs,
    r_ss,
    r_rs,
    p_ss,
    p_rs,
    q_ss,
    q_rs,
):
    tok, chans = x_ref.shape
    modes = res_ref.shape[0]
    dim = w_v.shape[1]
    rows = tok // (NX * NZ)
    steps = tok // SUB
    lanes = chans // LANE
    half, quarter = dim // 2, dim // 4
    a_cols, b_cols = half // A_PIECES, half // B_PIECES
    n_blocks = dim // a_cols

    me = lax.axis_index("ctx")
    tp = lax.axis_index("tp")
    xl, z = tp // NZ, lax.rem(tp, NZ)
    ox = 1 - xl
    zr, zl, zo = lax.rem(z + 1, NZ), lax.rem(z + 3, NZ), lax.rem(z + 2, NZ)
    to_x = {"tp": ox * NZ + z}
    to_r = {"tp": xl * NZ + zr}
    to_l = {"tp": xl * NZ + zl}

    def cols(block):
        return pl.ds(pl.multiple_of(block * a_cols, a_cols), a_cols)

    def w_copy(block):
        return pltpu.make_async_copy(
            w_hbm.at[:, cols(block)], w_v.at[:, cols(block)], w_sem.at[block]
        )

    ins = [
        pltpu.make_async_copy(src, dst, in_sem.at[i])
        for i, (src, dst) in enumerate(
            (
                (lr_hbm, lr_ref),
                (res_hbm, res_ref),
                (x_hbm, x_ref),
                (skip_hbm, skip_ref),
                (og_hbm, og.at[xl, z]),
            )
        )
    ]
    for copy in ins:
        copy.start()
    barrier = pltpu.get_barrier_semaphore()
    for peer in (to_x, to_r, to_l):
        pl.semaphore_signal(barrier, inc=1, device_id=peer, device_id_type=MESH)

    @pl.loop(1, n_ctx)
    def _(k):
        pl.semaphore_signal(
            barrier, inc=1, device_id={"ctx": lax.rem(me + k, n_ctx)}, device_id_type=MESH
        )

    @pl.loop(0, n_blocks)
    def _(block):
        w_copy(block).start()

    for copy in ins[:4]:
        copy.wait()
    rate = jnp.exp(lr_ref[...]) / seq
    rate_t[...] = rate
    c_t[...] = res_ref[...] * jnp.sqrt(2.0 * rate)
    far = jnp.exp(-float(tok) * rate)
    for n in range(modes):
        row = pl.ds(n, 1)
        rate8[n] = jnp.broadcast_to(rate_t[row, :], (SUB, chans))
        c8[n] = jnp.broadcast_to(c_t[row, :], (SUB, chans))
    a8[...] = jnp.exp(-rate8[...])

    def lane(k):
        return pl.ds(k * LANE, LANE)

    for k in range(lanes):
        x32[k] = x_ref[:, lane(k)].astype(F32)
        far4[:, pl.ds(k, 1), :] = far[:, k * LANE : (k + 1) * LANE][:, None, :]

    place = lax.broadcasted_iota(jnp.int32, (modes, SUB, LANE), 1)
    place_f = place.astype(F32)
    span = float(steps)
    zero = jnp.zeros((modes, SUB, LANE), F32)

    def at_step(ref, i, k):
        return ref[k, pl.ds(i, SUB, stride=steps), :]

    for k in range(lanes):
        a = a8[:, :, lane(k)]

        def grow(i, h, a=a, k=k):
            return a * h + at_step(x32, i, k)[None]

        end = lax.fori_loop(0, steps, grow, zero, unroll=4)
        rk = rate8[:, :, lane(k)]
        for s in (1, 2, 4):
            moved = jnp.where(place >= s, pltpu.roll(end, s, 1), 0.0)
            end = end + jnp.exp(-(span * s) * rk) * moved
        ex8[:, :, lane(k)] = jnp.where(place >= 1, pltpu.roll(end, 1, 1), 0.0)
        s_send[:, lane(k)] = jnp.sum(jnp.where(place == SUB - 1, end, 0.0), axis=1).astype(BF16)

    pl.semaphore_wait(barrier, n_ctx + 2)

    def ctx_copy(src, dst, sends, recvs, peer, sender):
        return pltpu.make_async_remote_copy(
            src_ref=src,
            dst_ref=dst,
            send_sem=sends.at[peer],
            recv_sem=recvs.at[sender],
            device_id={"ctx": peer},
            device_id_type=MESH,
        )

    def s_copy(peer, sender):
        return ctx_copy(s_send, s_recv.at[sender], s_ss, s_rs, peer, sender)

    def r_copy(peer, sender):
        return ctx_copy(r_send, r_recv.at[sender], r_ss, r_rs, peer, sender)

    def p_copy(peer, sender):
        return ctx_copy(red.at[peer], rr.at[sender], p_ss, p_rs, peer, sender)

    def q_copy(peer, sender):
        return ctx_copy(fin.at[sender], fin.at[sender], q_ss, q_rs, peer, sender)

    def others(step):
        pl.loop(1, n_ctx)(lambda k: step(lax.rem(me + k, n_ctx)))

    @pl.loop(me + 1, n_ctx)
    def _(peer):
        s_copy(peer, me).start()

    tags = iter(range(100))

    def ag(src, dst, peer):
        index = next(tags)
        return pltpu.make_async_remote_copy(
            src_ref=src,
            dst_ref=dst,
            send_sem=ag_s.at[index],
            recv_sem=ag_r.at[index],
            device_id=peer,
            device_id_type=MESH,
        )

    def relay(shard_x, shard_z, columns, peer):
        piece = og.at[shard_x, shard_z, :, columns]
        return ag(piece, piece, peer)

    def mine(columns, peer):
        return ag(og_hbm.at[:, columns], og.at[xl, z, :, columns], peer)

    all_a, all_b = pl.ds(0, half), pl.ds(half, half)
    a1, a2 = pl.ds(0, quarter), pl.ds(quarter, quarter)
    b1, b2 = pl.ds(half, quarter), pl.ds(half + quarter, quarter)

    x_a, r_b, l_b = mine(all_a, to_x), mine(all_b, to_r), mine(all_b, to_l)
    x_b, r_a, l_a = mine(all_b, to_x), mine(all_a, to_r), mine(all_a, to_l)
    gathers = [x_a, r_b, l_b, x_b, r_a, l_a]
    for copy in gathers:
        copy.start()

    x_a.wait_recv()
    r_xa, l_xa = relay(ox, z, all_a, to_r), relay(ox, z, all_a, to_l)
    r_xa.start()
    l_xa.start()
    r_b.wait_recv()
    l_b.wait_recv()
    x_lb, x_rb = relay(xl, zl, all_b, to_x), relay(xl, zr, all_b, to_x)
    r_ob, l_ob = relay(xl, zl, b1, to_r), relay(xl, zr, b2, to_l)
    more = [r_ob, l_ob, x_lb, x_rb]
    for copy in more:
        copy.start()
    gathers += [r_xa, l_xa] + more

    def join(sender, total):
        s_copy(0, sender).wait_recv()
        return far * total + s_recv[sender].astype(F32)

    st_t[...] = lax.fori_loop(0, me, join, jnp.zeros((modes, chans), F32))
    for n in range(modes):
        in8[n] = jnp.broadcast_to(st_t[pl.ds(n, 1), :], (SUB, chans))

    for k in range(lanes):
        a, c = a8[:, :, lane(k)], c8[:, :, lane(k)]
        skip = skip_ref[:, lane(k)]
        start = ex8[:, :, lane(k)] + jnp.exp(-span * place_f * rate8[:, :, lane(k)]) * in8[
            :, :, lane(k)
        ]

        def emit(i, h, a=a, c=c, skip=skip, k=k):
            now = at_step(x32, i, k)
            h = a * h + now[None]
            hall[i, :, :, lane(k)] = h
            y32[k, pl.ds(i, SUB, stride=steps), :] = jnp.sum(c * h, axis=0) + skip * now
            return h

        lax.fori_loop(0, steps, emit, start, unroll=2)
        mb[:, lane(k)] = y32[k].astype(BF16)

    r_a.wait_recv()
    l_a.wait_recv()
    r_oa, l_oa = relay(xl, zl, a1, to_r), relay(xl, zr, a2, to_l)
    r_oa.start()
    l_oa.start()
    r_xa.wait_recv()
    l_xa.wait_recv()
    r_oxa, l_oxa = relay(ox, zl, a1, to_r), relay(ox, zr, a2, to_l)
    r_oxa.start()
    l_oxa.start()
    r_ob.wait_recv()
    l_ob.wait_recv()
    x_ob = relay(xl, zo, all_b, to_x)
    x_ob.start()
    gathers += [r_oa, l_oa, r_oxa, l_oxa, x_ob]

    sums = iter(range(100))
    reduces = []

    def rs(src, dst, peer):
        index = next(sums)
        copy = pltpu.make_async_remote_copy(
            src_ref=src,
            dst_ref=dst,
            send_sem=rs_s.at[index],
            recv_sem=rs_r.at[index],
            device_id=peer,
            device_id_type=MESH,
        )
        copy.start()
        reduces.append(copy)
        return copy

    def project(block):
        w_copy(block).wait()
        p = jnp.dot(mb[...], w_v[:, cols(block)], preferred_element_type=F32)
        part[:, :, :, cols(block)] = p.astype(BF16).reshape(NX, NZ, rows, a_cols)

    def a_span(i):
        return pl.ds(i * a_cols, a_cols)

    def a_halves(i):
        h = a_cols // 2
        return pl.ds(i * a_cols, h), pl.ds(i * a_cols + h, h)

    def b_span(i):
        return pl.ds(half + i * b_cols, b_cols)

    def b_halves(i):
        h = b_cols // 2
        return pl.ds(half + i * b_cols, h), pl.ds(half + i * b_cols + h, h)

    rs_x1 = []
    for i in range(A_PIECES):
        project(i)
        rs_x1.append(rs(part.at[ox, :, :, a_span(i)], bx1.at[i], to_x))
    rs_l1, rs_r1 = [], []
    for i in range(B_PIECES):
        per = A_PIECES // B_PIECES
        pl.loop(A_PIECES + i * per, A_PIECES + (i + 1) * per)(project)
        h1, h2 = b_halves(i)
        rs_l1.append(rs(part.at[:, zo, :, h1], bl1.at[i], to_r))
        rs_r1.append(rs(part.at[:, zo, :, h2], br1.at[i], to_l))

    for k in range(lanes):
        a = a8[:, :, lane(k)]

        def lift(i, v, a=a, k=k):
            return a * v + hall[i, :, :, lane(k)]

        v8[:, :, lane(k)] = a * lax.fori_loop(0, steps, lift, zero, unroll=4)

    x_a_parts = [r_oa, l_oa, r_oxa, l_oxa]
    for copy in x_a_parts:
        copy.wait_recv()
    ins[4].wait()

    gacc[...] = jnp.zeros_like(gacc)

    def project_back(block):
        gacc[...] += lax.dot_general(
            og[:, :, :, cols(block)].reshape(tok, a_cols),
            w_v[:, cols(block)],
            (((1,), (1,)), ((), ())),
            preferred_element_type=F32,
        )

    pl.loop(0, n_blocks // 2)(project_back)

    for copy in (x_b, x_lb, x_rb, x_ob):
        copy.wait_recv()

    pl.loop(n_blocks // 2, n_blocks)(project_back)

    for k in range(lanes):
        g32[k] = gacc[:, lane(k)].astype(BF16).astype(F32)
        lv = lane(k)
        hm = modes // 2
        for m0 in (0, hm):
            ms = pl.ds(m0, hm)
            a = a8[ms, :, lv]
            zh = jnp.zeros((hm, SUB, LANE), F32)

            def back(j, carry, a=a, k=k, lv=lv, ms=ms):
                h, gs, mloc = carry
                i = steps - 1 - j
                now = at_step(g32, i, k)[None]
                held = hall[i, ms, :, lv]
                h = a * h + now
                return h, gs + now * held, mloc + h * held

            end, gs, mloc = lax.fori_loop(0, steps, back, (zh, zh, zh), unroll=2)

            v = v8[ms, :, lv]
            pm = place[:hm]
            rk = rate8[ms, :, lv]
            for s in (1, 2, 4):
                moved = jnp.where(pm < SUB - s, pltpu.roll(end, SUB - s, 1), 0.0)
                end = end + jnp.exp(-(span * s) * rk) * moved
            ex = jnp.where(pm < SUB - 1, pltpu.roll(end, SUB - 1, 1), 0.0)
            ex8[ms, :, lv] = ex
            u = jnp.exp(-span * (SUB - 1.0 - place_f[:hm]) * rk) * v
            first = jnp.where(pm == 0, end, 0.0)
            r_send[ms, lv] = jnp.sum(first, axis=1).astype(BF16)
            for at, value in enumerate((gs, mloc + ex * v, u, first)):
                red[ms, pl.ds(at * lanes + k, 1), :] = jnp.sum(value, axis=1, keepdims=True)
        sk = jnp.sum(g32[k] * x32[k], axis=0, keepdims=True)
        red[:, pl.ds(4 * lanes + k, 1), :] = jnp.broadcast_to(sk[None], (modes, 1, LANE))

    others(lambda peer: p_copy(peer, me).start())

    @pl.loop(0, me)
    def _(peer):
        r_copy(peer, me).start()

    rr[me] = red[me]

    def merge(ref, got):
        ref[...] = (ref[...].astype(F32) + got[...].astype(F32)).astype(BF16)

    rs_l2, rs_r2 = [], []
    for i in range(B_PIECES):
        h1, h2 = b_halves(i)
        rs_l1[i].wait_recv()
        merge(part.at[:, zr, :, h1], bl1.at[i])
        rs_l2.append(rs(part.at[:, zr, :, b_span(i)], bl2.at[i], to_r))
        rs_r1[i].wait_recv()
        merge(part.at[:, zl, :, h2], br1.at[i])
        rs_r2.append(rs(part.at[:, zl, :, b_span(i)], br2.at[i], to_l))

    rs_al1, rs_ar1, rs_al2, rs_ar2 = [], [], [], []

    def take_x1(i):
        rs_x1[i].wait_recv()
        h1, h2 = a_halves(i)
        merge(part.at[xl, zo, :, a_span(i)], bx1.at[i, zo])
        rs_al1.append(rs(part.at[xl, zo, :, h1], al1.at[i], to_r))
        rs_ar1.append(rs(part.at[xl, zo, :, h2], ar1.at[i], to_l))
        merge(part.at[xl, zr, :, a_span(i)], bx1.at[i, zr])
        merge(part.at[xl, zl, :, a_span(i)], bx1.at[i, zl])

    def take_z1(i):
        h1, h2 = a_halves(i)
        rs_al1[i].wait_recv()
        merge(part.at[xl, zr, :, h1], al1.at[i])
        rs_al2.append(rs(part.at[xl, zr, :, a_span(i)], al2.at[i], to_r))
        rs_ar1[i].wait_recv()
        merge(part.at[xl, zl, :, h2], ar1.at[i])
        rs_ar2.append(rs(part.at[xl, zl, :, a_span(i)], ar2.at[i], to_l))

    for i in range(A_PIECES // 2):
        take_x1(i)

    def join_back(j, total):
        sender = n_ctx - 1 - j
        r_copy(0, sender).wait_recv()
        return far * total + r_recv[sender].astype(F32)

    st_t[...] = lax.fori_loop(0, n_ctx - 1 - me, join_back, jnp.zeros((modes, chans), F32))
    for n in range(modes):
        in8[n] = jnp.broadcast_to(st_t[pl.ds(n, 1), :], (SUB, chans))

    for k in range(lanes):
        a, c = a8[:, :, lane(k)], c8[:, :, lane(k)]
        skip = skip_ref[:, lane(k)]
        start = ex8[:, :, lane(k)] + jnp.exp(
            -span * (SUB - 1.0 - place_f) * rate8[:, :, lane(k)]
        ) * in8[:, :, lane(k)]

        def emit_back(j, h, a=a, c=c, skip=skip, k=k):
            i = steps - 1 - j
            now = at_step(g32, i, k)
            h = a * h + now[None]
            y32[k, pl.ds(i, SUB, stride=steps), :] = jnp.sum(c * h, axis=0) + skip * now
            return h

        lax.fori_loop(0, steps, emit_back, start, unroll=2)
        gi_ref[:, lane(k)] = y32[k].astype(BF16)

    for i in range(A_PIECES // 2, A_PIECES):
        take_x1(i)

    for i in range(A_PIECES // 2):
        take_z1(i)

    others(lambda peer: p_copy(0, peer).wait_recv())

    far_me = far4[me]

    def owner(j, carry):
        lam, gsum, msum, ksum = carry
        sender = n_ctx - 1 - j
        got = rr[sender]
        gsum = gsum + got[:lanes]
        msum = msum + got[lanes : 2 * lanes] + lam * got[2 * lanes : 3 * lanes]
        ksum = ksum + got[4 * lanes : 5 * lanes]
        return far_me * lam + got[3 * lanes : 4 * lanes], gsum, msum, ksum

    zl4 = jnp.zeros((lanes, LANE), F32)
    _, gsum, msum, ksum = lax.fori_loop(0, n_ctx, owner, (zl4, zl4, zl4, zl4))
    fin[me, pl.ds(0, lanes), :] = gsum
    fin[me, pl.ds(lanes, lanes), :] = msum
    others(lambda peer: q_copy(peer, me).start())
    scale = 1.0 / math.sqrt(seq)
    gskip_ref[...] = ksum * scale

    def total3(ref, left, right):
        return ref[...].astype(F32) + left[...].astype(F32) + right[...].astype(F32)

    rs_x3 = []
    for i in range(B_PIECES):
        rs_l2[i].wait_recv()
        rs_r2[i].wait_recv()
        far_part = part.at[ox, z, :, b_span(i)]
        far_part[...] = total3(far_part, bl2.at[i, ox], br2.at[i, ox]).astype(BF16)
        rs_x3.append(rs(far_part, bx3.at[i], to_x))

    for i in range(A_PIECES // 2, A_PIECES):
        take_z1(i)

    for i in range(A_PIECES):
        rs_al2[i].wait_recv()
        rs_ar2[i].wait_recv()
        out_ref[:, a_span(i)] = (
            total3(part.at[xl, z, :, a_span(i)], al2.at[i], ar2.at[i]) + bx1[i, z].astype(F32)
        ).astype(BF16)

    others(lambda peer: q_copy(0, peer).wait_recv())

    for k in range(lanes):
        rate = rate_t[:, lane(k)]
        gr = jnp.sum(fin[:, pl.ds(k, 1), :], axis=1)
        ml = jnp.sum(fin[:, pl.ds(lanes + k, 1), :], axis=1)
        gres_ref[:, lane(k)] = gr * (jnp.sqrt(2.0 * rate) * scale)
        glog_ref[:, lane(k)] = c_t[:, lane(k)] * ((0.5 + rate) * gr - rate * ml) * scale

    for i in range(B_PIECES):
        rs_x3[i].wait_recv()
        out_ref[:, b_span(i)] = (
            total3(part.at[xl, z, :, b_span(i)], bl2.at[i, xl], br2.at[i, xl])
            + bx3[i].astype(F32)
        ).astype(BF16)

    for copy in gathers + reduces:
        copy.wait_send()

    @pl.loop(me + 1, n_ctx)
    def _(peer):
        s_copy(peer, me).wait_send()

    @pl.loop(0, me)
    def _(peer):
        r_copy(peer, me).wait_send()

    others(lambda peer: p_copy(peer, me).wait_send())
    others(lambda peer: q_copy(peer, me).wait_send())


def store(*refs):
    n = len(refs) // 2
    copies = [
        pltpu.make_async_copy(refs[i], refs[n + i], refs[-1].at[i]) for i in range(n)
    ]
    for copy in copies:
        copy.start()
    for copy in copies:
        copy.wait()


def per_device(inputs, residue, log_rate, skip, out_weight, out_grad):
    n_ctx = lax.axis_size("ctx")
    tok, chans = inputs.shape
    modes = residue.shape[1]
    dim = out_weight.shape[1]
    rows = tok // (NX * NZ)
    steps = tok // SUB
    lanes = chans // LANE
    half = dim // 2
    a_cols, b_cols = half // A_PIECES, half // B_PIECES
    n_blocks = dim // a_cols
    wide = (modes, SUB, chans)
    flat = (modes, chans)
    packed = -(-5 * lanes // SUB) * SUB
    vmem = pl.BlockSpec(memory_space=pltpu.VMEM)
    anywhere = pl.BlockSpec(memory_space=pl.ANY)
    dma = pltpu.SemaphoreType.DMA
    results = (
        jax.ShapeDtypeStruct((rows, dim), BF16),
        jax.ShapeDtypeStruct((tok, chans), BF16),
        jax.ShapeDtypeStruct(flat, F32),
        jax.ShapeDtypeStruct(flat, F32),
        jax.ShapeDtypeStruct((lanes, LANE), F32),
    )
    held = pl.pallas_call(
        functools.partial(kernel, tok * n_ctx, n_ctx),
        out_shape=results,
        in_specs=[anywhere] * 6,
        out_specs=(vmem,) * 5,
        scratch_shapes=[
            pltpu.VMEM((tok, chans), BF16),
            pltpu.VMEM(flat, F32),
            pltpu.VMEM(flat, F32),
            pltpu.VMEM((1, chans), F32),
            pltpu.VMEM((chans, dim), BF16),
            pltpu.VMEM((NX, NZ, rows, dim), BF16),
            pltpu.VMEM((NX, NZ, rows, dim), BF16),
            pltpu.VMEM((steps, *wide), F32),
            pltpu.VMEM((lanes, tok, LANE), F32),
            pltpu.VMEM((lanes, tok, LANE), F32),
            pltpu.VMEM((lanes, tok, LANE), F32),
            pltpu.VMEM((tok, chans), F32),
            pltpu.VMEM((tok, chans), BF16),
            pltpu.VMEM(flat, F32),
            pltpu.VMEM(flat, F32),
            pltpu.VMEM((modes, lanes, LANE), F32),
            pltpu.VMEM(wide, F32),
            pltpu.VMEM(wide, F32),
            pltpu.VMEM(wide, F32),
            pltpu.VMEM(wide, F32),
            pltpu.VMEM(wide, F32),
            pltpu.VMEM(wide, F32),
            pltpu.VMEM(flat, F32),
            pltpu.VMEM(flat, BF16),
            pltpu.VMEM((n_ctx, *flat), BF16),
            pltpu.VMEM(flat, BF16),
            pltpu.VMEM((n_ctx, *flat), BF16),
            pltpu.VMEM((modes, packed, LANE), F32),
            pltpu.VMEM((n_ctx, packed, LANE), F32),
            pltpu.VMEM((n_ctx, 2 * lanes, LANE), F32),
            pltpu.VMEM((A_PIECES, NZ, rows, a_cols), BF16),
            pltpu.VMEM((A_PIECES, rows, a_cols // 2), BF16),
            pltpu.VMEM((A_PIECES, rows, a_cols // 2), BF16),
            pltpu.VMEM((A_PIECES, rows, a_cols), BF16),
            pltpu.VMEM((A_PIECES, rows, a_cols), BF16),
            pltpu.VMEM((B_PIECES, NX, rows, b_cols // 2), BF16),
            pltpu.VMEM((B_PIECES, NX, rows, b_cols // 2), BF16),
            pltpu.VMEM((B_PIECES, NX, rows, b_cols), BF16),
            pltpu.VMEM((B_PIECES, NX, rows, b_cols), BF16),
            pltpu.VMEM((B_PIECES, rows, b_cols), BF16),
            dma((5,)),
            dma((n_blocks,)),
            dma((17,)),
            dma((17,)),
            dma((5 * (A_PIECES + B_PIECES),)),
            dma((5 * (A_PIECES + B_PIECES),)),
            *[dma((n_ctx,)) for _ in range(8)],
        ],
        compiler_params=pltpu.CompilerParams(
            collective_id=0, has_side_effects=True, vmem_limit_bytes=56 * 1024 * 1024
        ),
    )(inputs, residue.T, log_rate.T, skip.reshape(1, chans), out_weight, out_grad)
    out, gi, gres, glog, gskip = pl.pallas_call(
        store,
        out_shape=results,
        in_specs=[vmem] * 5,
        out_specs=(anywhere,) * 5,
        scratch_shapes=[dma((5,))],
    )(*held)
    return out, gi, gres.T, glog.T, gskip.reshape(chans)


def solution(mesh):
    return jax.shard_map(
        per_device,
        mesh=mesh,
        in_specs=(
            P("ctx", "tp"),
            P("tp", None),
            P("tp", None),
            P("tp"),
            P("tp", None),
            P(("ctx", "tp"), None),
        ),
        out_specs=(P(("ctx", "tp"), None), P("ctx", "tp"), P("tp", None), P("tp", None), P("tp")),
        check_vma=False,
    )
```

```python
import functools
import math

import jax
import jax.numpy as jnp
from jax import lax
from jax.experimental import pallas as pl
from jax.experimental.pallas import tpu as pltpu
from jax.sharding import PartitionSpec as P

MESH = pl.DeviceIdType.MESH
F32 = jnp.float32
BF16 = jnp.bfloat16
SUB = 8
LANE = 128
NX, NZ = 2, 4
PIECES, A_PIECES, B_PIECES = 8, 2, 3


def kernel(
    seq,
    n_ctx,
    x_hbm,
    res_hbm,
    lr_hbm,
    skip_hbm,
    w_hbm,
    og_hbm,
    out_hbm,
    gi_hbm,
    gres_hbm,
    glog_hbm,
    gskip_hbm,
    out_ref,
    gi_ref,
    gres_ref,
    glog_ref,
    gskip_ref,
    x_ref,
    res_ref,
    lr_ref,
    skip_ref,
    w_v,
    og,
    part,
    hall,
    x32,
    y32,
    g32,
    mb,
    rate_t,
    c_t,
    far4,
    rate8,
    a8,
    c8,
    ex8,
    in8,
    v8,
    s_own,
    s_sib,
    s_pair,
    s_recv,
    h_t,
    r_own,
    r_sib,
    r_pair,
    r_recv,
    l_t,
    red,
    rr,
    dec,
    fin,
    bx1,
    al1,
    ar1,
    al2,
    ar2,
    bl1,
    br1,
    bl2,
    br2,
    bx3,
    in_sem,
    out_sem,
    w_sem,
    ag_s,
    ag_r,
    rs_s,
    rs_r,
    sr_ss,
    s_rs,
    r_rs,
    sib_s,
    sib_r,
    p_ss,
    p_rs,
    q_ss,
    q_rs,
):
    tok, chans = x_ref.shape
    modes = res_ref.shape[0]
    dim = w_v.shape[1]
    rows = tok // (NX * NZ)
    steps = tok // SUB
    lanes = chans // LANE
    half, quarter = dim // 2, dim // 4
    a_cols = dim // PIECES
    split = A_PIECES * a_cols
    b_cols = (dim - split) // B_PIECES

    me = lax.axis_index("ctx")
    tp = lax.axis_index("tp")
    xl, z = tp // NZ, lax.rem(tp, NZ)
    ox = 1 - xl
    zr, zl, zo = lax.rem(z + 1, NZ), lax.rem(z + 3, NZ), lax.rem(z + 2, NZ)
    to_x = {"tp": ox * NZ + z}
    to_r = {"tp": xl * NZ + zr}
    to_l = {"tp": xl * NZ + zl}
    pairs = n_ctx // 2
    pair, core = me // 2, lax.rem(me, 2)
    to_sib = {"ctx": me + 1 - 2 * core}
    my_half = pl.ds(pl.multiple_of(core * (chans // 2), chans // 2), chans // 2)

    w_copy = pltpu.make_async_copy(w_hbm, w_v, w_sem)

    barrier = pltpu.get_barrier_semaphore()
    for peer in (to_x, to_r, to_l):
        pl.semaphore_signal(barrier, inc=1, device_id=peer, device_id_type=MESH)

    @pl.loop(1, n_ctx)
    def _(k):
        pl.semaphore_signal(
            barrier, inc=1, device_id={"ctx": lax.rem(me + k, n_ctx)}, device_id_type=MESH
        )

    ins = [
        pltpu.make_async_copy(src, dst, in_sem.at[i])
        for i, (src, dst) in enumerate(
            (
                (lr_hbm, lr_ref),
                (res_hbm, res_ref),
                (x_hbm, x_ref),
                (skip_hbm, skip_ref),
                (og_hbm, og.at[xl, z]),
            )
        )
    ]
    for copy in ins:
        copy.start()
    w_copy.start()

    def save(index, src, dst):
        copy = pltpu.make_async_copy(src, dst, out_sem.at[index])
        copy.start()
        return copy

    pl.semaphore_wait(barrier, n_ctx + 2)

    def ctx_copy(src, dst, send, recv, peer):
        return pltpu.make_async_remote_copy(
            src_ref=src,
            dst_ref=dst,
            send_sem=send,
            recv_sem=recv,
            device_id={"ctx": peer},
            device_id_type=MESH,
        )

    def pair_copy(src, dst, recvs, peer, sender):
        return pltpu.make_async_remote_copy(
            src_ref=src,
            dst_ref=dst.at[sender],
            send_sem=sr_ss,
            recv_sem=recvs.at[sender],
            device_id={"ctx": 2 * peer + core},
            device_id_type=MESH,
        )

    def s_copy(peer, sender):
        return pair_copy(s_pair, s_recv, s_rs, peer, sender)

    def r_copy(peer, sender):
        return pair_copy(r_pair, r_recv, r_rs, peer, sender)

    def sib_copy(index, src, dst):
        return pltpu.make_async_remote_copy(
            src_ref=src,
            dst_ref=dst,
            send_sem=sib_s.at[index],
            recv_sem=sib_r.at[index],
            device_id=to_sib,
            device_id_type=MESH,
        )

    def p_copy(peer):
        return ctx_copy(red.at[peer], rr.at[me], p_ss, p_rs, peer)

    def q_copy(peer):
        return ctx_copy(fin.at[me], fin.at[me], q_ss, q_rs, peer)

    def wait_all(ref, sem):
        rest = ref.at[pl.ds(0, n_ctx - 1)]
        pltpu.make_async_copy(rest, rest, sem).wait()

    def others(step):
        pl.loop(1, n_ctx)(lambda k: step(lax.rem(me + k, n_ctx)))

    tags = iter(range(100))

    def ag(src, dst, peer):
        index = next(tags)
        return pltpu.make_async_remote_copy(
            src_ref=src,
            dst_ref=dst,
            send_sem=ag_s,
            recv_sem=ag_r.at[index],
            device_id=peer,
            device_id_type=MESH,
        )

    def relay(shard_x, shard_z, columns, peer):
        piece = og.at[shard_x, shard_z, :, columns]
        return ag(piece, piece, peer)

    def mine(columns, peer):
        return ag(og_hbm.at[:, columns], og.at[xl, z, :, columns], peer)

    all_a, all_b = pl.ds(0, half), pl.ds(half, half)
    a1, a2 = pl.ds(0, quarter), pl.ds(quarter, quarter)
    b1, b2 = pl.ds(half, quarter), pl.ds(half + quarter, quarter)

    x_a, r_b, l_b = mine(all_a, to_x), mine(all_b, to_r), mine(all_b, to_l)
    x_b, r_a, l_a = mine(all_b, to_x), mine(all_a, to_r), mine(all_a, to_l)
    for copy in (x_a, r_b, l_b, r_a, l_a):
        copy.start()
    gathers = [x_a, r_b, l_b, r_a, l_a, x_b]

    for copy in ins[:4]:
        copy.wait()
    rate = jnp.exp(lr_ref[...]) / seq
    rate_t[...] = rate
    c_t[...] = res_ref[...] * jnp.sqrt(2.0 * rate)
    far = jnp.exp(-float(tok) * rate)
    for n in range(modes):
        row = pl.ds(n, 1)
        rate8[n] = jnp.broadcast_to(rate_t[row, :], (SUB, chans))
        c8[n] = jnp.broadcast_to(c_t[row, :], (SUB, chans))
    a8[...] = jnp.exp(-rate8[...])

    def lane(k):
        return pl.ds(k * LANE, LANE)

    for k in range(lanes):
        x32[k] = x_ref[:, lane(k)].astype(F32)
        far4[:, pl.ds(k, 1), :] = far[:, k * LANE : (k + 1) * LANE][:, None, :]

    place = lax.broadcasted_iota(jnp.int32, (modes, SUB, LANE), 1)
    place_f = place.astype(F32)
    span = float(steps)
    zero = jnp.zeros((modes, SUB, LANE), F32)

    def at_step(ref, i, k):
        return ref[k, pl.ds(i, SUB, stride=steps), :]

    for k in range(lanes):
        a = a8[:, :, lane(k)]

        def grow(i, h, a=a, k=k):
            return a * h + at_step(x32, i, k)[None]

        end = lax.fori_loop(0, steps, grow, zero, unroll=4)
        rk = rate8[:, :, lane(k)]
        for s in (1, 2, 4):
            moved = jnp.where(place >= s, pltpu.roll(end, s, 1), 0.0)
            end = end + jnp.exp(-(span * s) * rk) * moved
        ex8[:, :, lane(k)] = jnp.where(place >= 1, pltpu.roll(end, 1, 1), 0.0)
        s_own[:, lane(k)] = jnp.sum(jnp.where(place == SUB - 1, end, 0.0), axis=1)

    sib_first = sib_copy(0, s_own, s_sib)
    sib_first.start()

    far_half = jnp.exp(-float(tok) * rate_t[:, my_half])
    sib_first.wait_recv()
    mine_s, sib_s_half = s_own[:, my_half], s_sib[:, my_half]
    s_early = jnp.where(core == 0, mine_s, sib_s_half)
    s_late = jnp.where(core == 0, sib_s_half, mine_s)
    s_pair[...] = (s_late + far_half * s_early).astype(BF16)

    @pl.loop(pair + 1, pairs)
    def _(peer):
        s_copy(peer, pair).start()

    x_b.start()

    for k in range(lanes):
        a = a8[:, :, lane(k)]
        rk = rate8[:, :, lane(k)]
        for at, s in enumerate((1, 2, 4)):
            dec[at, :, :, lane(k)] = jnp.exp(-(span * s) * rk)
        dec[3, :, :, lane(k)] = jnp.exp(-span * (SUB - 1.0 - place_f) * rk)
        dec[4, :, :, lane(k)] = jnp.exp(-span * place_f * rk)

        def lift(i, carry, a=a, k=k):
            h, v = carry
            h = a * h + at_step(x32, i, k)[None]
            return h, a * v + h

        _, v = lax.fori_loop(0, steps, lift, (zero, zero), unroll=2)
        v8[:, :, lane(k)] = a * v

    r_b.wait_recv()
    l_b.wait_recv()
    r_ob, l_ob = relay(xl, zl, b1, to_r), relay(xl, zr, b2, to_l)
    x_lb, x_rb = relay(xl, zl, all_b, to_x), relay(xl, zr, all_b, to_x)
    x_a.wait_recv()
    r_xa1, l_xa2 = relay(ox, z, a1, to_r), relay(ox, z, a2, to_l)
    r_xa2, l_xa1 = relay(ox, z, a2, to_r), relay(ox, z, a1, to_l)
    for copy in (r_xa1, l_xa2, x_lb, x_rb, r_ob, l_ob, r_xa2, l_xa1):
        copy.start()
    gathers += [r_xa1, l_xa2, x_lb, x_rb, r_ob, l_ob, r_xa2, l_xa1]

    def join(sender, total):
        s_copy(0, sender).wait_recv()
        return far_half * far_half * total + s_recv[sender].astype(F32)

    none = jnp.zeros((modes, chans // 2), F32)
    h_t[:, my_half] = lax.fori_loop(0, pair, join, none)
    sib_h = sib_copy(1, h_t.at[:, my_half], h_t.at[:, my_half])
    sib_h.start()

    r_a.wait_recv()
    l_a.wait_recv()
    r_oa, l_oa = relay(xl, zl, a1, to_r), relay(xl, zr, a2, to_l)
    r_oa.start()
    l_oa.start()
    gathers += [r_oa, l_oa]

    sib_h.wait_recv()
    far = jnp.exp(-float(tok) * rate_t[...])
    h_in = jnp.where(core == 0, h_t[...], far * h_t[...] + s_sib[...])
    for n in range(modes):
        in8[n] = jnp.broadcast_to(h_in[n : n + 1], (SUB, chans))

    for k in range(lanes):
        a, c = a8[:, :, lane(k)], c8[:, :, lane(k)]
        skip = skip_ref[:, lane(k)]
        start = ex8[:, :, lane(k)] + dec[4, :, :, lane(k)] * in8[:, :, lane(k)]
        v = v8[:, :, lane(k)] + span * a * dec[0, :, :, lane(k)] * start
        v8[:, :, lane(k)] = v
        u = jnp.sum(dec[3, :, :, lane(k)] * v, axis=1, keepdims=True)
        red[:, pl.ds(2 * lanes + k, 1), :] = u

        def emit(i, h, a=a, c=c, skip=skip, k=k):
            now = at_step(x32, i, k)
            h = a * h + now[None]
            hall[i, :, :, lane(k)] = h
            y32[k, pl.ds(i, SUB, stride=steps), :] = jnp.sum(c * h, axis=0) + skip * now
            return h

        lax.fori_loop(0, steps, emit, start, unroll=2)
        mb[:, lane(k)] = y32[k].astype(BF16)

    r_xa1.wait_recv()
    l_xa2.wait_recv()
    r_oxa, l_oxa = relay(ox, zl, a1, to_r), relay(ox, zr, a2, to_l)
    r_oxa.start()
    l_oxa.start()
    gathers += [r_oxa, l_oxa]

    r_ob.wait_recv()
    x_ob1 = relay(xl, zo, b1, to_x)
    x_ob1.start()
    l_ob.wait_recv()
    x_ob2 = relay(xl, zo, b2, to_x)
    x_ob2.start()
    gathers += [x_ob1, x_ob2]
    sums = iter(range(100))
    reduces = []

    def rs(src, dst, peer):
        index = next(sums)
        copy = pltpu.make_async_remote_copy(
            src_ref=src,
            dst_ref=dst,
            send_sem=rs_s,
            recv_sem=rs_r.at[index],
            device_id=peer,
            device_id_type=MESH,
        )
        copy.start()
        reduces.append(copy)
        return copy

    def a_span(i):
        return pl.ds(i * a_cols, a_cols)

    def a_halves(i):
        h = a_cols // 2
        return pl.ds(i * a_cols, h), pl.ds(i * a_cols + h, h)

    def b_span(i):
        return pl.ds(split + i * b_cols, b_cols)

    def b_halves(i):
        h = b_cols // 2
        return pl.ds(split + i * b_cols, h), pl.ds(split + i * b_cols + h, h)

    w_copy.wait()
    for lo, hi in ((0, split), (split, dim)):
        p = jnp.dot(mb[...], w_v[:, lo:hi], preferred_element_type=F32)
        part[:, :, :, lo:hi] = p.astype(BF16).reshape(NX, NZ, rows, hi - lo)

    rs_l1, rs_r1 = [], []
    for i in range(B_PIECES):
        h1, h2 = b_halves(i)
        rs_l1.append(rs(part.at[:, zo, :, h1], bl1.at[i], to_r))
        rs_r1.append(rs(part.at[:, zo, :, h2], br1.at[i], to_l))

    rs_x1 = []

    def send_x1():
        i = len(rs_x1)
        rs_x1.append(rs(part.at[ox, :, :, a_span(i)], bx1.at[i], to_x))

    send_x1()
    send_x1()

    x_a_parts = [r_xa2, l_xa1, r_oa, l_oa, r_oxa, l_oxa]
    for copy in x_a_parts:
        copy.wait_recv()
    ins[4].wait()

    def project_back(lo, hi, fresh=False):
        left = og[:, :, :, lo:hi].reshape(tok, hi - lo)
        for k in range(lanes):
            got = lax.dot_general(
                left,
                w_v[k * LANE : (k + 1) * LANE, lo:hi],
                (((1,), (1,)), ((), ())),
                preferred_element_type=F32,
            )
            g32[k] = got if fresh else g32[k] + got

    project_back(0, half, True)

    def merge(ref, got):
        ref[...] = (ref[...].astype(F32) + got[...].astype(F32)).astype(BF16)

    rs_l2, rs_r2 = [], []

    def take_b_z1():
        i = len(rs_l2)
        h1, h2 = b_halves(i)
        rs_l1[i].wait_recv()
        merge(part.at[:, zr, :, h1], bl1.at[i])
        rs_l2.append(rs(part.at[:, zr, :, b_span(i)], bl2.at[i], to_r))
        rs_r1[i].wait_recv()
        merge(part.at[:, zl, :, h2], br1.at[i])
        rs_r2.append(rs(part.at[:, zl, :, b_span(i)], br2.at[i], to_l))

    take_b_z1()

    for copy in (x_b, x_lb, x_rb, x_ob1):
        copy.wait_recv()

    project_back(half, half + quarter)
    x_ob2.wait_recv()
    project_back(half + quarter, dim)

    for k in range(lanes):
        g32[k] = g32[k].astype(BF16).astype(F32)
        sk = jnp.sum(g32[k] * x32[k], axis=0, keepdims=True)
        red[:, pl.ds(4 * lanes + k, 1), :] = jnp.broadcast_to(sk[None], (modes, 1, LANE))

    hm = modes // 2
    zh = jnp.zeros((hm, SUB, LANE), F32)
    pm = place[:hm]
    for m0 in (0, hm):
        ms = pl.ds(m0, hm)
        for k in range(lanes):
            lv = lane(k)
            a = a8[ms, :, lv]

            def back(j, carry, a=a, k=k, lv=lv, ms=ms):
                h, gs, mloc = carry
                i = steps - 1 - j
                now = at_step(g32, i, k)[None]
                held = hall[i, ms, :, lv]
                h = a * h + now
                return h, gs + now * held, mloc + h * held

            end, gs, mloc = lax.fori_loop(0, steps, back, (zh, zh, zh), unroll=2)
            for at, s in enumerate((1, 2, 4)):
                moved = jnp.where(pm < SUB - s, pltpu.roll(end, SUB - s, 1), 0.0)
                end = end + dec[at, ms, :, lv] * moved
            ex = jnp.where(pm < SUB - 1, pltpu.roll(end, SUB - 1, 1), 0.0)
            ex8[ms, :, lv] = ex
            first = jnp.where(pm == 0, end, 0.0)
            r_own[ms, lv] = jnp.sum(first, axis=1)
            for at, value in ((0, gs), (1, mloc + ex * v8[ms, :, lv]), (3, first)):
                red[ms, pl.ds(at * lanes + k, 1), :] = jnp.sum(value, axis=1, keepdims=True)

        @pl.loop(m0, m0 + hm)
        def _(peer):
            @pl.when(peer != me)
            def _():
                p_copy(peer).start()

        if m0 == 0:
            take_b_z1()

    take_b_z1()
    sib_back = sib_copy(2, r_own, r_sib)
    sib_back.start()
    rr[me] = red[me]

    rs_al1, rs_ar1, rs_al2, rs_ar2 = [], [], [], []

    def take_x1():
        i = len(rs_al1)
        rs_x1[i].wait_recv()
        h1, h2 = a_halves(i)
        merge(part.at[xl, zo, :, a_span(i)], bx1.at[i, zo])
        rs_al1.append(rs(part.at[xl, zo, :, h1], al1.at[i], to_r))
        rs_ar1.append(rs(part.at[xl, zo, :, h2], ar1.at[i], to_l))
        merge(part.at[xl, zr, :, a_span(i)], bx1.at[i, zr])
        merge(part.at[xl, zl, :, a_span(i)], bx1.at[i, zl])

    def take_z1():
        i = len(rs_al2)
        h1, h2 = a_halves(i)
        rs_al1[i].wait_recv()
        merge(part.at[xl, zr, :, h1], al1.at[i])
        rs_al2.append(rs(part.at[xl, zr, :, a_span(i)], al2.at[i], to_r))
        rs_ar1[i].wait_recv()
        merge(part.at[xl, zl, :, h2], ar1.at[i])
        rs_ar2.append(rs(part.at[xl, zl, :, a_span(i)], ar2.at[i], to_l))

    def total3(ref, left, right):
        return ref[...].astype(F32) + left[...].astype(F32) + right[...].astype(F32)

    rs_x3 = []

    def take_b_z2():
        i = len(rs_x3)
        rs_l2[i].wait_recv()
        rs_r2[i].wait_recv()
        far_part = part.at[ox, z, :, b_span(i)]
        far_part[...] = total3(far_part, bl2.at[i, ox], br2.at[i, ox]).astype(BF16)
        rs_x3.append(rs(far_part, bx3.at[i], to_x))

    take_x1()

    sib_back.wait_recv()
    mine_r, sib_r_half = r_own[:, my_half], r_sib[:, my_half]
    r_early = jnp.where(core == 0, mine_r, sib_r_half)
    r_late = jnp.where(core == 0, sib_r_half, mine_r)
    r_pair[...] = (r_early + far_half * r_late).astype(BF16)

    @pl.loop(0, pair)
    def _(peer):
        r_copy(peer, pair).start()


    take_x1()

    take_b_z2()

    wait_all(rr, p_rs)

    far_me = far4[me]

    def owner(j, carry):
        lam, gsum, msum, ksum = carry
        sender = n_ctx - 1 - j
        got = rr[sender]
        gsum = gsum + got[:lanes]
        msum = msum + got[lanes : 2 * lanes] + lam * got[2 * lanes : 3 * lanes]
        ksum = ksum + got[4 * lanes : 5 * lanes]
        return far_me * lam + got[3 * lanes : 4 * lanes], gsum, msum, ksum

    zl4 = jnp.zeros((lanes, LANE), F32)
    _, gsum, msum, ksum = lax.fori_loop(0, n_ctx, owner, (zl4, zl4, zl4, zl4))
    fin[me, pl.ds(0, lanes), :] = gsum
    fin[me, pl.ds(lanes, lanes), :] = msum
    others(lambda peer: q_copy(peer).start())
    scale = 1.0 / math.sqrt(seq)
    gskip_ref[...] = ksum * scale
    saves = [save(0, gskip_ref, gskip_hbm)]

    take_b_z2()

    take_z1()

    take_z1()

    take_b_z2()

    def join_back(j, total):
        sender = pairs - 1 - j
        r_copy(0, sender).wait_recv()
        return far_half * far_half * total + r_recv[sender].astype(F32)

    l_t[:, my_half] = lax.fori_loop(0, pairs - 1 - pair, join_back, none)
    sib_l = sib_copy(3, l_t.at[:, my_half], l_t.at[:, my_half])
    sib_l.start()

    sib_l.wait_recv()
    l_in = jnp.where(core == 1, l_t[...], far * l_t[...] + r_sib[...])
    for n in range(modes):
        in8[n] = jnp.broadcast_to(l_in[n : n + 1], (SUB, chans))

    for k in range(lanes):
        a, c = a8[:, :, lane(k)], c8[:, :, lane(k)]
        skip = skip_ref[:, lane(k)]
        start = ex8[:, :, lane(k)] + dec[3, :, :, lane(k)] * in8[:, :, lane(k)]

        def emit_back(j, h, a=a, c=c, skip=skip, k=k):
            i = steps - 1 - j
            now = at_step(g32, i, k)
            h = a * h + now[None]
            y32[k, pl.ds(i, SUB, stride=steps), :] = jnp.sum(c * h, axis=0) + skip * now
            return h

        lax.fori_loop(0, steps, emit_back, start, unroll=2)
        gi_ref[:, lane(k)] = y32[k].astype(BF16)
    saves.append(save(1, gi_ref, gi_hbm))

    for i in range(A_PIECES):
        rs_al2[i].wait_recv()
        rs_ar2[i].wait_recv()
        out_ref[:, a_span(i)] = (
            total3(part.at[xl, z, :, a_span(i)], al2.at[i], ar2.at[i]) + bx1[i, z].astype(F32)
        ).astype(BF16)

    part_a, part_b = pl.ds(0, split), pl.ds(split, dim - split)
    saves.append(save(2, out_ref.at[:, part_a], out_hbm.at[:, part_a]))

    for i in range(B_PIECES):
        rs_x3[i].wait_recv()
        out_ref[:, b_span(i)] = (
            total3(part.at[xl, z, :, b_span(i)], bl2.at[i, xl], br2.at[i, xl])
            + bx3[i].astype(F32)
        ).astype(BF16)

    saves.append(save(3, out_ref.at[:, part_b], out_hbm.at[:, part_b]))

    wait_all(fin, q_rs)

    for k in range(lanes):
        rate = rate_t[:, lane(k)]
        gr = jnp.sum(fin[:, pl.ds(k, 1), :], axis=1)
        ml = jnp.sum(fin[:, pl.ds(lanes + k, 1), :], axis=1)
        gres_ref[:, lane(k)] = gr * (jnp.sqrt(2.0 * rate) * scale)
        glog_ref[:, lane(k)] = c_t[:, lane(k)] * ((0.5 + rate) * gr - rate * ml) * scale

    saves += [save(4, gres_ref, gres_hbm), save(5, glog_ref, glog_hbm)]

    sent = w_v.at[pl.ds(0, tok - rows)]
    pltpu.make_async_copy(sent, sent, ag_s).wait()
    pltpu.make_async_copy(sent, sent, rs_s).wait()
    for copy in (sib_first, sib_h, sib_back, sib_l):
        copy.wait_send()
    rest = s_recv.at[pl.ds(0, pairs - 1)]
    pltpu.make_async_copy(rest, rest, sr_ss).wait()
    wait_all(rr, p_ss)
    wait_all(fin, q_ss)

    for copy in saves:
        copy.wait()


def store(*refs):
    n = (len(refs) - 2) // 3
    ins, outs, bufs = refs[:n], refs[n : 2 * n], refs[2 * n : 3 * n]
    loads = [pltpu.make_async_copy(ins[i], bufs[i], refs[-2].at[i]) for i in range(n)]
    saves = [pltpu.make_async_copy(bufs[i], outs[i], refs[-1].at[i]) for i in range(n)]
    for copy in loads:
        copy.start()
    for load, copy in zip(loads, saves):
        load.wait()
        copy.start()
    for copy in saves:
        copy.wait()


def per_device(inputs, residue, log_rate, skip, out_weight, out_grad):
    n_ctx = lax.axis_size("ctx")
    tok, chans = inputs.shape
    modes = residue.shape[1]
    dim = out_weight.shape[1]
    rows = tok // (NX * NZ)
    steps = tok // SUB
    lanes = chans // LANE
    a_cols = dim // PIECES
    b_cols = (dim - A_PIECES * a_cols) // B_PIECES
    wide = (modes, SUB, chans)
    flat = (modes, chans)
    packed = -(-5 * lanes // SUB) * SUB
    anywhere = pl.BlockSpec(memory_space=pl.ANY)
    dma = pltpu.SemaphoreType.DMA
    results = (
        jax.ShapeDtypeStruct((rows, dim), BF16),
        jax.ShapeDtypeStruct((tok, chans), BF16),
        jax.ShapeDtypeStruct(flat, F32),
        jax.ShapeDtypeStruct(flat, F32),
        jax.ShapeDtypeStruct((lanes, LANE), F32),
    )
    held_shapes = [pltpu.VMEM(r.shape, r.dtype) for r in results]
    held = pl.pallas_call(
        functools.partial(kernel, tok * n_ctx, n_ctx),
        out_shape=results,
        in_specs=[anywhere] * 6,
        out_specs=(anywhere,) * 5,
        scratch_shapes=[
            *held_shapes,
            pltpu.VMEM((tok, chans), BF16),
            pltpu.VMEM(flat, F32),
            pltpu.VMEM(flat, F32),
            pltpu.VMEM((1, chans), F32),
            pltpu.VMEM((chans, dim), BF16),
            pltpu.VMEM((NX, NZ, rows, dim), BF16),
            pltpu.VMEM((NX, NZ, rows, dim), BF16),
            pltpu.VMEM((steps, *wide), F32),
            pltpu.VMEM((lanes, tok, LANE), F32),
            pltpu.VMEM((lanes, tok, LANE), F32),
            pltpu.VMEM((lanes, tok, LANE), F32),
            pltpu.VMEM((tok, chans), BF16),
            pltpu.VMEM(flat, F32),
            pltpu.VMEM(flat, F32),
            pltpu.VMEM((modes, lanes, LANE), F32),
            pltpu.VMEM(wide, F32),
            pltpu.VMEM(wide, F32),
            pltpu.VMEM(wide, F32),
            pltpu.VMEM(wide, F32),
            pltpu.VMEM(wide, F32),
            pltpu.VMEM(wide, F32),
            *[
                pltpu.VMEM(flat, F32),
                pltpu.VMEM(flat, F32),
                pltpu.VMEM((modes, chans // 2), BF16),
                pltpu.VMEM((n_ctx // 2, modes, chans // 2), BF16),
                pltpu.VMEM(flat, F32),
            ]
            * 2,
            pltpu.VMEM((modes, packed, LANE), F32),
            pltpu.VMEM((n_ctx, packed, LANE), F32),
            pltpu.VMEM((5, *wide), F32),
            pltpu.VMEM((n_ctx, 2 * lanes, LANE), F32),
            pltpu.VMEM((A_PIECES, NZ, rows, a_cols), BF16),
            pltpu.VMEM((A_PIECES, rows, a_cols // 2), BF16),
            pltpu.VMEM((A_PIECES, rows, a_cols // 2), BF16),
            pltpu.VMEM((A_PIECES, rows, a_cols), BF16),
            pltpu.VMEM((A_PIECES, rows, a_cols), BF16),
            pltpu.VMEM((B_PIECES, NX, rows, b_cols // 2), BF16),
            pltpu.VMEM((B_PIECES, NX, rows, b_cols // 2), BF16),
            pltpu.VMEM((B_PIECES, NX, rows, b_cols), BF16),
            pltpu.VMEM((B_PIECES, NX, rows, b_cols), BF16),
            pltpu.VMEM((B_PIECES, rows, b_cols), BF16),
            dma((5,)),
            dma((6,)),
            dma,
            dma,
            dma((21,)),
            dma,
            dma((5 * (A_PIECES + B_PIECES),)),
            dma,
            dma((n_ctx // 2,)),
            dma((n_ctx // 2,)),
            dma((4,)),
            dma((4,)),
            *[dma] * 4,
        ],
        compiler_params=pltpu.CompilerParams(
            collective_id=0, has_side_effects=True, vmem_limit_bytes=56 * 1024 * 1024
        ),
    )(inputs, residue.T, log_rate.T, skip.reshape(1, chans), out_weight, out_grad)
    out, gi, gres, glog, gskip = pl.pallas_call(
        store,
        out_shape=results,
        in_specs=[anywhere] * 5,
        out_specs=(anywhere,) * 5,
        scratch_shapes=[*held_shapes, dma((5,)), dma((5,))],
    )(*held)
    return out, gi, gres.T, glog.T, gskip.reshape(chans)


def solution(mesh):
    return jax.shard_map(
        per_device,
        mesh=mesh,
        in_specs=(
            P("ctx", "tp"),
            P("tp", None),
            P("tp", None),
            P("tp"),
            P("tp", None),
            P(("ctx", "tp"), None),
        ),
        out_specs=(P(("ctx", "tp"), None), P("ctx", "tp"), P("tp", None), P("tp", None), P("tp")),
        check_vma=False,
    )
```

```python
import functools
import math

import jax
import jax.numpy as jnp
from jax import lax
from jax.experimental import pallas as pl
from jax.experimental.pallas import tpu as pltpu
from jax.sharding import PartitionSpec as P

MESH = pl.DeviceIdType.MESH
F32 = jnp.float32
BF16 = jnp.bfloat16
SUB = 8
LANE = 128
NX, NZ = 2, 4
PIECES, A_PIECES, B_SHARES = 8, 2, (5, 4, 3)
B_PIECES = len(B_SHARES)


def kernel(
    seq,
    n_ctx,
    x_hbm,
    res_hbm,
    lr_hbm,
    skip_hbm,
    w_hbm,
    og_hbm,
    out_hbm,
    gi_hbm,
    gres_hbm,
    glog_hbm,
    gskip_hbm,
    out_ref,
    gi_ref,
    gres_ref,
    glog_ref,
    gskip_ref,
    x_ref,
    res_ref,
    lr_ref,
    skip_ref,
    w_v,
    og,
    part,
    hall,
    x32,
    y32,
    g32,
    mb,
    rate_t,
    c_t,
    far4,
    rate8,
    a8,
    c8,
    ex8,
    in8,
    v8,
    s_own,
    s_sib,
    s_recv,
    h_t,
    r_own,
    r_sib,
    r_pair,
    r_recv,
    l_t,
    red,
    rr,
    dec,
    fin,
    bx1,
    al1,
    ar1,
    al2,
    ar2,
    bl1,
    br1,
    bl2,
    br2,
    bx3,
    near,
    in_sem,
    out_sem,
    w_sem,
    ag_s,
    ag_r,
    rs_s,
    rs_r,
    s_ss,
    s_rs,
    r_ss,
    r_rs,
    sib_s,
    sib_r,
    p_ss,
    p_rs,
    q_ss,
    q_rs,
):
    tok, chans = x_ref.shape
    modes = res_ref.shape[0]
    dim = w_v.shape[1]
    rows = tok // (NX * NZ)
    steps = tok // SUB
    lanes = chans // LANE
    half, quarter = dim // 2, dim // 4
    a_cols = dim // PIECES
    split = A_PIECES * a_cols
    b_unit = (dim - split) // sum(B_SHARES)

    me = lax.axis_index("ctx")
    tp = lax.axis_index("tp")
    xl, z = tp // NZ, lax.rem(tp, NZ)
    ox = 1 - xl
    zr, zl, zo = lax.rem(z + 1, NZ), lax.rem(z + 3, NZ), lax.rem(z + 2, NZ)
    to_x = {"tp": ox * NZ + z}
    to_r = {"tp": xl * NZ + zr}
    to_l = {"tp": xl * NZ + zl}
    pairs = n_ctx // 2
    pair, core = me // 2, lax.rem(me, 2)
    y, xh, n_y = me // 4, lax.rem(pair, 2), n_ctx // 4
    across = me + 2 - 4 * xh
    to_sib, to_xh = {"ctx": me + 1 - 2 * core}, {"ctx": across}
    to_x_other = {"ctx": across, "tp": ox * NZ + z}
    to_up, to_down = {"ctx": lax.rem(me + 4, n_ctx)}, {"ctx": lax.rem(me + n_ctx - 4, n_ctx)}
    my_half = pl.ds(pl.multiple_of(core * (chans // 2), chans // 2), chans // 2)

    w_copy = pltpu.make_async_copy(w_hbm, w_v, w_sem)

    barrier = pltpu.get_barrier_semaphore()
    for peer in (to_x, to_r, to_l, to_x_other, to_sib, to_up, to_down):
        pl.semaphore_signal(barrier, inc=1, device_id=peer, device_id_type=MESH)

    ins = [
        pltpu.make_async_copy(src, dst, in_sem.at[i])
        for i, (src, dst) in enumerate(
            (
                (lr_hbm, lr_ref),
                (res_hbm, res_ref),
                (x_hbm, x_ref),
                (skip_hbm, skip_ref),
                (og_hbm, og.at[xl, z]),
            )
        )
    ]
    for copy in ins:
        copy.start()
    w_copy.start()

    def save(index, src, dst):
        copy = pltpu.make_async_copy(src, dst, out_sem.at[index])
        copy.start()
        return copy

    pl.semaphore_wait(barrier, 7)
    for peer in (to_x, to_up, to_down):
        pl.semaphore_signal(near, inc=1, device_id=peer, device_id_type=MESH)

    def ctx_copy(src, dst, send, recv, peer):
        return pltpu.make_async_remote_copy(
            src_ref=src,
            dst_ref=dst,
            send_sem=send,
            recv_sem=recv,
            device_id={"ctx": peer},
            device_id_type=MESH,
        )

    def ctx_s(src, dst, index, peer):
        return ctx_copy(src, dst, s_ss, s_rs.at[index], peer)

    def s_copy(other):
        both = s_recv.at[pl.ds(2 * y, 2)]
        return ctx_s(both, both, 1, 4 * other + 2 * xh + core)

    def r_copy(peer, sender):
        return ctx_copy(r_pair, r_recv.at[sender], r_ss.at[peer], r_rs.at[sender], 2 * peer + core)

    def sib_copy(index, src, dst):
        return pltpu.make_async_remote_copy(
            src_ref=src,
            dst_ref=dst,
            send_sem=sib_s.at[index],
            recv_sem=sib_r.at[index],
            device_id=to_sib,
            device_id_type=MESH,
        )

    def p_copy(peer):
        return ctx_copy(red.at[peer], rr.at[me], p_ss, p_rs, peer)

    def q_copy(peer):
        return ctx_copy(fin.at[me], fin.at[me], q_ss, q_rs, peer)

    def wait_all(ref, sem):
        rest = ref.at[pl.ds(0, n_ctx - 1)]
        pltpu.make_async_copy(rest, rest, sem).wait()

    def others(step):
        pl.loop(1, n_ctx)(lambda k: step(lax.rem(me + k, n_ctx)))

    tags = iter(range(2, 100))

    def ag(src, dst, peer, group):
        copy = pltpu.make_async_remote_copy(
            src_ref=src,
            dst_ref=dst,
            send_sem=ag_s,
            recv_sem=ag_r.at[next(tags) if group is None else group],
            device_id=peer,
            device_id_type=MESH,
        )
        copy.start()
        return copy

    def relay(shard_x, shard_z, columns, peer, group=None):
        piece = og.at[shard_x, shard_z, :, columns]
        return ag(piece, piece, peer, group)

    def mine(columns, peer, group=None):
        return ag(og_hbm.at[:, columns], og.at[xl, z, :, columns], peer, group)

    def wait_bytes(sem, depth, width):
        size = w_v.at[pl.ds(0, depth), pl.ds(0, width)]
        pltpu.make_async_copy(size, size, sem).wait()

    all_a, all_b = pl.ds(0, half), pl.ds(half, half)
    a1, a2 = pl.ds(0, quarter), pl.ds(quarter, quarter)
    b1, b2 = pl.ds(half, quarter), pl.ds(half + quarter, quarter)
    late_a, late_b = 0, 1

    x_a1, r_b1, l_b2 = mine(a1, to_x), mine(b1, to_r), mine(b2, to_l)
    x_a2, r_b2, l_b1 = mine(a2, to_x), mine(b2, to_r), mine(b1, to_l)
    r_a, l_a = mine(all_a, to_r), mine(all_a, to_l)

    for copy in ins[:4]:
        copy.wait()
    rate = jnp.exp(lr_ref[...]) / seq
    rate_t[...] = rate
    c_t[...] = res_ref[...] * jnp.sqrt(2.0 * rate)
    far = jnp.exp(-float(tok) * rate)
    for n in range(modes):
        row = pl.ds(n, 1)
        rate8[n] = jnp.broadcast_to(rate_t[row, :], (SUB, chans))
        c8[n] = jnp.broadcast_to(c_t[row, :], (SUB, chans))
    a8[...] = jnp.exp(-rate8[...])

    def lane(k):
        return pl.ds(k * LANE, LANE)

    for k in range(lanes):
        x32[k] = x_ref[:, lane(k)].astype(F32)
        far4[:, pl.ds(k, 1), :] = far[:, k * LANE : (k + 1) * LANE][:, None, :]

    place = lax.broadcasted_iota(jnp.int32, (modes, SUB, LANE), 1)
    place_f = place.astype(F32)
    span = float(steps)
    zero = jnp.zeros((modes, SUB, LANE), F32)

    def at_step(ref, i, k):
        return ref[k, pl.ds(i, SUB, stride=steps), :]

    for k in range(lanes):
        a = a8[:, :, lane(k)]

        def grow(i, h, a=a, k=k):
            return a * h + at_step(x32, i, k)[None]

        end = lax.fori_loop(0, steps, grow, zero, unroll=8)
        rk = rate8[:, :, lane(k)]
        for s in (1, 2, 4):
            moved = jnp.where(place >= s, pltpu.roll(end, s, 1), 0.0)
            end = end + jnp.exp(-(span * s) * rk) * moved
        ex8[:, :, lane(k)] = jnp.where(place >= 1, pltpu.roll(end, 1, 1), 0.0)
        s_own[:, lane(k)] = jnp.sum(jnp.where(place == SUB - 1, end, 0.0), axis=1)

    sib_first = sib_copy(0, s_own, s_sib)
    sib_first.start()

    far_half = jnp.exp(-float(tok) * rate_t[:, my_half])
    sib_first.wait_recv()
    mine_s, sib_s_half = s_own[:, my_half], s_sib[:, my_half]
    s_early = jnp.where(core == 0, mine_s, sib_s_half)
    s_late = jnp.where(core == 0, sib_s_half, mine_s)
    s_recv[pair] = (s_late + far_half * s_early).astype(BF16)
    pl.semaphore_wait(near, 3)
    s_across = ctx_s(s_recv.at[pair], s_recv.at[pair], 0, across)
    s_across.start()

    mine(all_b, to_x, late_b)

    for k in range(lanes):
        a = a8[:, :, lane(k)]
        rk = rate8[:, :, lane(k)]
        for at, s in enumerate((1, 2, 4)):
            dec[at, :, :, lane(k)] = jnp.exp(-(span * s) * rk)
        dec[3, :, :, lane(k)] = jnp.exp(-span * (SUB - 1.0 - place_f) * rk)
        dec[4, :, :, lane(k)] = jnp.exp(-span * place_f * rk)

        def lift(i, carry, a=a, k=k):
            h, v = carry
            h = a * h + at_step(x32, i, k)[None]
            return h, a * v + h

        _, v = lax.fori_loop(0, steps, lift, (zero, zero), unroll=8)
        v8[:, :, lane(k)] = a * v

    x_a1.wait_recv()
    r_xa1 = relay(ox, z, a1, to_r)
    r_b1.wait_recv()
    r_ob = relay(xl, zl, b1, to_r)
    relay(xl, zl, b1, to_x, late_b)
    l_b2.wait_recv()
    l_ob = relay(xl, zr, b2, to_l)
    relay(xl, zr, b2, to_x, late_b)
    s_across.wait_recv()

    @pl.loop(1, n_y)
    def _(step):
        s_copy(lax.rem(y + step, n_y)).start()

    x_a2.wait_recv()
    l_xa2 = relay(ox, z, a2, to_l)
    r_b2.wait_recv()
    relay(xl, zl, b2, to_x, late_b)
    l_b1.wait_recv()
    relay(xl, zr, b1, to_x, late_b)
    relay(ox, z, a2, to_r, late_a)
    relay(ox, z, a1, to_l, late_a)

    def join(sender, total):
        return far_half * far_half * total + s_recv[sender].astype(F32)

    got_y = s_recv.at[pl.ds(0, pairs - 2)]
    pltpu.make_async_copy(got_y, got_y, s_rs.at[1]).wait()
    none = jnp.zeros((modes, chans // 2), F32)
    h_t[:, my_half] = lax.fori_loop(0, pair, join, none)
    sib_h = sib_copy(1, h_t.at[:, my_half], h_t.at[:, my_half])
    sib_h.start()

    r_a.wait_recv()
    l_a.wait_recv()
    relay(xl, zl, a1, to_r, late_a)
    relay(xl, zr, a2, to_l, late_a)

    sib_h.wait_recv()
    far = jnp.exp(-float(tok) * rate_t[...])
    h_in = jnp.where(core == 0, h_t[...], far * h_t[...] + s_sib[...])
    for n in range(modes):
        in8[n] = jnp.broadcast_to(h_in[n : n + 1], (SUB, chans))

    for k in range(lanes):
        a, c = a8[:, :, lane(k)], c8[:, :, lane(k)]
        skip = skip_ref[:, lane(k)]
        start = ex8[:, :, lane(k)] + dec[4, :, :, lane(k)] * in8[:, :, lane(k)]
        v = v8[:, :, lane(k)] + span * a * dec[0, :, :, lane(k)] * start
        v8[:, :, lane(k)] = v
        u = jnp.sum(dec[3, :, :, lane(k)] * v, axis=1, keepdims=True)
        red[:, pl.ds(2 * lanes + k, 1), :] = u

        def emit(i, h, a=a, c=c, skip=skip, k=k):
            now = at_step(x32, i, k)
            h = a * h + now[None]
            hall[i, :, :, lane(k)] = h
            y32[k, pl.ds(i, SUB, stride=steps), :] = jnp.sum(c * h, axis=0) + skip * now
            return h

        lax.fori_loop(0, steps, emit, start, unroll=8)
        mb[:, lane(k)] = y32[k].astype(BF16)

    r_xa1.wait_recv()
    l_xa2.wait_recv()
    relay(ox, zl, a1, to_r, late_a)
    relay(ox, zr, a2, to_l, late_a)

    r_ob.wait_recv()
    relay(xl, zo, b1, to_x, late_b)
    l_ob.wait_recv()
    x_ob2 = relay(xl, zo, b2, to_x)

    def rs(src, dst, peer, index):
        copy = pltpu.make_async_remote_copy(
            src_ref=src,
            dst_ref=dst,
            send_sem=rs_s,
            recv_sem=rs_r.at[index],
            device_id=peer,
            device_id_type=MESH,
        )
        copy.start()

    at_x1, at_az1, at_az2 = 0, A_PIECES, 2 * A_PIECES
    at_bz1 = at_az2 + 1
    at_bz2 = at_bz1 + B_PIECES
    at_x3 = at_bz2 + B_PIECES
    done = {"x1": 0, "az1": 0, "bz1": 0, "bz2": 0}

    def following(name):
        done[name] += 1
        return done[name] - 1

    def a_span(i):
        return pl.ds(i * a_cols, a_cols)

    def a_halves(i):
        h = a_cols // 2
        return pl.ds(i * a_cols, h), pl.ds(i * a_cols + h, h)

    def b_place(i):
        return b_unit * sum(B_SHARES[:i]), b_unit * B_SHARES[i]

    def b_span(i, base=split):
        at, width = b_place(i)
        return pl.ds(base + at, width)

    def b_halves(i):
        at, width = b_place(i)
        return pl.ds(split + at, width // 2), pl.ds(split + at + width // 2, width // 2)

    def b_half(i):
        at, width = b_place(i)
        return pl.ds(at // 2, width // 2)

    w_copy.wait()
    for lo, hi in ((0, split), (split, dim)):
        p = jnp.dot(mb[...], w_v[:, lo:hi], preferred_element_type=F32)
        part[:, :, :, lo:hi] = p.astype(BF16).reshape(NX, NZ, rows, hi - lo)

    for i in range(B_PIECES):
        h1, h2 = b_halves(i)
        rs(part.at[:, zo, :, h1], bl1.at[:, :, b_half(i)], to_r, at_bz1 + i)
        rs(part.at[:, zo, :, h2], br1.at[:, :, b_half(i)], to_l, at_bz1 + i)
    for i in range(A_PIECES):
        rs(part.at[ox, :, :, a_span(i)], bx1.at[i], to_x, at_x1 + i)

    wait_bytes(ag_r.at[late_a], 6 * rows, quarter)
    ins[4].wait()

    def project_back(lo, hi, fresh=False):
        left = og[:, :, :, lo:hi].reshape(tok, hi - lo)
        for k in range(lanes):
            got = lax.dot_general(
                left,
                w_v[k * LANE : (k + 1) * LANE, lo:hi],
                (((1,), (1,)), ((), ())),
                preferred_element_type=F32,
            )
            g32[k] = got if fresh else g32[k] + got

    project_back(0, half, True)

    def merge(ref, got):
        ref[...] = (ref[...].astype(F32) + got[...].astype(F32)).astype(BF16)

    def take_b_z1():
        i = following("bz1")
        h1, h2 = b_halves(i)
        wait_bytes(rs_r.at[at_bz1 + i], 2 * NX * rows, b_place(i)[1] // 2)
        merge(part.at[:, zr, :, h1], bl1.at[:, :, b_half(i)])
        rs(part.at[:, zr, :, b_span(i)], bl2.at[:, :, b_span(i, 0)], to_r, at_bz2 + i)
        merge(part.at[:, zl, :, h2], br1.at[:, :, b_half(i)])
        rs(part.at[:, zl, :, b_span(i)], br2.at[:, :, b_span(i, 0)], to_l, at_bz2 + i)

    def take_x1():
        i = following("x1")
        pltpu.make_async_copy(bx1.at[i], bx1.at[i], rs_r.at[at_x1 + i]).wait()
        h1, h2 = a_halves(i)
        merge(part.at[xl, zo, :, a_span(i)], bx1.at[i, zo])
        rs(part.at[xl, zo, :, h1], al1.at[i], to_r, at_az1 + i)
        rs(part.at[xl, zo, :, h2], ar1.at[i], to_l, at_az1 + i)
        merge(part.at[xl, zr, :, a_span(i)], bx1.at[i, zr])
        merge(part.at[xl, zl, :, a_span(i)], bx1.at[i, zl])

    def take_z1():
        i = following("az1")
        h1, h2 = a_halves(i)
        wait_bytes(rs_r.at[at_az1 + i], 2 * rows, a_cols // 2)
        merge(part.at[xl, zr, :, h1], al1.at[i])
        rs(part.at[xl, zr, :, a_span(i)], al2.at[i], to_r, at_az2)
        merge(part.at[xl, zl, :, h2], ar1.at[i])
        rs(part.at[xl, zl, :, a_span(i)], ar2.at[i], to_l, at_az2)

    def total3(ref, left, right):
        return ref[...].astype(F32) + left[...].astype(F32) + right[...].astype(F32)

    def take_b_z2():
        i = following("bz2")
        wait_bytes(rs_r.at[at_bz2 + i], 2 * NX * rows, b_place(i)[1])
        far_part = part.at[ox, z, :, b_span(i)]
        here = b_span(i, 0)
        far_part[...] = total3(far_part, bl2.at[ox, :, here], br2.at[ox, :, here]).astype(BF16)
        rs(far_part, bx3.at[:, here], to_x, at_x3)

    take_b_z1()

    wait_bytes(ag_r.at[late_b], 7 * rows, quarter)

    project_back(half, half + quarter)
    x_ob2.wait_recv()
    project_back(half + quarter, dim)

    for k in range(lanes):
        g32[k] = g32[k].astype(BF16).astype(F32)
        sk = jnp.sum(g32[k] * x32[k], axis=0, keepdims=True)
        red[:, pl.ds(4 * lanes + k, 1), :] = jnp.broadcast_to(sk[None], (modes, 1, LANE))

    hm = modes // 2
    zh = jnp.zeros((hm, SUB, LANE), F32)
    pm = place[:hm]
    for m0 in (0, hm):
        ms = pl.ds(m0, hm)
        for k in range(lanes):
            lv = lane(k)
            a = a8[ms, :, lv]

            def back(j, carry, a=a, k=k, lv=lv, ms=ms):
                h, gs, mloc = carry
                i = steps - 1 - j
                now = at_step(g32, i, k)[None]
                held = hall[i, ms, :, lv]
                h = a * h + now
                return h, gs + now * held, mloc + h * held

            end, gs, mloc = lax.fori_loop(0, steps, back, (zh, zh, zh), unroll=8)
            for at, s in enumerate((1, 2, 4)):
                moved = jnp.where(pm < SUB - s, pltpu.roll(end, SUB - s, 1), 0.0)
                end = end + dec[at, ms, :, lv] * moved
            ex = jnp.where(pm < SUB - 1, pltpu.roll(end, SUB - 1, 1), 0.0)
            ex8[ms, :, lv] = ex
            first = jnp.where(pm == 0, end, 0.0)
            r_own[ms, lv] = jnp.sum(first, axis=1)
            for at, value in ((0, gs), (1, mloc + ex * v8[ms, :, lv]), (3, first)):
                red[ms, pl.ds(at * lanes + k, 1), :] = jnp.sum(value, axis=1, keepdims=True)

        @pl.loop(m0, m0 + hm)
        def _(peer):
            @pl.when(peer != me)
            def _():
                p_copy(peer).start()

        if m0 == 0:
            take_x1()
            take_b_z1()

    sib_back = sib_copy(2, r_own, r_sib)
    sib_back.start()
    rr[me] = red[me]

    sib_back.wait_recv()
    mine_r, sib_r_half = r_own[:, my_half], r_sib[:, my_half]
    r_early = jnp.where(core == 0, mine_r, sib_r_half)
    r_late = jnp.where(core == 0, sib_r_half, mine_r)
    r_pair[...] = (r_early + far_half * r_late).astype(BF16)

    @pl.loop(0, pair)
    def _(peer):
        r_copy(peer, pair).start()


    take_x1()
    take_b_z1()

    take_b_z2()

    take_z1()

    wait_all(rr, p_rs)

    far_me = far4[me]

    def owner(j, carry):
        lam, gsum, msum, ksum = carry
        sender = n_ctx - 1 - j
        got = rr[sender]
        gsum = gsum + got[:lanes]
        msum = msum + got[lanes : 2 * lanes] + lam * got[2 * lanes : 3 * lanes]
        ksum = ksum + got[4 * lanes : 5 * lanes]
        return far_me * lam + got[3 * lanes : 4 * lanes], gsum, msum, ksum

    zl4 = jnp.zeros((lanes, LANE), F32)
    _, gsum, msum, ksum = lax.fori_loop(0, n_ctx, owner, (zl4, zl4, zl4, zl4))
    fin[me, pl.ds(0, lanes), :] = gsum
    fin[me, pl.ds(lanes, lanes), :] = msum
    others(lambda peer: q_copy(peer).start())
    scale = 1.0 / math.sqrt(seq)
    gskip_ref[...] = ksum * scale
    saves = [save(0, gskip_ref, gskip_hbm)]

    take_b_z2()

    take_z1()

    def join_back(j, total):
        sender = pairs - 1 - j
        r_copy(0, sender).wait_recv()
        return far_half * far_half * total + r_recv[sender].astype(F32)

    l_t[:, my_half] = lax.fori_loop(0, pairs - 1 - pair, join_back, none)
    sib_l = sib_copy(3, l_t.at[:, my_half], l_t.at[:, my_half])
    sib_l.start()

    take_b_z2()

    sib_l.wait_recv()
    l_in = jnp.where(core == 1, l_t[...], far * l_t[...] + r_sib[...])
    for n in range(modes):
        in8[n] = jnp.broadcast_to(l_in[n : n + 1], (SUB, chans))

    for k in range(lanes):
        a, c = a8[:, :, lane(k)], c8[:, :, lane(k)]
        skip = skip_ref[:, lane(k)]
        start = ex8[:, :, lane(k)] + dec[3, :, :, lane(k)] * in8[:, :, lane(k)]

        def emit_back(j, h, a=a, c=c, skip=skip, k=k):
            i = steps - 1 - j
            now = at_step(g32, i, k)
            h = a * h + now[None]
            y32[k, pl.ds(i, SUB, stride=steps), :] = jnp.sum(c * h, axis=0) + skip * now
            return h

        lax.fori_loop(0, steps, emit_back, start, unroll=8)
        gi_ref[:, lane(k)] = y32[k].astype(BF16)
    saves.append(save(1, gi_ref, gi_hbm))

    wait_bytes(rs_r.at[at_az2], 2 * A_PIECES * rows, a_cols)
    for i in range(A_PIECES):
        out_ref[:, a_span(i)] = (
            total3(part.at[xl, z, :, a_span(i)], al2.at[i], ar2.at[i]) + bx1[i, z].astype(F32)
        ).astype(BF16)

    part_a, part_b = pl.ds(0, split), pl.ds(split, dim - split)
    saves.append(save(2, out_ref.at[:, part_a], out_hbm.at[:, part_a]))

    wait_bytes(rs_r.at[at_x3], rows, dim - split)
    out_ref[:, split:] = (
        total3(part.at[xl, z, :, pl.ds(split, dim - split)], bl2.at[xl], br2.at[xl])
        + bx3[...].astype(F32)
    ).astype(BF16)

    saves.append(save(3, out_ref.at[:, part_b], out_hbm.at[:, part_b]))

    wait_all(fin, q_rs)

    for k in range(lanes):
        rate = rate_t[:, lane(k)]
        gr = jnp.sum(fin[:, pl.ds(k, 1), :], axis=1)
        ml = jnp.sum(fin[:, pl.ds(lanes + k, 1), :], axis=1)
        gres_ref[:, lane(k)] = gr * (jnp.sqrt(2.0 * rate) * scale)
        glog_ref[:, lane(k)] = c_t[:, lane(k)] * ((0.5 + rate) * gr - rate * ml) * scale

    saves += [save(4, gres_ref, gres_hbm), save(5, glog_ref, glog_hbm)]

    sent = w_v.at[pl.ds(0, tok - rows)]
    pltpu.make_async_copy(sent, sent, ag_s).wait()
    pltpu.make_async_copy(sent, sent, rs_s).wait()
    for copy in (sib_first, sib_h, sib_back, sib_l):
        copy.wait_send()
    rest = r_recv.at[pl.ds(0, pairs - 1)]
    pltpu.make_async_copy(rest, rest, s_ss).wait()

    @pl.loop(0, pair)
    def _(peer):
        r_copy(peer, pair).wait_send()

    wait_all(rr, p_ss)
    wait_all(fin, q_ss)

    for copy in saves:
        copy.wait()


def store(*refs):
    n = (len(refs) - 2) // 3
    ins, outs, bufs = refs[:n], refs[n : 2 * n], refs[2 * n : 3 * n]
    loads = [pltpu.make_async_copy(ins[i], bufs[i], refs[-2].at[i]) for i in range(n)]
    saves = [pltpu.make_async_copy(bufs[i], outs[i], refs[-1].at[i]) for i in range(n)]
    for copy in loads:
        copy.start()
    for load, copy in zip(loads, saves):
        load.wait()
        copy.start()
    for copy in saves:
        copy.wait()


def per_device(inputs, residue, log_rate, skip, out_weight, out_grad):
    n_ctx = lax.axis_size("ctx")
    tok, chans = inputs.shape
    modes = residue.shape[1]
    dim = out_weight.shape[1]
    rows = tok // (NX * NZ)
    steps = tok // SUB
    lanes = chans // LANE
    a_cols = dim // PIECES
    b_cols = dim - A_PIECES * a_cols
    wide = (modes, SUB, chans)
    flat = (modes, chans)
    packed = -(-5 * lanes // SUB) * SUB
    anywhere = pl.BlockSpec(memory_space=pl.ANY)
    dma = pltpu.SemaphoreType.DMA
    results = (
        jax.ShapeDtypeStruct((rows, dim), BF16),
        jax.ShapeDtypeStruct((tok, chans), BF16),
        jax.ShapeDtypeStruct(flat, F32),
        jax.ShapeDtypeStruct(flat, F32),
        jax.ShapeDtypeStruct((lanes, LANE), F32),
    )
    held_shapes = [pltpu.VMEM(r.shape, r.dtype) for r in results]
    held = pl.pallas_call(
        functools.partial(kernel, tok * n_ctx, n_ctx),
        out_shape=results,
        in_specs=[anywhere] * 6,
        out_specs=(anywhere,) * 5,
        scratch_shapes=[
            *held_shapes,
            pltpu.VMEM((tok, chans), BF16),
            pltpu.VMEM(flat, F32),
            pltpu.VMEM(flat, F32),
            pltpu.VMEM((1, chans), F32),
            pltpu.VMEM((chans, dim), BF16),
            pltpu.VMEM((NX, NZ, rows, dim), BF16),
            pltpu.VMEM((NX, NZ, rows, dim), BF16),
            pltpu.VMEM((steps, *wide), F32),
            pltpu.VMEM((lanes, tok, LANE), F32),
            pltpu.VMEM((lanes, tok, LANE), F32),
            pltpu.VMEM((lanes, tok, LANE), F32),
            pltpu.VMEM((tok, chans), BF16),
            pltpu.VMEM(flat, F32),
            pltpu.VMEM(flat, F32),
            pltpu.VMEM((modes, lanes, LANE), F32),
            pltpu.VMEM(wide, F32),
            pltpu.VMEM(wide, F32),
            pltpu.VMEM(wide, F32),
            pltpu.VMEM(wide, F32),
            pltpu.VMEM(wide, F32),
            pltpu.VMEM(wide, F32),
            pltpu.VMEM(flat, F32),
            pltpu.VMEM(flat, F32),
            pltpu.VMEM((n_ctx // 2, modes, chans // 2), BF16),
            pltpu.VMEM(flat, F32),
            pltpu.VMEM(flat, F32),
            pltpu.VMEM(flat, F32),
            pltpu.VMEM((modes, chans // 2), BF16),
            pltpu.VMEM((n_ctx // 2, modes, chans // 2), BF16),
            pltpu.VMEM(flat, F32),
            pltpu.VMEM((modes, packed, LANE), F32),
            pltpu.VMEM((n_ctx, packed, LANE), F32),
            pltpu.VMEM((5, *wide), F32),
            pltpu.VMEM((n_ctx, 2 * lanes, LANE), F32),
            pltpu.VMEM((A_PIECES, NZ, rows, a_cols), BF16),
            pltpu.VMEM((A_PIECES, rows, a_cols // 2), BF16),
            pltpu.VMEM((A_PIECES, rows, a_cols // 2), BF16),
            pltpu.VMEM((A_PIECES, rows, a_cols), BF16),
            pltpu.VMEM((A_PIECES, rows, a_cols), BF16),
            pltpu.VMEM((NX, rows, b_cols // 2), BF16),
            pltpu.VMEM((NX, rows, b_cols // 2), BF16),
            pltpu.VMEM((NX, rows, b_cols), BF16),
            pltpu.VMEM((NX, rows, b_cols), BF16),
            pltpu.VMEM((rows, b_cols), BF16),
            pltpu.SemaphoreType.REGULAR,
            dma((5,)),
            dma((6,)),
            dma,
            dma,
            dma((15,)),
            dma,
            dma((2 * (A_PIECES + B_PIECES) + 2,)),
            dma,
            dma((2,)),
            dma((n_ctx // 2,)),
            dma((n_ctx // 2,)),
            dma((4,)),
            dma((4,)),
            *[dma] * 4,
        ],
        compiler_params=pltpu.CompilerParams(
            collective_id=0, has_side_effects=True, vmem_limit_bytes=56 * 1024 * 1024
        ),
    )(inputs, residue.T, log_rate.T, skip.reshape(1, chans), out_weight, out_grad)
    out, gi, gres, glog, gskip = pl.pallas_call(
        store,
        out_shape=results,
        in_specs=[anywhere] * 5,
        out_specs=(anywhere,) * 5,
        scratch_shapes=[*held_shapes, dma((5,)), dma((5,))],
    )(*held)
    return out, gi, gres.T, glog.T, gskip.reshape(chans)


def solution(mesh):
    return jax.shard_map(
        per_device,
        mesh=mesh,
        in_specs=(
            P("ctx", "tp"),
            P("tp", None),
            P("tp", None),
            P("tp"),
            P("tp", None),
            P(("ctx", "tp"), None),
        ),
        out_specs=(P(("ctx", "tp"), None), P("ctx", "tp"), P("tp", None), P("tp", None), P("tp")),
        check_vma=False,
    )
```

```python
import functools
import math

import jax
import jax.numpy as jnp
from jax import lax
from jax.experimental import pallas as pl
from jax.experimental.pallas import tpu as pltpu
from jax.sharding import PartitionSpec as P

MESH = pl.DeviceIdType.MESH
F32 = jnp.float32
BF16 = jnp.bfloat16
SUB = 8
LANE = 128
NX, NZ = 2, 4
SHARES, A_SHARES, B_SHARES = 32, (4, 4), (8, 8, 5, 3)
A_PIECES, B_PIECES = len(A_SHARES), len(B_SHARES)


def kernel(
    seq,
    n_ctx,
    x_hbm,
    res_hbm,
    lr_hbm,
    skip_hbm,
    w_hbm,
    og_hbm,
    out_hbm,
    gi_hbm,
    gres_hbm,
    glog_hbm,
    gskip_hbm,
    out_ref,
    gi_ref,
    gres_ref,
    glog_ref,
    gskip_ref,
    x_ref,
    res_ref,
    lr_ref,
    skip_ref,
    w_v,
    og,
    part,
    hall,
    x32,
    y32,
    g32,
    mb,
    rate_t,
    c_t,
    far4,
    rate8,
    a8,
    c8,
    ex8,
    in8,
    v8,
    s_own,
    s_sib,
    s_recv,
    r_own,
    r_sib,
    r_pair,
    r_recv,
    l_t,
    red,
    rr,
    dec,
    fin,
    bx1,
    al1,
    ar1,
    al2,
    ar2,
    bl1,
    br1,
    bl2,
    br2,
    bx3,
    near,
    in_sem,
    out_sem,
    w_sem,
    ag_s,
    ag_r,
    rs_s,
    rs_r,
    s_ss,
    s_rs,
    r_ss,
    r_rs,
    sib_s,
    sib_r,
    p_ss,
    p_rs,
    q_ss,
    q_rs,
):
    tok, chans = x_ref.shape
    modes = res_ref.shape[0]
    dim = w_v.shape[1]
    rows = tok // (NX * NZ)
    steps = tok // SUB
    lanes = chans // LANE
    half, quarter = dim // 2, dim // 4
    unit = dim // SHARES
    split = unit * sum(A_SHARES)

    me = lax.axis_index("ctx")
    tp = lax.axis_index("tp")
    xl, z = tp // NZ, lax.rem(tp, NZ)
    ox = 1 - xl
    zr, zl, zo = lax.rem(z + 1, NZ), lax.rem(z + 3, NZ), lax.rem(z + 2, NZ)
    to_x = {"tp": ox * NZ + z}
    to_r = {"tp": xl * NZ + zr}
    to_l = {"tp": xl * NZ + zl}
    pairs = n_ctx // 2
    pair, core = me // 2, lax.rem(me, 2)
    y, xh, n_y = me // 4, lax.rem(pair, 2), n_ctx // 4
    across = me + 2 - 4 * xh
    to_sib, to_xh = {"ctx": me + 1 - 2 * core}, {"ctx": across}
    to_x_other = {"ctx": across, "tp": ox * NZ + z}
    to_up, to_down = {"ctx": lax.rem(me + 4, n_ctx)}, {"ctx": lax.rem(me + n_ctx - 4, n_ctx)}
    my_half = pl.ds(pl.multiple_of(core * (chans // 2), chans // 2), chans // 2)

    w_copy = pltpu.make_async_copy(w_hbm, w_v, w_sem)

    barrier = pltpu.get_barrier_semaphore()
    for peer in (to_x, to_r, to_l, to_x_other, to_sib, to_up, to_down):
        pl.semaphore_signal(barrier, inc=1, device_id=peer, device_id_type=MESH)

    ins = [
        pltpu.make_async_copy(src, dst, in_sem.at[i])
        for i, (src, dst) in enumerate(
            (
                (lr_hbm, lr_ref),
                (res_hbm, res_ref),
                (x_hbm, x_ref),
                (skip_hbm, skip_ref),
                (og_hbm, og.at[xl, z]),
            )
        )
    ]
    for copy in ins:
        copy.start()
    w_copy.start()

    def save(index, src, dst):
        copy = pltpu.make_async_copy(src, dst, out_sem.at[index])
        copy.start()
        return copy

    pl.semaphore_wait(barrier, 7)
    for peer in (to_x, to_up, to_down):
        pl.semaphore_signal(near, inc=1, device_id=peer, device_id_type=MESH)

    def ctx_copy(src, dst, send, recv, peer):
        return pltpu.make_async_remote_copy(
            src_ref=src,
            dst_ref=dst,
            send_sem=send,
            recv_sem=recv,
            device_id={"ctx": peer},
            device_id_type=MESH,
        )

    def ctx_s(src, dst, index, peer):
        return ctx_copy(src, dst, s_ss, s_rs.at[index], peer)

    def s_copy(other):
        both = s_recv.at[pl.ds(2 * y, 2)]
        return ctx_s(both, both, 1, 4 * other + 2 * xh + core)

    def r_copy(peer, sender):
        return ctx_copy(r_pair, r_recv.at[sender], r_ss.at[peer], r_rs.at[sender], 2 * peer + core)

    def sib_copy(index, src, dst):
        return pltpu.make_async_remote_copy(
            src_ref=src,
            dst_ref=dst,
            send_sem=sib_s.at[index],
            recv_sem=sib_r.at[index],
            device_id=to_sib,
            device_id_type=MESH,
        )

    def p_copy(peer):
        return ctx_copy(red.at[peer], rr.at[me], p_ss, p_rs, peer)

    def q_copy(peer):
        return ctx_copy(fin.at[me], fin.at[me], q_ss, q_rs, peer)

    def wait_all(ref, sem):
        rest = ref.at[pl.ds(0, n_ctx - 1)]
        pltpu.make_async_copy(rest, rest, sem).wait()

    def others(step):
        pl.loop(1, n_ctx)(lambda k: step(lax.rem(me + k, n_ctx)))

    tags = iter(range(2, 100))

    def ag(src, dst, peer, group):
        copy = pltpu.make_async_remote_copy(
            src_ref=src,
            dst_ref=dst,
            send_sem=ag_s,
            recv_sem=ag_r.at[next(tags) if group is None else group],
            device_id=peer,
            device_id_type=MESH,
        )
        copy.start()
        return copy

    def relay(shard_x, shard_z, columns, peer, group=None):
        piece = og.at[shard_x, shard_z, :, columns]
        return ag(piece, piece, peer, group)

    def mine(columns, peer, group=None):
        return ag(og_hbm.at[:, columns], og.at[xl, z, :, columns], peer, group)

    def wait_bytes(sem, depth, width):
        size = w_v.at[pl.ds(0, depth), pl.ds(0, width)]
        pltpu.make_async_copy(size, size, sem).wait()

    all_a, all_b = pl.ds(0, half), pl.ds(half, half)
    a1, a2 = pl.ds(0, quarter), pl.ds(quarter, quarter)
    b1, b2 = pl.ds(half, quarter), pl.ds(half + quarter, quarter)
    late_a, late_b = 0, 1

    x_a1, r_b1, l_b2 = mine(a1, to_x), mine(b1, to_r), mine(b2, to_l)
    x_a2, r_b2, l_b1 = mine(a2, to_x), mine(b2, to_r), mine(b1, to_l)
    r_a, l_a = mine(all_a, to_r), mine(all_a, to_l)

    for copy in ins[:4]:
        copy.wait()
    rate = jnp.exp(lr_ref[...]) / seq
    rate_t[...] = rate
    c_t[...] = res_ref[...] * jnp.sqrt(2.0 * rate)
    far = jnp.exp(-float(tok) * rate)
    for n in range(modes):
        row = pl.ds(n, 1)
        rate8[n] = jnp.broadcast_to(rate_t[row, :], (SUB, chans))
        c8[n] = jnp.broadcast_to(c_t[row, :], (SUB, chans))
    a8[...] = jnp.exp(-rate8[...])

    def lane(k):
        return pl.ds(k * LANE, LANE)

    for k in range(lanes):
        x32[k] = x_ref[:, lane(k)].astype(F32)
        far4[:, pl.ds(k, 1), :] = far[:, k * LANE : (k + 1) * LANE][:, None, :]

    place = lax.broadcasted_iota(jnp.int32, (modes, SUB, LANE), 1)
    place_f = place.astype(F32)
    span = float(steps)
    zero = jnp.zeros((modes, SUB, LANE), F32)

    def at_step(ref, i, k):
        return ref[k, pl.ds(i, SUB, stride=steps), :]

    for k in range(lanes):
        a = a8[:, :, lane(k)]

        def grow(i, h, a=a, k=k):
            return a * h + at_step(x32, i, k)[None]

        end = lax.fori_loop(0, steps, grow, zero, unroll=8)
        rk = rate8[:, :, lane(k)]
        for s in (1, 2, 4):
            moved = jnp.where(place >= s, pltpu.roll(end, s, 1), 0.0)
            end = end + jnp.exp(-(span * s) * rk) * moved
        ex8[:, :, lane(k)] = jnp.where(place >= 1, pltpu.roll(end, 1, 1), 0.0)
        s_own[:, lane(k)] = jnp.sum(jnp.where(place == SUB - 1, end, 0.0), axis=1)

    sib_first = sib_copy(0, s_own, s_sib)
    sib_first.start()

    far_half = jnp.exp(-float(tok) * rate_t[:, my_half])
    sib_first.wait_recv()
    s_early = jnp.where(core == 0, s_own[...], s_sib[...])
    s_late = jnp.where(core == 0, s_sib[...], s_own[...])
    far = jnp.exp(-float(tok) * rate_t[...])
    s_recv[pair] = (s_late + far * s_early).astype(BF16)
    pl.semaphore_wait(near, 3)
    s_across = ctx_s(s_recv.at[pair], s_recv.at[pair], 0, across)
    s_across.start()

    mine(all_b, to_x, late_b)

    for k in range(lanes):
        a = a8[:, :, lane(k)]
        rk = rate8[:, :, lane(k)]
        for at, s in enumerate((1, 2, 4)):
            dec[at, :, :, lane(k)] = jnp.exp(-(span * s) * rk)
        dec[3, :, :, lane(k)] = jnp.exp(-span * (SUB - 1.0 - place_f) * rk)
        dec[4, :, :, lane(k)] = jnp.exp(-span * place_f * rk)

        def lift(i, carry, a=a, k=k):
            h, v = carry
            h = a * h + at_step(x32, i, k)[None]
            return h, a * v + h

        _, v = lax.fori_loop(0, steps, lift, (zero, zero), unroll=8)
        v8[:, :, lane(k)] = a * v

    x_a1.wait_recv()
    r_xa1 = relay(ox, z, a1, to_r)
    r_b1.wait_recv()
    r_ob = relay(xl, zl, b1, to_r)
    relay(xl, zl, b1, to_x, late_b)
    l_b2.wait_recv()
    l_ob = relay(xl, zr, b2, to_l)
    relay(xl, zr, b2, to_x, late_b)
    s_across.wait_recv()

    @pl.loop(1, n_y)
    def _(step):
        s_copy(lax.rem(y + step, n_y)).start()

    x_a2.wait_recv()
    l_xa2 = relay(ox, z, a2, to_l)
    r_b2.wait_recv()
    relay(xl, zl, b2, to_x, late_b)
    l_b1.wait_recv()
    relay(xl, zr, b1, to_x, late_b)
    relay(ox, z, a2, to_r, late_a)
    relay(ox, z, a1, to_l, late_a)

    def join(sender, total):
        return far * far * total + s_recv[sender].astype(F32)

    got_y = s_recv.at[pl.ds(0, pairs - 2)]
    pltpu.make_async_copy(got_y, got_y, s_rs.at[1]).wait()
    none = jnp.zeros((modes, chans // 2), F32)
    h_in = lax.fori_loop(0, pair, join, jnp.zeros((modes, chans), F32))
    h_in = jnp.where(core == 0, h_in, far * h_in + s_sib[...])
    for n in range(modes):
        in8[n] = jnp.broadcast_to(h_in[n : n + 1], (SUB, chans))

    r_a.wait_recv()
    l_a.wait_recv()
    relay(xl, zl, a1, to_r, late_a)
    relay(xl, zr, a2, to_l, late_a)

    for k in range(lanes // 2):
        a, c = a8[:, :, lane(k)], c8[:, :, lane(k)]
        skip = skip_ref[:, lane(k)]
        start = ex8[:, :, lane(k)] + dec[4, :, :, lane(k)] * in8[:, :, lane(k)]
        v = v8[:, :, lane(k)] + span * a * dec[0, :, :, lane(k)] * start
        v8[:, :, lane(k)] = v
        u = jnp.sum(dec[3, :, :, lane(k)] * v, axis=1, keepdims=True)
        red[:, pl.ds(2 * lanes + k, 1), :] = u

        def emit(i, h, a=a, c=c, skip=skip, k=k):
            now = at_step(x32, i, k)
            h = a * h + now[None]
            hall[i, :, :, lane(k)] = h
            y32[k, pl.ds(i, SUB, stride=steps), :] = jnp.sum(c * h, axis=0) + skip * now
            return h

        lax.fori_loop(0, steps, emit, start, unroll=8)
        mb[:, lane(k)] = y32[k].astype(BF16)

    r_xa1.wait_recv()
    l_xa2.wait_recv()
    relay(ox, zl, a1, to_r, late_a)
    relay(ox, zr, a2, to_l, late_a)

    r_ob.wait_recv()
    relay(xl, zo, b1, to_x, late_b)
    l_ob.wait_recv()
    x_ob2 = relay(xl, zo, b2, to_x)

    for k in range(lanes // 2, lanes):
        a, c = a8[:, :, lane(k)], c8[:, :, lane(k)]
        skip = skip_ref[:, lane(k)]
        start = ex8[:, :, lane(k)] + dec[4, :, :, lane(k)] * in8[:, :, lane(k)]
        v = v8[:, :, lane(k)] + span * a * dec[0, :, :, lane(k)] * start
        v8[:, :, lane(k)] = v
        u = jnp.sum(dec[3, :, :, lane(k)] * v, axis=1, keepdims=True)
        red[:, pl.ds(2 * lanes + k, 1), :] = u

        def emit(i, h, a=a, c=c, skip=skip, k=k):
            now = at_step(x32, i, k)
            h = a * h + now[None]
            hall[i, :, :, lane(k)] = h
            y32[k, pl.ds(i, SUB, stride=steps), :] = jnp.sum(c * h, axis=0) + skip * now
            return h

        lax.fori_loop(0, steps, emit, start, unroll=8)
        mb[:, lane(k)] = y32[k].astype(BF16)

    def rs(src, dst, peer, index):
        copy = pltpu.make_async_remote_copy(
            src_ref=src,
            dst_ref=dst,
            send_sem=rs_s,
            recv_sem=rs_r.at[index],
            device_id=peer,
            device_id_type=MESH,
        )
        copy.start()

    at_x1, at_az1, at_az2 = 0, A_PIECES, 2 * A_PIECES
    at_bz1 = at_az2 + 1
    at_bz2 = at_bz1 + B_PIECES
    at_x3 = at_bz2 + B_PIECES
    done = {"x1": 0, "az1": 0, "bz1": 0, "bz2": 0}

    def following(name):
        done[name] += 1
        return done[name] - 1

    def a_place(i):
        return unit * sum(A_SHARES[:i]), unit * A_SHARES[i]

    def a_span(i):
        return pl.ds(*a_place(i))

    def a_halves(i):
        at, width = a_place(i)
        return pl.ds(at, width // 2), pl.ds(at + width // 2, width // 2)

    def a_half(i):
        at, width = a_place(i)
        return pl.ds(at // 2, width // 2)

    def b_place(i):
        return unit * sum(B_SHARES[:i]), unit * B_SHARES[i]

    def b_span(i, base=split):
        at, width = b_place(i)
        return pl.ds(base + at, width)

    def b_halves(i):
        at, width = b_place(i)
        return pl.ds(split + at, width // 2), pl.ds(split + at + width // 2, width // 2)

    def b_half(i):
        at, width = b_place(i)
        return pl.ds(at // 2, width // 2)

    w_copy.wait()

    def project(lo, hi):
        p = jnp.dot(mb[...], w_v[:, lo:hi], preferred_element_type=F32)
        part[:, :, :, lo:hi] = p.astype(BF16).reshape(NX, NZ, rows, hi - lo)

    def send_z1(i):
        h1, h2 = b_halves(i)
        rs(part.at[:, zo, :, h1], bl1.at[:, :, b_half(i)], to_r, at_bz1 + i)
        rs(part.at[:, zo, :, h2], br1.at[:, :, b_half(i)], to_l, at_bz1 + i)

    middle = split + b_place(2)[0]
    project(split, middle)
    send_z1(0)
    send_z1(1)
    project(middle, dim)
    for i in range(2, B_PIECES):
        send_z1(i)
    project(0, split)
    for i in range(A_PIECES):
        rs(part.at[ox, :, :, a_span(i)], bx1.at[:, :, a_span(i)], to_x, at_x1 + i)

    wait_bytes(ag_r.at[late_a], 6 * rows, quarter)
    ins[4].wait()

    def project_back(lo, hi, fresh=False):
        left = og[:, :, :, lo:hi].reshape(tok, hi - lo)
        for k in range(lanes):
            got = lax.dot_general(
                left,
                w_v[k * LANE : (k + 1) * LANE, lo:hi],
                (((1,), (1,)), ((), ())),
                preferred_element_type=F32,
            )
            g32[k] = got if fresh else g32[k] + got

    project_back(0, half, True)

    def merge(ref, got):
        ref[...] = (ref[...].astype(F32) + got[...].astype(F32)).astype(BF16)

    def take_b_z1():
        i = following("bz1")
        h1, h2 = b_halves(i)
        wait_bytes(rs_r.at[at_bz1 + i], 2 * NX * rows, b_place(i)[1] // 2)
        merge(part.at[:, zr, :, h1], bl1.at[:, :, b_half(i)])
        rs(part.at[:, zr, :, b_span(i)], bl2.at[:, :, b_span(i, 0)], to_r, at_bz2 + i)
        merge(part.at[:, zl, :, h2], br1.at[:, :, b_half(i)])
        rs(part.at[:, zl, :, b_span(i)], br2.at[:, :, b_span(i, 0)], to_l, at_bz2 + i)

    def take_x1():
        i = following("x1")
        here = bx1.at[:, :, a_span(i)]
        pltpu.make_async_copy(here, here, rs_r.at[at_x1 + i]).wait()
        h1, h2 = a_halves(i)
        merge(part.at[xl, zo, :, a_span(i)], here.at[zo])
        rs(part.at[xl, zo, :, h1], al1.at[:, a_half(i)], to_r, at_az1 + i)
        rs(part.at[xl, zo, :, h2], ar1.at[:, a_half(i)], to_l, at_az1 + i)
        merge(part.at[xl, zr, :, a_span(i)], here.at[zr])
        merge(part.at[xl, zl, :, a_span(i)], here.at[zl])

    def take_z1():
        i = following("az1")
        h1, h2 = a_halves(i)
        wait_bytes(rs_r.at[at_az1 + i], 2 * rows, a_place(i)[1] // 2)
        merge(part.at[xl, zr, :, h1], al1.at[:, a_half(i)])
        rs(part.at[xl, zr, :, a_span(i)], al2.at[:, a_span(i)], to_r, at_az2)
        merge(part.at[xl, zl, :, h2], ar1.at[:, a_half(i)])
        rs(part.at[xl, zl, :, a_span(i)], ar2.at[:, a_span(i)], to_l, at_az2)

    def total3(ref, left, right):
        return ref[...].astype(F32) + left[...].astype(F32) + right[...].astype(F32)

    def take_b_z2():
        i = following("bz2")
        wait_bytes(rs_r.at[at_bz2 + i], 2 * NX * rows, b_place(i)[1])
        far_part = part.at[ox, z, :, b_span(i)]
        here = b_span(i, 0)
        far_part[...] = total3(far_part, bl2.at[ox, :, here], br2.at[ox, :, here]).astype(BF16)
        rs(far_part, bx3.at[:, here], to_x, at_x3)

    wait_bytes(ag_r.at[late_b], 7 * rows, quarter)

    project_back(half, half + quarter)
    x_ob2.wait_recv()
    project_back(half + quarter, dim)
    take_b_z1()

    for k in range(lanes):
        g32[k] = g32[k].astype(BF16).astype(F32)
        sk = jnp.sum(g32[k] * x32[k], axis=0, keepdims=True)
        red[:, pl.ds(4 * lanes + k, 1), :] = jnp.broadcast_to(sk[None], (modes, 1, LANE))

    hm = modes // 2
    zh = jnp.zeros((hm, SUB, LANE), F32)
    pm = place[:hm]
    for m0 in (0, hm):
        ms = pl.ds(m0, hm)
        for k in range(lanes):
            lv = lane(k)
            a = a8[ms, :, lv]

            def back(j, carry, a=a, k=k, lv=lv, ms=ms):
                h, gs, mloc = carry
                i = steps - 1 - j
                now = at_step(g32, i, k)[None]
                held = hall[i, ms, :, lv]
                h = a * h + now
                return h, gs + now * held, mloc + h * held

            end, gs, mloc = lax.fori_loop(0, steps, back, (zh, zh, zh), unroll=8)
            for at, s in enumerate((1, 2, 4)):
                moved = jnp.where(pm < SUB - s, pltpu.roll(end, SUB - s, 1), 0.0)
                end = end + dec[at, ms, :, lv] * moved
            ex = jnp.where(pm < SUB - 1, pltpu.roll(end, SUB - 1, 1), 0.0)
            ex8[ms, :, lv] = ex
            first = jnp.where(pm == 0, end, 0.0)
            r_own[ms, lv] = jnp.sum(first, axis=1)
            for at, value in ((0, gs), (1, mloc + ex * v8[ms, :, lv]), (3, first)):
                red[ms, pl.ds(at * lanes + k, 1), :] = jnp.sum(value, axis=1, keepdims=True)

        @pl.loop(m0, m0 + hm)
        def _(peer):
            @pl.when(peer != me)
            def _():
                p_copy(peer).start()

        if m0 == 0:
            take_x1()
            take_b_z1()

    sib_back = sib_copy(2, r_own, r_sib)
    sib_back.start()
    rr[me] = red[me]

    sib_back.wait_recv()
    mine_r, sib_r_half = r_own[:, my_half], r_sib[:, my_half]
    r_early = jnp.where(core == 0, mine_r, sib_r_half)
    r_late = jnp.where(core == 0, sib_r_half, mine_r)
    r_pair[...] = (r_early + far_half * r_late).astype(BF16)

    @pl.loop(0, pair)
    def _(peer):
        r_copy(peer, pair).start()


    take_x1()
    take_b_z1()
    take_b_z1()

    take_b_z2()

    take_z1()

    wait_all(rr, p_rs)

    far_me = far4[me]

    def owner(j, carry):
        lam, gsum, msum, ksum = carry
        sender = n_ctx - 1 - j
        got = rr[sender]
        gsum = gsum + got[:lanes]
        msum = msum + got[lanes : 2 * lanes] + lam * got[2 * lanes : 3 * lanes]
        ksum = ksum + got[4 * lanes : 5 * lanes]
        return far_me * lam + got[3 * lanes : 4 * lanes], gsum, msum, ksum

    zl4 = jnp.zeros((lanes, LANE), F32)
    _, gsum, msum, ksum = lax.fori_loop(0, n_ctx, owner, (zl4, zl4, zl4, zl4))
    fin[me, pl.ds(0, lanes), :] = gsum
    fin[me, pl.ds(lanes, lanes), :] = msum
    others(lambda peer: q_copy(peer).start())
    scale = 1.0 / math.sqrt(seq)
    gskip_ref[...] = ksum * scale
    saves = [save(0, gskip_ref, gskip_hbm)]

    take_b_z2()

    take_z1()

    def join_back(j, total):
        sender = pairs - 1 - j
        r_copy(0, sender).wait_recv()
        return far_half * far_half * total + r_recv[sender].astype(F32)

    l_t[:, my_half] = lax.fori_loop(0, pairs - 1 - pair, join_back, none)
    sib_l = sib_copy(3, l_t.at[:, my_half], l_t.at[:, my_half])
    sib_l.start()

    take_b_z2()

    take_b_z2()

    sib_l.wait_recv()
    l_in = jnp.where(core == 1, l_t[...], far * l_t[...] + r_sib[...])
    for n in range(modes):
        in8[n] = jnp.broadcast_to(l_in[n : n + 1], (SUB, chans))

    for k in range(lanes):
        a, c = a8[:, :, lane(k)], c8[:, :, lane(k)]
        skip = skip_ref[:, lane(k)]
        start = ex8[:, :, lane(k)] + dec[3, :, :, lane(k)] * in8[:, :, lane(k)]

        def emit_back(j, h, a=a, c=c, skip=skip, k=k):
            i = steps - 1 - j
            now = at_step(g32, i, k)
            h = a * h + now[None]
            y32[k, pl.ds(i, SUB, stride=steps), :] = jnp.sum(c * h, axis=0) + skip * now
            return h

        lax.fori_loop(0, steps, emit_back, start, unroll=8)
        gi_ref[:, lane(k)] = y32[k].astype(BF16)
    saves.append(save(1, gi_ref, gi_hbm))

    wait_bytes(rs_r.at[at_az2], 2 * rows, split)
    out_ref[:, :split] = (
        total3(part.at[xl, z, :, pl.ds(0, split)], al2, ar2) + bx1[z].astype(F32)
    ).astype(BF16)

    part_a, part_b = pl.ds(0, split), pl.ds(split, dim - split)
    saves.append(save(2, out_ref.at[:, part_a], out_hbm.at[:, part_a]))

    wait_bytes(rs_r.at[at_x3], rows, dim - split)
    out_ref[:, split:] = (
        total3(part.at[xl, z, :, pl.ds(split, dim - split)], bl2.at[xl], br2.at[xl])
        + bx3[...].astype(F32)
    ).astype(BF16)

    saves.append(save(3, out_ref.at[:, part_b], out_hbm.at[:, part_b]))

    wait_all(fin, q_rs)

    for k in range(lanes):
        rate = rate_t[:, lane(k)]
        gr = jnp.sum(fin[:, pl.ds(k, 1), :], axis=1)
        ml = jnp.sum(fin[:, pl.ds(lanes + k, 1), :], axis=1)
        gres_ref[:, lane(k)] = gr * (jnp.sqrt(2.0 * rate) * scale)
        glog_ref[:, lane(k)] = c_t[:, lane(k)] * ((0.5 + rate) * gr - rate * ml) * scale

    saves += [save(4, gres_ref, gres_hbm), save(5, glog_ref, glog_hbm)]

    sent = w_v.at[pl.ds(0, tok - rows)]
    pltpu.make_async_copy(sent, sent, ag_s).wait()
    pltpu.make_async_copy(sent, sent, rs_s).wait()
    for copy in (sib_first, sib_back, sib_l):
        copy.wait_send()
    rest = s_recv.at[pl.ds(0, 2 * n_y - 1)]
    pltpu.make_async_copy(rest, rest, s_ss).wait()

    @pl.loop(0, pair)
    def _(peer):
        r_copy(peer, pair).wait_send()

    wait_all(rr, p_ss)
    wait_all(fin, q_ss)

    for copy in saves:
        copy.wait()


def store(*refs):
    n = (len(refs) - 2) // 3
    ins, outs, bufs = refs[:n], refs[n : 2 * n], refs[2 * n : 3 * n]
    loads = [pltpu.make_async_copy(ins[i], bufs[i], refs[-2].at[i]) for i in range(n)]
    saves = [pltpu.make_async_copy(bufs[i], outs[i], refs[-1].at[i]) for i in range(n)]
    for copy in loads:
        copy.start()
    for load, copy in zip(loads, saves):
        load.wait()
        copy.start()
    for copy in saves:
        copy.wait()


def per_device(inputs, residue, log_rate, skip, out_weight, out_grad):
    n_ctx = lax.axis_size("ctx")
    tok, chans = inputs.shape
    modes = residue.shape[1]
    dim = out_weight.shape[1]
    rows = tok // (NX * NZ)
    steps = tok // SUB
    lanes = chans // LANE
    split = dim // SHARES * sum(A_SHARES)
    b_cols = dim - split
    wide = (modes, SUB, chans)
    flat = (modes, chans)
    packed = -(-5 * lanes // SUB) * SUB
    anywhere = pl.BlockSpec(memory_space=pl.ANY)
    dma = pltpu.SemaphoreType.DMA
    results = (
        jax.ShapeDtypeStruct((rows, dim), BF16),
        jax.ShapeDtypeStruct((tok, chans), BF16),
        jax.ShapeDtypeStruct(flat, F32),
        jax.ShapeDtypeStruct(flat, F32),
        jax.ShapeDtypeStruct((lanes, LANE), F32),
    )
    held_shapes = [pltpu.VMEM(r.shape, r.dtype) for r in results]
    held = pl.pallas_call(
        functools.partial(kernel, tok * n_ctx, n_ctx),
        out_shape=results,
        in_specs=[anywhere] * 6,
        out_specs=(anywhere,) * 5,
        scratch_shapes=[
            *held_shapes,
            pltpu.VMEM((tok, chans), BF16),
            pltpu.VMEM(flat, F32),
            pltpu.VMEM(flat, F32),
            pltpu.VMEM((1, chans), F32),
            pltpu.VMEM((chans, dim), BF16),
            pltpu.VMEM((NX, NZ, rows, dim), BF16),
            pltpu.VMEM((NX, NZ, rows, dim), BF16),
            pltpu.VMEM((steps, *wide), F32),
            pltpu.VMEM((lanes, tok, LANE), F32),
            pltpu.VMEM((lanes, tok, LANE), F32),
            pltpu.VMEM((lanes, tok, LANE), F32),
            pltpu.VMEM((tok, chans), BF16),
            pltpu.VMEM(flat, F32),
            pltpu.VMEM(flat, F32),
            pltpu.VMEM((modes, lanes, LANE), F32),
            pltpu.VMEM(wide, F32),
            pltpu.VMEM(wide, F32),
            pltpu.VMEM(wide, F32),
            pltpu.VMEM(wide, F32),
            pltpu.VMEM(wide, F32),
            pltpu.VMEM(wide, F32),
            pltpu.VMEM(flat, F32),
            pltpu.VMEM(flat, F32),
            pltpu.VMEM((n_ctx // 2, modes, chans), BF16),
            pltpu.VMEM(flat, F32),
            pltpu.VMEM(flat, F32),
            pltpu.VMEM((modes, chans // 2), BF16),
            pltpu.VMEM((n_ctx // 2, modes, chans // 2), BF16),
            pltpu.VMEM(flat, F32),
            pltpu.VMEM((modes, packed, LANE), F32),
            pltpu.VMEM((n_ctx, packed, LANE), F32),
            pltpu.VMEM((5, *wide), F32),
            pltpu.VMEM((n_ctx, 2 * lanes, LANE), F32),
            pltpu.VMEM((NZ, rows, split), BF16),
            pltpu.VMEM((rows, split // 2), BF16),
            pltpu.VMEM((rows, split // 2), BF16),
            pltpu.VMEM((rows, split), BF16),
            pltpu.VMEM((rows, split), BF16),
            pltpu.VMEM((NX, rows, b_cols // 2), BF16),
            pltpu.VMEM((NX, rows, b_cols // 2), BF16),
            pltpu.VMEM((NX, rows, b_cols), BF16),
            pltpu.VMEM((NX, rows, b_cols), BF16),
            pltpu.VMEM((rows, b_cols), BF16),
            pltpu.SemaphoreType.REGULAR,
            dma((5,)),
            dma((6,)),
            dma,
            dma,
            dma((15,)),
            dma,
            dma((2 * (A_PIECES + B_PIECES) + 2,)),
            dma,
            dma((2,)),
            dma((n_ctx // 2,)),
            dma((n_ctx // 2,)),
            dma((4,)),
            dma((4,)),
            *[dma] * 4,
        ],
        compiler_params=pltpu.CompilerParams(
            collective_id=0, has_side_effects=True, vmem_limit_bytes=56 * 1024 * 1024
        ),
    )(inputs, residue.T, log_rate.T, skip.reshape(1, chans), out_weight, out_grad)
    out, gi, gres, glog, gskip = pl.pallas_call(
        store,
        out_shape=results,
        in_specs=[anywhere] * 5,
        out_specs=(anywhere,) * 5,
        scratch_shapes=[*held_shapes, dma((5,)), dma((5,))],
    )(*held)
    return out, gi, gres.T, glog.T, gskip.reshape(chans)


def solution(mesh):
    return jax.shard_map(
        per_device,
        mesh=mesh,
        in_specs=(
            P("ctx", "tp"),
            P("tp", None),
            P("tp", None),
            P("tp"),
            P("tp", None),
            P(("ctx", "tp"), None),
        ),
        out_specs=(P(("ctx", "tp"), None), P("ctx", "tp"), P("tp", None), P("tp", None), P("tp")),
        check_vma=False,
    )
```

```python
import functools
import math

import jax
import jax.numpy as jnp
from jax import lax
from jax.experimental import pallas as pl
from jax.experimental.pallas import tpu as pltpu
from jax.sharding import PartitionSpec as P

MESH = pl.DeviceIdType.MESH
F32 = jnp.float32
BF16 = jnp.bfloat16
SUB = 8
LANE = 128
NX, NZ = 2, 4
SHARES, A_SHARES, B_SHARES = 32, (4, 4), (8, 8, 5, 3)
A_PIECES, B_PIECES = len(A_SHARES), len(B_SHARES)


def kernel(
    seq,
    n_ctx,
    x_hbm,
    res_hbm,
    lr_hbm,
    skip_hbm,
    w_hbm,
    og_hbm,
    out_ref,
    gi_ref,
    gres_ref,
    glog_ref,
    gskip_ref,
    x_ref,
    res_ref,
    lr_ref,
    skip_ref,
    w_v,
    og,
    part,
    hall,
    x32,
    y32,
    g32,
    mb,
    rate_t,
    c_t,
    far4,
    rate8,
    a8,
    c8,
    ex8,
    in8,
    v8,
    s_own,
    s_sib,
    s_recv,
    r_own,
    r_sib,
    r_pair,
    r_recv,
    l_t,
    red,
    rr,
    dec,
    fin,
    bx1,
    al1,
    ar1,
    al2,
    ar2,
    bl1,
    br1,
    bl2,
    br2,
    bx3,
    near,
    in_sem,
    w_sem,
    ag_s,
    ag_r,
    rs_s,
    rs_r,
    s_ss,
    s_rs,
    r_ss,
    r_rs,
    sib_s,
    sib_r,
    p_ss,
    p_rs,
    q_ss,
    q_rs,
):
    tok, chans = x_ref.shape
    modes = res_ref.shape[0]
    dim = w_v.shape[1]
    rows = tok // (NX * NZ)
    steps = tok // SUB
    lanes = chans // LANE
    half, quarter = dim // 2, dim // 4
    unit = dim // SHARES
    split = unit * sum(A_SHARES)

    me = lax.axis_index("ctx")
    tp = lax.axis_index("tp")
    xl, z = tp // NZ, lax.rem(tp, NZ)
    ox = 1 - xl
    zr, zl, zo = lax.rem(z + 1, NZ), lax.rem(z + 3, NZ), lax.rem(z + 2, NZ)
    to_x = {"tp": ox * NZ + z}
    to_r = {"tp": xl * NZ + zr}
    to_l = {"tp": xl * NZ + zl}
    pairs = n_ctx // 2
    pair, core = me // 2, lax.rem(me, 2)
    y, xh, n_y = me // 4, lax.rem(pair, 2), n_ctx // 4
    across = me + 2 - 4 * xh
    to_sib, to_xh = {"ctx": me + 1 - 2 * core}, {"ctx": across}
    to_x_other = {"ctx": across, "tp": ox * NZ + z}
    to_up, to_down = {"ctx": lax.rem(me + 4, n_ctx)}, {"ctx": lax.rem(me + n_ctx - 4, n_ctx)}
    my_half = pl.ds(pl.multiple_of(core * (chans // 2), chans // 2), chans // 2)

    w_copy = pltpu.make_async_copy(w_hbm, w_v, w_sem)

    barrier = pltpu.get_barrier_semaphore()
    for peer in (to_x, to_r, to_l, to_x_other, to_sib, to_up, to_down):
        pl.semaphore_signal(barrier, inc=1, device_id=peer, device_id_type=MESH)

    ins = [
        pltpu.make_async_copy(src, dst, in_sem.at[i])
        for i, (src, dst) in enumerate(
            (
                (lr_hbm, lr_ref),
                (res_hbm, res_ref),
                (x_hbm, x_ref),
                (skip_hbm, skip_ref),
                (og_hbm, og.at[xl, z]),
            )
        )
    ]
    for copy in ins:
        copy.start()
    w_copy.start()

    pl.semaphore_wait(barrier, 7)
    for peer in (to_x, to_up, to_down):
        pl.semaphore_signal(near, inc=1, device_id=peer, device_id_type=MESH)

    def ctx_copy(src, dst, send, recv, peer):
        return pltpu.make_async_remote_copy(
            src_ref=src,
            dst_ref=dst,
            send_sem=send,
            recv_sem=recv,
            device_id={"ctx": peer},
            device_id_type=MESH,
        )

    def ctx_s(src, dst, index, peer):
        return ctx_copy(src, dst, s_ss, s_rs.at[index], peer)

    def s_copy(other):
        both = s_recv.at[pl.ds(2 * y, 2)]
        return ctx_s(both, both, 1, 4 * other + 2 * xh + core)

    def r_copy(peer, sender):
        return ctx_copy(r_pair, r_recv.at[sender], r_ss.at[peer], r_rs.at[sender], 2 * peer + core)

    def sib_copy(index, src, dst):
        return pltpu.make_async_remote_copy(
            src_ref=src,
            dst_ref=dst,
            send_sem=sib_s.at[index],
            recv_sem=sib_r.at[index],
            device_id=to_sib,
            device_id_type=MESH,
        )

    def p_copy(peer):
        return ctx_copy(red.at[peer], rr.at[me], p_ss, p_rs, peer)

    def q_copy(peer):
        return ctx_copy(fin.at[me], fin.at[me], q_ss, q_rs, peer)

    def wait_all(ref, sem):
        rest = ref.at[pl.ds(0, n_ctx - 1)]
        pltpu.make_async_copy(rest, rest, sem).wait()

    def others(step):
        pl.loop(1, n_ctx)(lambda k: step(lax.rem(me + k, n_ctx)))

    tags = iter(range(2, 100))

    def ag(src, dst, peer, group):
        copy = pltpu.make_async_remote_copy(
            src_ref=src,
            dst_ref=dst,
            send_sem=ag_s,
            recv_sem=ag_r.at[next(tags) if group is None else group],
            device_id=peer,
            device_id_type=MESH,
        )
        copy.start()
        return copy

    def relay(shard_x, shard_z, columns, peer, group=None):
        piece = og.at[shard_x, shard_z, :, columns]
        return ag(piece, piece, peer, group)

    def mine(columns, peer, group=None):
        return ag(og_hbm.at[:, columns], og.at[xl, z, :, columns], peer, group)

    def wait_bytes(sem, depth, width):
        size = w_v.at[pl.ds(0, depth), pl.ds(0, width)]
        pltpu.make_async_copy(size, size, sem).wait()

    all_a, all_b = pl.ds(0, half), pl.ds(half, half)
    a1, a2 = pl.ds(0, quarter), pl.ds(quarter, quarter)
    b1, b2 = pl.ds(half, quarter), pl.ds(half + quarter, quarter)
    late_a, late_b = 0, 1

    x_a1, r_b1, l_b2 = mine(a1, to_x), mine(b1, to_r), mine(b2, to_l)
    x_a2, r_b2, l_b1 = mine(a2, to_x), mine(b2, to_r), mine(b1, to_l)

    for copy in ins[:4]:
        copy.wait()
    rate = jnp.exp(lr_ref[...]) / seq
    rate_t[...] = rate
    c_t[...] = res_ref[...] * jnp.sqrt(2.0 * rate)
    far = jnp.exp(-float(tok) * rate)
    for n in range(modes):
        row = pl.ds(n, 1)
        rate8[n] = jnp.broadcast_to(rate_t[row, :], (SUB, chans))
        c8[n] = jnp.broadcast_to(c_t[row, :], (SUB, chans))
    a8[...] = jnp.exp(-rate8[...])

    def lane(k):
        return pl.ds(k * LANE, LANE)

    for k in range(lanes):
        x32[k] = x_ref[:, lane(k)].astype(F32)
        far4[:, pl.ds(k, 1), :] = far[:, k * LANE : (k + 1) * LANE][:, None, :]

    place = lax.broadcasted_iota(jnp.int32, (modes, SUB, LANE), 1)
    place_f = place.astype(F32)
    span = float(steps)
    zero = jnp.zeros((modes, SUB, LANE), F32)

    def at_step(ref, i, k):
        return ref[k, pl.ds(i, SUB, stride=steps), :]

    for k in range(lanes):
        a = a8[:, :, lane(k)]

        def grow(i, h, a=a, k=k):
            return a * h + at_step(x32, i, k)[None]

        end = lax.fori_loop(0, steps, grow, zero, unroll=8)
        rk = rate8[:, :, lane(k)]
        for s in (1, 2, 4):
            moved = jnp.where(place >= s, pltpu.roll(end, s, 1), 0.0)
            end = end + jnp.exp(-(span * s) * rk) * moved
        ex8[:, :, lane(k)] = jnp.where(place >= 1, pltpu.roll(end, 1, 1), 0.0)
        s_own[:, lane(k)] = jnp.sum(jnp.where(place == SUB - 1, end, 0.0), axis=1)

    sib_first = sib_copy(0, s_own, s_sib)
    sib_first.start()

    r_a, l_a = mine(all_a, to_r), mine(all_a, to_l)

    far_half = jnp.exp(-float(tok) * rate_t[:, my_half])
    sib_first.wait_recv()
    s_early = jnp.where(core == 0, s_own[...], s_sib[...])
    s_late = jnp.where(core == 0, s_sib[...], s_own[...])
    far = jnp.exp(-float(tok) * rate_t[...])
    s_recv[pair] = (s_late + far * s_early).astype(BF16)
    pl.semaphore_wait(near, 3)
    s_across = ctx_s(s_recv.at[pair], s_recv.at[pair], 0, across)
    s_across.start()

    mine(all_b, to_x, late_b)

    for k in range(lanes):
        a = a8[:, :, lane(k)]
        rk = rate8[:, :, lane(k)]
        for at, s in enumerate((1, 2, 4)):
            dec[at, :, :, lane(k)] = jnp.exp(-(span * s) * rk)
        dec[3, :, :, lane(k)] = jnp.exp(-span * (SUB - 1.0 - place_f) * rk)
        dec[4, :, :, lane(k)] = jnp.exp(-span * place_f * rk)

        def lift(i, carry, a=a, k=k):
            h, v = carry
            h = a * h + at_step(x32, i, k)[None]
            return h, a * v + h

        _, v = lax.fori_loop(0, steps, lift, (zero, zero), unroll=8)
        v8[:, :, lane(k)] = a * v

    x_a1.wait_recv()
    r_xa1 = relay(ox, z, a1, to_r)
    r_b1.wait_recv()
    r_ob = relay(xl, zl, b1, to_r)
    relay(xl, zl, b1, to_x, late_b)
    l_b2.wait_recv()
    l_ob = relay(xl, zr, b2, to_l)
    relay(xl, zr, b2, to_x, late_b)
    s_across.wait_recv()

    @pl.loop(1, n_y)
    def _(step):
        s_copy(lax.rem(y + step, n_y)).start()

    x_a2.wait_recv()
    l_xa2 = relay(ox, z, a2, to_l)
    r_b2.wait_recv()
    relay(xl, zl, b2, to_x, late_b)
    l_b1.wait_recv()
    relay(xl, zr, b1, to_x, late_b)
    relay(ox, z, a2, to_r, late_a)
    relay(ox, z, a1, to_l, late_a)

    def join(sender, total):
        return far * far * total + s_recv[sender].astype(F32)

    got_y = s_recv.at[pl.ds(0, pairs - 2)]
    pltpu.make_async_copy(got_y, got_y, s_rs.at[1]).wait()
    none = jnp.zeros((modes, chans // 2), F32)
    h_in = lax.fori_loop(0, pair, join, jnp.zeros((modes, chans), F32))
    h_in = jnp.where(core == 0, h_in, far * h_in + s_sib[...])
    for n in range(modes):
        in8[n] = jnp.broadcast_to(h_in[n : n + 1], (SUB, chans))

    r_a.wait_recv()
    l_a.wait_recv()
    relay(xl, zl, a1, to_r, late_a)
    relay(xl, zr, a2, to_l, late_a)

    for k in range(lanes // 2):
        a, c = a8[:, :, lane(k)], c8[:, :, lane(k)]
        skip = skip_ref[:, lane(k)]
        start = ex8[:, :, lane(k)] + dec[4, :, :, lane(k)] * in8[:, :, lane(k)]
        v = v8[:, :, lane(k)] + span * a * dec[0, :, :, lane(k)] * start
        v8[:, :, lane(k)] = v
        u = jnp.sum(dec[3, :, :, lane(k)] * v, axis=1, keepdims=True)
        red[:, pl.ds(2 * lanes + k, 1), :] = u

        def emit(i, h, a=a, c=c, skip=skip, k=k):
            now = at_step(x32, i, k)
            h = a * h + now[None]
            hall[i, :, :, lane(k)] = h
            y32[k, pl.ds(i, SUB, stride=steps), :] = jnp.sum(c * h, axis=0) + skip * now
            return h

        lax.fori_loop(0, steps, emit, start, unroll=8)
        mb[:, lane(k)] = y32[k].astype(BF16)

    r_xa1.wait_recv()
    l_xa2.wait_recv()
    relay(ox, zl, a1, to_r, late_a)
    relay(ox, zr, a2, to_l, late_a)

    r_ob.wait_recv()
    relay(xl, zo, b1, to_x, late_b)
    l_ob.wait_recv()
    x_ob2 = relay(xl, zo, b2, to_x)

    for k in range(lanes // 2, lanes):
        a, c = a8[:, :, lane(k)], c8[:, :, lane(k)]
        skip = skip_ref[:, lane(k)]
        start = ex8[:, :, lane(k)] + dec[4, :, :, lane(k)] * in8[:, :, lane(k)]
        v = v8[:, :, lane(k)] + span * a * dec[0, :, :, lane(k)] * start
        v8[:, :, lane(k)] = v
        u = jnp.sum(dec[3, :, :, lane(k)] * v, axis=1, keepdims=True)
        red[:, pl.ds(2 * lanes + k, 1), :] = u

        def emit(i, h, a=a, c=c, skip=skip, k=k):
            now = at_step(x32, i, k)
            h = a * h + now[None]
            hall[i, :, :, lane(k)] = h
            y32[k, pl.ds(i, SUB, stride=steps), :] = jnp.sum(c * h, axis=0) + skip * now
            return h

        lax.fori_loop(0, steps, emit, start, unroll=8)
        mb[:, lane(k)] = y32[k].astype(BF16)

    def rs(src, dst, peer, index):
        copy = pltpu.make_async_remote_copy(
            src_ref=src,
            dst_ref=dst,
            send_sem=rs_s,
            recv_sem=rs_r.at[index],
            device_id=peer,
            device_id_type=MESH,
        )
        copy.start()

    at_x1, at_az1, at_az2 = 0, A_PIECES, 2 * A_PIECES
    at_bz1 = at_az2 + 1
    at_bz2 = at_bz1 + B_PIECES
    at_x3 = at_bz2 + B_PIECES
    done = {"x1": 0, "az1": 0, "bz1": 0, "bz2": 0}

    def following(name):
        done[name] += 1
        return done[name] - 1

    def a_place(i):
        return unit * sum(A_SHARES[:i]), unit * A_SHARES[i]

    def a_span(i):
        return pl.ds(*a_place(i))

    def a_halves(i):
        at, width = a_place(i)
        return pl.ds(at, width // 2), pl.ds(at + width // 2, width // 2)

    def a_half(i):
        at, width = a_place(i)
        return pl.ds(at // 2, width // 2)

    def b_place(i):
        return unit * sum(B_SHARES[:i]), unit * B_SHARES[i]

    def b_span(i, base=split):
        at, width = b_place(i)
        return pl.ds(base + at, width)

    def b_halves(i):
        at, width = b_place(i)
        return pl.ds(split + at, width // 2), pl.ds(split + at + width // 2, width // 2)

    def b_half(i):
        at, width = b_place(i)
        return pl.ds(at // 2, width // 2)

    w_copy.wait()

    def project(lo, hi):
        p = jnp.dot(mb[...], w_v[:, lo:hi], preferred_element_type=F32)
        part[:, :, :, lo:hi] = p.astype(BF16).reshape(NX, NZ, rows, hi - lo)

    def send_z1(i):
        h1, h2 = b_halves(i)
        rs(part.at[:, zo, :, h1], bl1.at[:, :, b_half(i)], to_r, at_bz1 + i)
        rs(part.at[:, zo, :, h2], br1.at[:, :, b_half(i)], to_l, at_bz1 + i)

    middle = split + b_place(2)[0]
    project(split, middle)
    send_z1(0)
    send_z1(1)
    project(middle, dim)
    for i in range(2, B_PIECES):
        send_z1(i)
    project(0, split)
    for i in range(A_PIECES):
        rs(part.at[ox, :, :, a_span(i)], bx1.at[:, :, a_span(i)], to_x, at_x1 + i)

    wait_bytes(ag_r.at[late_a], 6 * rows, quarter)
    ins[4].wait()

    def project_back(lo, hi, fresh=False):
        left = og[:, :, :, lo:hi].reshape(tok, hi - lo)
        for k in range(lanes):
            got = lax.dot_general(
                left,
                w_v[k * LANE : (k + 1) * LANE, lo:hi],
                (((1,), (1,)), ((), ())),
                preferred_element_type=F32,
            )
            g32[k] = got if fresh else g32[k] + got

    project_back(0, half, True)

    def merge(ref, got):
        ref[...] = (ref[...].astype(F32) + got[...].astype(F32)).astype(BF16)

    def take_b_z1():
        i = following("bz1")
        h1, h2 = b_halves(i)
        wait_bytes(rs_r.at[at_bz1 + i], 2 * NX * rows, b_place(i)[1] // 2)
        merge(part.at[:, zr, :, h1], bl1.at[:, :, b_half(i)])
        rs(part.at[:, zr, :, b_span(i)], bl2.at[:, :, b_span(i, 0)], to_r, at_bz2 + i)
        merge(part.at[:, zl, :, h2], br1.at[:, :, b_half(i)])
        rs(part.at[:, zl, :, b_span(i)], br2.at[:, :, b_span(i, 0)], to_l, at_bz2 + i)

    def take_x1():
        i = following("x1")
        here = bx1.at[:, :, a_span(i)]
        pltpu.make_async_copy(here, here, rs_r.at[at_x1 + i]).wait()
        h1, h2 = a_halves(i)
        merge(part.at[xl, zo, :, a_span(i)], here.at[zo])
        rs(part.at[xl, zo, :, h1], al1.at[:, a_half(i)], to_r, at_az1 + i)
        rs(part.at[xl, zo, :, h2], ar1.at[:, a_half(i)], to_l, at_az1 + i)
        merge(part.at[xl, zr, :, a_span(i)], here.at[zr])
        merge(part.at[xl, zl, :, a_span(i)], here.at[zl])

    def take_z1():
        i = following("az1")
        h1, h2 = a_halves(i)
        wait_bytes(rs_r.at[at_az1 + i], 2 * rows, a_place(i)[1] // 2)
        merge(part.at[xl, zr, :, h1], al1.at[:, a_half(i)])
        rs(part.at[xl, zr, :, a_span(i)], al2.at[:, a_span(i)], to_r, at_az2)
        merge(part.at[xl, zl, :, h2], ar1.at[:, a_half(i)])
        rs(part.at[xl, zl, :, a_span(i)], ar2.at[:, a_span(i)], to_l, at_az2)

    def total3(ref, left, right):
        return ref[...].astype(F32) + left[...].astype(F32) + right[...].astype(F32)

    def take_b_z2():
        i = following("bz2")
        wait_bytes(rs_r.at[at_bz2 + i], 2 * NX * rows, b_place(i)[1])
        far_part = part.at[ox, z, :, b_span(i)]
        here = b_span(i, 0)
        far_part[...] = total3(far_part, bl2.at[ox, :, here], br2.at[ox, :, here]).astype(BF16)
        rs(far_part, bx3.at[:, here], to_x, at_x3)

    take_b_z1()

    wait_bytes(ag_r.at[late_b], 7 * rows, quarter)

    project_back(half, half + quarter)
    x_ob2.wait_recv()
    project_back(half + quarter, dim)

    for k in range(lanes):
        g32[k] = g32[k].astype(BF16).astype(F32)
        sk = jnp.sum(g32[k] * x32[k], axis=0, keepdims=True)
        red[:, pl.ds(4 * lanes + k, 1), :] = jnp.broadcast_to(sk[None], (modes, 1, LANE))

    hm = modes // 2
    zh = jnp.zeros((hm, SUB, LANE), F32)
    pm = place[:hm]
    for m0 in (0, hm):
        ms = pl.ds(m0, hm)
        for k in range(lanes):
            lv = lane(k)
            a = a8[ms, :, lv]

            def back(j, carry, a=a, k=k, lv=lv, ms=ms):
                h, gs, mloc = carry
                i = steps - 1 - j
                now = at_step(g32, i, k)[None]
                held = hall[i, ms, :, lv]
                h = a * h + now
                return h, gs + now * held, mloc + h * held

            end, gs, mloc = lax.fori_loop(0, steps, back, (zh, zh, zh), unroll=8)
            for at, s in enumerate((1, 2, 4)):
                moved = jnp.where(pm < SUB - s, pltpu.roll(end, SUB - s, 1), 0.0)
                end = end + dec[at, ms, :, lv] * moved
            ex = jnp.where(pm < SUB - 1, pltpu.roll(end, SUB - 1, 1), 0.0)
            ex8[ms, :, lv] = ex
            first = jnp.where(pm == 0, end, 0.0)
            r_own[ms, lv] = jnp.sum(first, axis=1)
            for at, value in ((0, gs), (1, mloc + ex * v8[ms, :, lv]), (3, first)):
                red[ms, pl.ds(at * lanes + k, 1), :] = jnp.sum(value, axis=1, keepdims=True)

        @pl.loop(m0, m0 + hm)
        def _(peer):
            @pl.when(peer != me)
            def _():
                p_copy(peer).start()

        if m0 == 0:
            take_x1()
            take_b_z1()

    sib_back = sib_copy(2, r_own, r_sib)
    sib_back.start()
    rr[me] = red[me]

    sib_back.wait_recv()
    mine_r, sib_r_half = r_own[:, my_half], r_sib[:, my_half]
    r_early = jnp.where(core == 0, mine_r, sib_r_half)
    r_late = jnp.where(core == 0, sib_r_half, mine_r)
    r_pair[...] = (r_early + far_half * r_late).astype(BF16)

    @pl.loop(0, pair)
    def _(peer):
        r_copy(peer, pair).start()


    take_x1()
    take_b_z1()
    take_b_z1()

    take_b_z2()

    take_z1()

    wait_all(rr, p_rs)

    far_me = far4[me]

    def owner(j, carry):
        lam, gsum, msum, ksum = carry
        sender = n_ctx - 1 - j
        got = rr[sender]
        gsum = gsum + got[:lanes]
        msum = msum + got[lanes : 2 * lanes] + lam * got[2 * lanes : 3 * lanes]
        ksum = ksum + got[4 * lanes : 5 * lanes]
        return far_me * lam + got[3 * lanes : 4 * lanes], gsum, msum, ksum

    zl4 = jnp.zeros((lanes, LANE), F32)
    _, gsum, msum, ksum = lax.fori_loop(0, n_ctx, owner, (zl4, zl4, zl4, zl4))
    fin[me, pl.ds(0, lanes), :] = gsum
    fin[me, pl.ds(lanes, lanes), :] = msum
    others(lambda peer: q_copy(peer).start())
    scale = 1.0 / math.sqrt(seq)
    gskip_ref[...] = ksum * scale

    take_b_z2()

    take_z1()

    def join_back(j, total):
        sender = pairs - 1 - j
        r_copy(0, sender).wait_recv()
        return far_half * far_half * total + r_recv[sender].astype(F32)

    l_t[:, my_half] = lax.fori_loop(0, pairs - 1 - pair, join_back, none)
    sib_l = sib_copy(3, l_t.at[:, my_half], l_t.at[:, my_half])
    sib_l.start()

    take_b_z2()

    take_b_z2()

    sib_l.wait_recv()
    l_in = jnp.where(core == 1, l_t[...], far * l_t[...] + r_sib[...])
    for n in range(modes):
        in8[n] = jnp.broadcast_to(l_in[n : n + 1], (SUB, chans))

    for k in range(lanes):
        a, c = a8[:, :, lane(k)], c8[:, :, lane(k)]
        skip = skip_ref[:, lane(k)]
        start = ex8[:, :, lane(k)] + dec[3, :, :, lane(k)] * in8[:, :, lane(k)]

        def emit_back(j, h, a=a, c=c, skip=skip, k=k):
            i = steps - 1 - j
            now = at_step(g32, i, k)
            h = a * h + now[None]
            y32[k, pl.ds(i, SUB, stride=steps), :] = jnp.sum(c * h, axis=0) + skip * now
            return h

        lax.fori_loop(0, steps, emit_back, start, unroll=8)
        gi_ref[:, lane(k)] = y32[k].astype(BF16)

    wait_bytes(rs_r.at[at_az2], 2 * rows, split)
    out_ref[:, :split] = (
        total3(part.at[xl, z, :, pl.ds(0, split)], al2, ar2) + bx1[z].astype(F32)
    ).astype(BF16)

    wait_bytes(rs_r.at[at_x3], rows, dim - split)
    out_ref[:, split:] = (
        total3(part.at[xl, z, :, pl.ds(split, dim - split)], bl2.at[xl], br2.at[xl])
        + bx3[...].astype(F32)
    ).astype(BF16)


    wait_all(fin, q_rs)

    for k in range(lanes):
        rate = rate_t[:, lane(k)]
        gr = jnp.sum(fin[:, pl.ds(k, 1), :], axis=1)
        ml = jnp.sum(fin[:, pl.ds(lanes + k, 1), :], axis=1)
        gres_ref[:, lane(k)] = gr * (jnp.sqrt(2.0 * rate) * scale)
        glog_ref[:, lane(k)] = c_t[:, lane(k)] * ((0.5 + rate) * gr - rate * ml) * scale


    sent = w_v.at[pl.ds(0, tok - rows)]
    pltpu.make_async_copy(sent, sent, ag_s).wait()
    pltpu.make_async_copy(sent, sent, rs_s).wait()
    for copy in (sib_first, sib_back, sib_l):
        copy.wait_send()
    rest = s_recv.at[pl.ds(0, 2 * n_y - 1)]
    pltpu.make_async_copy(rest, rest, s_ss).wait()

    @pl.loop(0, pair)
    def _(peer):
        r_copy(peer, pair).wait_send()

    wait_all(rr, p_ss)
    wait_all(fin, q_ss)


def store(*refs):
    n = len(refs) // 2
    copies = [pltpu.make_async_copy(refs[i], refs[n + i], refs[-1].at[i]) for i in range(n)]
    for copy in copies:
        copy.start()
    for copy in copies:
        copy.wait()


def per_device(inputs, residue, log_rate, skip, out_weight, out_grad):
    n_ctx = lax.axis_size("ctx")
    tok, chans = inputs.shape
    modes = residue.shape[1]
    dim = out_weight.shape[1]
    rows = tok // (NX * NZ)
    steps = tok // SUB
    lanes = chans // LANE
    split = dim // SHARES * sum(A_SHARES)
    b_cols = dim - split
    wide = (modes, SUB, chans)
    flat = (modes, chans)
    packed = -(-5 * lanes // SUB) * SUB
    anywhere = pl.BlockSpec(memory_space=pl.ANY)
    dma = pltpu.SemaphoreType.DMA
    results = (
        jax.ShapeDtypeStruct((rows, dim), BF16),
        jax.ShapeDtypeStruct((tok, chans), BF16),
        jax.ShapeDtypeStruct(flat, F32),
        jax.ShapeDtypeStruct(flat, F32),
        jax.ShapeDtypeStruct((lanes, LANE), F32),
    )
    vmem = pl.BlockSpec(memory_space=pltpu.VMEM)
    held = pl.pallas_call(
        functools.partial(kernel, tok * n_ctx, n_ctx),
        out_shape=tuple(pltpu.VMEM(r.shape, r.dtype) for r in results),
        in_specs=[anywhere] * 6,
        out_specs=(vmem,) * 5,
        scratch_shapes=[
            pltpu.VMEM((tok, chans), BF16),
            pltpu.VMEM(flat, F32),
            pltpu.VMEM(flat, F32),
            pltpu.VMEM((1, chans), F32),
            pltpu.VMEM((chans, dim), BF16),
            pltpu.VMEM((NX, NZ, rows, dim), BF16),
            pltpu.VMEM((NX, NZ, rows, dim), BF16),
            pltpu.VMEM((steps, *wide), F32),
            pltpu.VMEM((lanes, tok, LANE), F32),
            pltpu.VMEM((lanes, tok, LANE), F32),
            pltpu.VMEM((lanes, tok, LANE), F32),
            pltpu.VMEM((tok, chans), BF16),
            pltpu.VMEM(flat, F32),
            pltpu.VMEM(flat, F32),
            pltpu.VMEM((modes, lanes, LANE), F32),
            pltpu.VMEM(wide, F32),
            pltpu.VMEM(wide, F32),
            pltpu.VMEM(wide, F32),
            pltpu.VMEM(wide, F32),
            pltpu.VMEM(wide, F32),
            pltpu.VMEM(wide, F32),
            pltpu.VMEM(flat, F32),
            pltpu.VMEM(flat, F32),
            pltpu.VMEM((n_ctx // 2, modes, chans), BF16),
            pltpu.VMEM(flat, F32),
            pltpu.VMEM(flat, F32),
            pltpu.VMEM((modes, chans // 2), BF16),
            pltpu.VMEM((n_ctx // 2, modes, chans // 2), BF16),
            pltpu.VMEM(flat, F32),
            pltpu.VMEM((modes, packed, LANE), F32),
            pltpu.VMEM((n_ctx, packed, LANE), F32),
            pltpu.VMEM((5, *wide), F32),
            pltpu.VMEM((n_ctx, 2 * lanes, LANE), F32),
            pltpu.VMEM((NZ, rows, split), BF16),
            pltpu.VMEM((rows, split // 2), BF16),
            pltpu.VMEM((rows, split // 2), BF16),
            pltpu.VMEM((rows, split), BF16),
            pltpu.VMEM((rows, split), BF16),
            pltpu.VMEM((NX, rows, b_cols // 2), BF16),
            pltpu.VMEM((NX, rows, b_cols // 2), BF16),
            pltpu.VMEM((NX, rows, b_cols), BF16),
            pltpu.VMEM((NX, rows, b_cols), BF16),
            pltpu.VMEM((rows, b_cols), BF16),
            pltpu.SemaphoreType.REGULAR,
            dma((5,)),
            dma,
            dma,
            dma((15,)),
            dma,
            dma((2 * (A_PIECES + B_PIECES) + 2,)),
            dma,
            dma((2,)),
            dma((n_ctx // 2,)),
            dma((n_ctx // 2,)),
            dma((4,)),
            dma((4,)),
            *[dma] * 4,
        ],
        compiler_params=pltpu.CompilerParams(
            collective_id=0, has_side_effects=True, vmem_limit_bytes=56 * 1024 * 1024
        ),
    )(inputs, residue.T, log_rate.T, skip.reshape(1, chans), out_weight, out_grad)
    out, gi, gres, glog, gskip = pl.pallas_call(
        store,
        out_shape=results,
        in_specs=[vmem] * 5,
        out_specs=(anywhere,) * 5,
        scratch_shapes=[dma((5,))],
        compiler_params=pltpu.CompilerParams(vmem_limit_bytes=2 * 1024 * 1024),
    )(*held)
    return out, gi, gres.T, glog.T, gskip.reshape(chans)


def solution(mesh):
    return jax.shard_map(
        per_device,
        mesh=mesh,
        in_specs=(
            P("ctx", "tp"),
            P("tp", None),
            P("tp", None),
            P("tp"),
            P("tp", None),
            P(("ctx", "tp"), None),
        ),
        out_specs=(P(("ctx", "tp"), None), P("ctx", "tp"), P("tp", None), P("tp", None), P("tp")),
        check_vma=False,
    )
```

```python
import functools
import math

import jax
import jax.numpy as jnp
from jax import lax
from jax.experimental import pallas as pl
from jax.experimental.pallas import tpu as pltpu
from jax.sharding import PartitionSpec as P

MESH = pl.DeviceIdType.MESH
F32 = jnp.float32
BF16 = jnp.bfloat16
SUB = 8
LANE = 128
NX, NZ = 2, 4
SHARES, A_SHARES, B_SHARES = 32, (4, 4), (8, 8, 5, 3)
A_PIECES, B_PIECES = len(A_SHARES), len(B_SHARES)


def kernel(
    seq,
    n_ctx,
    x_hbm,
    res_hbm,
    lr_hbm,
    skip_hbm,
    w_hbm,
    og_hbm,
    out_ref,
    gi_ref,
    gres_ref,
    glog_ref,
    gskip_ref,
    x_ref,
    res_ref,
    lr_ref,
    skip_ref,
    w_v,
    og,
    part,
    hall,
    x32,
    y32,
    g32,
    mb,
    rate_t,
    c_t,
    far4,
    rate8,
    a8,
    c8,
    ex8,
    in8,
    v8,
    s_own,
    s_sib,
    s_recv,
    r_own,
    r_sib,
    r_pair,
    r_recv,
    l_t,
    red,
    rr,
    dec,
    fin,
    bx1,
    al1,
    ar1,
    al2,
    ar2,
    bl1,
    br1,
    bl2,
    br2,
    bx3,
    near,
    in_sem,
    w_sem,
    ag_s,
    ag_r,
    rs_s,
    rs_r,
    s_ss,
    s_rs,
    r_ss,
    r_rs,
    sib_s,
    sib_r,
    p_ss,
    p_rs,
    q_ss,
    q_rs,
):
    tok, chans = x_ref.shape
    modes = res_ref.shape[0]
    dim = w_v.shape[1]
    rows = tok // (NX * NZ)
    steps = tok // SUB
    lanes = chans // LANE
    half, quarter = dim // 2, dim // 4
    unit = dim // SHARES
    split = unit * sum(A_SHARES)

    me = lax.axis_index("ctx")
    tp = lax.axis_index("tp")
    xl, z = tp // NZ, lax.rem(tp, NZ)
    ox = 1 - xl
    zr, zl, zo = lax.rem(z + 1, NZ), lax.rem(z + 3, NZ), lax.rem(z + 2, NZ)
    to_x = {"tp": ox * NZ + z}
    to_r = {"tp": xl * NZ + zr}
    to_l = {"tp": xl * NZ + zl}
    pairs = n_ctx // 2
    pair, core = me // 2, lax.rem(me, 2)
    y, xh, n_y = me // 4, lax.rem(pair, 2), n_ctx // 4
    across = me + 2 - 4 * xh
    to_sib, to_xh = {"ctx": me + 1 - 2 * core}, {"ctx": across}
    to_x_other = {"ctx": across, "tp": ox * NZ + z}
    to_up, to_down = {"ctx": lax.rem(me + 4, n_ctx)}, {"ctx": lax.rem(me + n_ctx - 4, n_ctx)}
    my_half = pl.ds(pl.multiple_of(core * (chans // 2), chans // 2), chans // 2)

    w_copy = pltpu.make_async_copy(w_hbm, w_v, w_sem)

    barrier = pltpu.get_barrier_semaphore()
    for peer in (to_x, to_r, to_l, to_x_other, to_sib, to_up, to_down):
        pl.semaphore_signal(barrier, inc=1, device_id=peer, device_id_type=MESH)

    ins = [
        pltpu.make_async_copy(src, dst, in_sem.at[i])
        for i, (src, dst) in enumerate(
            (
                (lr_hbm, lr_ref),
                (res_hbm, res_ref),
                (x_hbm, x_ref),
                (skip_hbm, skip_ref),
                (og_hbm, og.at[xl, z]),
            )
        )
    ]
    for copy in ins:
        copy.start()
    w_copy.start()

    pl.semaphore_wait(barrier, 7)
    for peer in (to_x, to_up, to_down):
        pl.semaphore_signal(near, inc=1, device_id=peer, device_id_type=MESH)

    def ctx_copy(src, dst, send, recv, peer):
        return pltpu.make_async_remote_copy(
            src_ref=src,
            dst_ref=dst,
            send_sem=send,
            recv_sem=recv,
            device_id={"ctx": peer},
            device_id_type=MESH,
        )

    def ctx_s(src, dst, index, peer):
        return ctx_copy(src, dst, s_ss, s_rs.at[index], peer)

    def s_copy(other):
        both = s_recv.at[pl.ds(2 * y, 2)]
        return ctx_s(both, both, 1, 4 * other + 2 * xh + core)

    def r_copy(peer, sender):
        return ctx_copy(r_pair, r_recv.at[sender], r_ss.at[peer], r_rs.at[sender], 2 * peer + core)

    def sib_copy(index, src, dst):
        return pltpu.make_async_remote_copy(
            src_ref=src,
            dst_ref=dst,
            send_sem=sib_s,
            recv_sem=sib_r.at[index],
            device_id=to_sib,
            device_id_type=MESH,
        )

    def p_copy(peer):
        used = pl.ds(0, 5 * lanes)
        return ctx_copy(red.at[peer, used], rr.at[me, used], p_ss, p_rs, peer)

    def q_copy(peer):
        return ctx_copy(fin.at[me], fin.at[me], q_ss, q_rs, peer)

    def wait_all(ref, sem):
        rest = ref.at[pl.ds(0, n_ctx - 1)]
        pltpu.make_async_copy(rest, rest, sem).wait()

    def others(step):
        pl.loop(1, n_ctx)(lambda k: step(lax.rem(me + k, n_ctx)))

    tags = iter(range(2, 100))

    def ag(src, dst, peer, group):
        copy = pltpu.make_async_remote_copy(
            src_ref=src,
            dst_ref=dst,
            send_sem=ag_s,
            recv_sem=ag_r.at[next(tags) if group is None else group],
            device_id=peer,
            device_id_type=MESH,
        )
        copy.start()
        return copy

    def relay(shard_x, shard_z, columns, peer, group=None):
        piece = og.at[shard_x, shard_z, :, columns]
        return ag(piece, piece, peer, group)

    def mine(columns, peer, group=None):
        return ag(og_hbm.at[:, columns], og.at[xl, z, :, columns], peer, group)

    def wait_bytes(sem, depth, width):
        size = w_v.at[pl.ds(0, depth), pl.ds(0, width)]
        pltpu.make_async_copy(size, size, sem).wait()

    all_a, all_b = pl.ds(0, half), pl.ds(half, half)
    a1, a2 = pl.ds(0, quarter), pl.ds(quarter, quarter)
    b1, b2 = pl.ds(half, quarter), pl.ds(half + quarter, quarter)
    late_a, late_b = 0, 1

    x_a1, r_b1, l_b2 = mine(a1, to_x), mine(b1, to_r), mine(b2, to_l)
    x_a2, r_b2, l_b1 = mine(a2, to_x), mine(b2, to_r), mine(b1, to_l)

    for copy in ins[:4]:
        copy.wait()
    rate = jnp.exp(lr_ref[...]) / seq
    rate_t[...] = rate
    c_t[...] = res_ref[...] * jnp.sqrt(2.0 * rate)
    far = jnp.exp(-float(tok) * rate)
    for n in range(modes):
        row = pl.ds(n, 1)
        rate8[n] = jnp.broadcast_to(rate_t[row, :], (SUB, chans))
        c8[n] = jnp.broadcast_to(c_t[row, :], (SUB, chans))
    a8[...] = jnp.exp(-rate8[...])

    def lane(k):
        return pl.ds(k * LANE, LANE)

    for k in range(lanes):
        x32[k] = x_ref[:, lane(k)].astype(F32)
        far4[:, pl.ds(k, 1), :] = far[:, k * LANE : (k + 1) * LANE][:, None, :]

    place = lax.broadcasted_iota(jnp.int32, (modes, SUB, LANE), 1)
    place_f = place.astype(F32)
    span = float(steps)
    zero = jnp.zeros((modes, SUB, LANE), F32)

    def at_step(ref, i, k):
        return ref[k, pl.ds(i, SUB, stride=steps), :]

    for k in range(lanes):
        a = a8[:, :, lane(k)]

        def grow(i, h, a=a, k=k):
            return a * h + at_step(x32, i, k)[None]

        end = lax.fori_loop(0, steps, grow, zero, unroll=16)
        rk = rate8[:, :, lane(k)]
        for s in (1, 2, 4):
            moved = jnp.where(place >= s, pltpu.roll(end, s, 1), 0.0)
            end = end + jnp.exp(-(span * s) * rk) * moved
        ex8[:, :, lane(k)] = jnp.where(place >= 1, pltpu.roll(end, 1, 1), 0.0)
        s_own[:, lane(k)] = jnp.sum(jnp.where(place == SUB - 1, end, 0.0), axis=1)

    sib_first = sib_copy(0, s_own, s_sib)
    sib_first.start()

    r_a, l_a = mine(all_a, to_r), mine(all_a, to_l)

    far_half = jnp.exp(-float(tok) * rate_t[:, my_half])
    sib_first.wait_recv()
    s_early = jnp.where(core == 0, s_own[...], s_sib[...])
    s_late = jnp.where(core == 0, s_sib[...], s_own[...])
    far = jnp.exp(-float(tok) * rate_t[...])
    s_recv[pair] = (s_late + far * s_early).astype(BF16)
    pl.semaphore_wait(near, 3)
    s_across = ctx_s(s_recv.at[pair], s_recv.at[pair], 0, across)
    s_across.start()

    mine(all_b, to_x, late_b)

    for k in range(lanes):
        a = a8[:, :, lane(k)]
        rk = rate8[:, :, lane(k)]
        for at, s in enumerate((1, 2, 4)):
            dec[at, :, :, lane(k)] = jnp.exp(-(span * s) * rk)
        dec[3, :, :, lane(k)] = jnp.exp(-span * (SUB - 1.0 - place_f) * rk)
        dec[4, :, :, lane(k)] = jnp.exp(-span * place_f * rk)

        def lift(i, carry, a=a, k=k):
            h, v = carry
            h = a * h + at_step(x32, i, k)[None]
            return h, a * v + h

        _, v = lax.fori_loop(0, steps, lift, (zero, zero), unroll=16)
        v8[:, :, lane(k)] = a * v

    x_a1.wait_recv()
    r_xa1 = relay(ox, z, a1, to_r)
    r_b1.wait_recv()
    r_ob = relay(xl, zl, b1, to_r)
    relay(xl, zl, b1, to_x, late_b)
    l_b2.wait_recv()
    l_ob = relay(xl, zr, b2, to_l)
    relay(xl, zr, b2, to_x, late_b)
    s_across.wait_recv()

    @pl.loop(1, n_y)
    def _(step):
        s_copy(lax.rem(y + step, n_y)).start()

    x_a2.wait_recv()
    l_xa2 = relay(ox, z, a2, to_l)
    r_b2.wait_recv()
    relay(xl, zl, b2, to_x, late_b)
    l_b1.wait_recv()
    relay(xl, zr, b1, to_x, late_b)
    relay(ox, z, a2, to_r, late_a)
    relay(ox, z, a1, to_l, late_a)

    def join(sender, total):
        return far * far * total + s_recv[sender].astype(F32)

    got_y = s_recv.at[pl.ds(0, pairs - 2)]
    pltpu.make_async_copy(got_y, got_y, s_rs.at[1]).wait()
    none = jnp.zeros((modes, chans // 2), F32)
    h_in = lax.fori_loop(0, pair, join, jnp.zeros((modes, chans), F32))
    h_in = jnp.where(core == 0, h_in, far * h_in + s_sib[...])
    for n in range(modes):
        in8[n] = jnp.broadcast_to(h_in[n : n + 1], (SUB, chans))

    r_a.wait_recv()
    l_a.wait_recv()
    relay(xl, zl, a1, to_r, late_a)
    relay(xl, zr, a2, to_l, late_a)

    for k in range(lanes // 2):
        a, c = a8[:, :, lane(k)], c8[:, :, lane(k)]
        skip = skip_ref[:, lane(k)]
        start = ex8[:, :, lane(k)] + dec[4, :, :, lane(k)] * in8[:, :, lane(k)]
        v = v8[:, :, lane(k)] + span * a * dec[0, :, :, lane(k)] * start
        v8[:, :, lane(k)] = v
        u = jnp.sum(dec[3, :, :, lane(k)] * v, axis=1, keepdims=True)
        red[:, pl.ds(2 * lanes + k, 1), :] = u

        def emit(i, h, a=a, c=c, skip=skip, k=k):
            now = at_step(x32, i, k)
            h = a * h + now[None]
            hall[i, :, :, lane(k)] = h
            y32[k, pl.ds(i, SUB, stride=steps), :] = jnp.sum(c * h, axis=0) + skip * now
            return h

        lax.fori_loop(0, steps, emit, start, unroll=16)
        mb[:, lane(k)] = y32[k].astype(BF16)

    r_xa1.wait_recv()
    l_xa2.wait_recv()
    relay(ox, zl, a1, to_r, late_a)
    relay(ox, zr, a2, to_l, late_a)

    r_ob.wait_recv()
    relay(xl, zo, b1, to_x, late_b)
    l_ob.wait_recv()
    x_ob2 = relay(xl, zo, b2, to_x)

    for k in range(lanes // 2, lanes):
        a, c = a8[:, :, lane(k)], c8[:, :, lane(k)]
        skip = skip_ref[:, lane(k)]
        start = ex8[:, :, lane(k)] + dec[4, :, :, lane(k)] * in8[:, :, lane(k)]
        v = v8[:, :, lane(k)] + span * a * dec[0, :, :, lane(k)] * start
        v8[:, :, lane(k)] = v
        u = jnp.sum(dec[3, :, :, lane(k)] * v, axis=1, keepdims=True)
        red[:, pl.ds(2 * lanes + k, 1), :] = u

        def emit(i, h, a=a, c=c, skip=skip, k=k):
            now = at_step(x32, i, k)
            h = a * h + now[None]
            hall[i, :, :, lane(k)] = h
            y32[k, pl.ds(i, SUB, stride=steps), :] = jnp.sum(c * h, axis=0) + skip * now
            return h

        lax.fori_loop(0, steps, emit, start, unroll=16)
        mb[:, lane(k)] = y32[k].astype(BF16)

    def rs(src, dst, peer, index):
        copy = pltpu.make_async_remote_copy(
            src_ref=src,
            dst_ref=dst,
            send_sem=rs_s,
            recv_sem=rs_r.at[index],
            device_id=peer,
            device_id_type=MESH,
        )
        copy.start()

    at_x1, at_az1, at_az2 = 0, A_PIECES, 2 * A_PIECES
    at_bz1 = at_az2 + 1
    at_bz2 = at_bz1 + B_PIECES
    at_x3 = at_bz2 + B_PIECES
    done = {"x1": 0, "az1": 0, "bz1": 0, "bz2": 0}

    def following(name):
        done[name] += 1
        return done[name] - 1

    def a_place(i):
        return unit * sum(A_SHARES[:i]), unit * A_SHARES[i]

    def a_span(i):
        return pl.ds(*a_place(i))

    def a_halves(i):
        at, width = a_place(i)
        return pl.ds(at, width // 2), pl.ds(at + width // 2, width // 2)

    def a_half(i):
        at, width = a_place(i)
        return pl.ds(at // 2, width // 2)

    def b_place(i):
        return unit * sum(B_SHARES[:i]), unit * B_SHARES[i]

    def b_span(i, base=split):
        at, width = b_place(i)
        return pl.ds(base + at, width)

    def b_halves(i):
        at, width = b_place(i)
        return pl.ds(split + at, width // 2), pl.ds(split + at + width // 2, width // 2)

    def b_half(i):
        at, width = b_place(i)
        return pl.ds(at // 2, width // 2)

    w_copy.wait()

    def project(lo, hi):
        p = jnp.dot(mb[...], w_v[:, lo:hi], preferred_element_type=F32)
        part[:, :, :, lo:hi] = p.astype(BF16).reshape(NX, NZ, rows, hi - lo)

    def send_z1(i):
        h1, h2 = b_halves(i)
        rs(part.at[:, zo, :, h1], bl1.at[:, :, b_half(i)], to_r, at_bz1 + i)
        rs(part.at[:, zo, :, h2], br1.at[:, :, b_half(i)], to_l, at_bz1 + i)

    middle = split + b_place(2)[0]
    project(split, middle)
    send_z1(0)
    send_z1(1)
    project(middle, dim)
    for i in range(2, B_PIECES):
        send_z1(i)
    project(0, split)
    for i in range(A_PIECES):
        rs(part.at[ox, :, :, a_span(i)], bx1.at[:, :, a_span(i)], to_x, at_x1 + i)

    wait_bytes(ag_r.at[late_a], 6 * rows, quarter)
    ins[4].wait()

    def project_back(lo, hi, fresh=False):
        left = og[:, :, :, lo:hi].reshape(tok, hi - lo)
        for k in range(lanes):
            got = lax.dot_general(
                left,
                w_v[k * LANE : (k + 1) * LANE, lo:hi],
                (((1,), (1,)), ((), ())),
                preferred_element_type=F32,
            )
            g32[k] = got if fresh else g32[k] + got

    project_back(0, half, True)

    def merge(ref, got):
        ref[...] = (ref[...].astype(F32) + got[...].astype(F32)).astype(BF16)

    def take_b_z1():
        i = following("bz1")
        h1, h2 = b_halves(i)
        wait_bytes(rs_r.at[at_bz1 + i], 2 * NX * rows, b_place(i)[1] // 2)
        merge(part.at[:, zr, :, h1], bl1.at[:, :, b_half(i)])
        rs(part.at[:, zr, :, b_span(i)], bl2.at[:, :, b_span(i, 0)], to_r, at_bz2 + i)
        merge(part.at[:, zl, :, h2], br1.at[:, :, b_half(i)])
        rs(part.at[:, zl, :, b_span(i)], br2.at[:, :, b_span(i, 0)], to_l, at_bz2 + i)

    def take_x1():
        i = following("x1")
        here = bx1.at[:, :, a_span(i)]
        pltpu.make_async_copy(here, here, rs_r.at[at_x1 + i]).wait()
        h1, h2 = a_halves(i)
        merge(part.at[xl, zo, :, a_span(i)], here.at[zo])
        rs(part.at[xl, zo, :, h1], al1.at[:, a_half(i)], to_r, at_az1 + i)
        rs(part.at[xl, zo, :, h2], ar1.at[:, a_half(i)], to_l, at_az1 + i)
        merge(part.at[xl, zr, :, a_span(i)], here.at[zr])
        merge(part.at[xl, zl, :, a_span(i)], here.at[zl])

    def take_z1():
        i = following("az1")
        h1, h2 = a_halves(i)
        wait_bytes(rs_r.at[at_az1 + i], 2 * rows, a_place(i)[1] // 2)
        merge(part.at[xl, zr, :, h1], al1.at[:, a_half(i)])
        rs(part.at[xl, zr, :, a_span(i)], al2.at[:, a_span(i)], to_r, at_az2)
        merge(part.at[xl, zl, :, h2], ar1.at[:, a_half(i)])
        rs(part.at[xl, zl, :, a_span(i)], ar2.at[:, a_span(i)], to_l, at_az2)

    def total3(ref, left, right):
        return ref[...].astype(F32) + left[...].astype(F32) + right[...].astype(F32)

    def take_b_z2():
        i = following("bz2")
        wait_bytes(rs_r.at[at_bz2 + i], 2 * NX * rows, b_place(i)[1])
        far_part = part.at[ox, z, :, b_span(i)]
        here = b_span(i, 0)
        far_part[...] = total3(far_part, bl2.at[ox, :, here], br2.at[ox, :, here]).astype(BF16)
        rs(far_part, bx3.at[:, here], to_x, at_x3)

    take_b_z1()

    wait_bytes(ag_r.at[late_b], 7 * rows, quarter)

    project_back(half, half + quarter)
    x_ob2.wait_recv()
    project_back(half + quarter, dim)

    for k in range(lanes):
        g32[k] = g32[k].astype(BF16).astype(F32)
        sk = jnp.sum(g32[k] * x32[k], axis=0, keepdims=True)
        red[:, pl.ds(4 * lanes + k, 1), :] = jnp.broadcast_to(sk[None], (modes, 1, LANE))

    hm = modes // 2
    zh = jnp.zeros((hm, SUB, LANE), F32)
    pm = place[:hm]
    for m0 in (0, hm):
        ms = pl.ds(m0, hm)
        for k in range(lanes):
            lv = lane(k)
            a = a8[ms, :, lv]

            def back(j, carry, a=a, k=k, lv=lv, ms=ms):
                h, gs, mloc = carry
                i = steps - 1 - j
                now = at_step(g32, i, k)[None]
                held = hall[i, ms, :, lv]
                h = a * h + now
                return h, gs + now * held, mloc + h * held

            end, gs, mloc = lax.fori_loop(0, steps, back, (zh, zh, zh), unroll=16)
            for at, s in enumerate((1, 2, 4)):
                moved = jnp.where(pm < SUB - s, pltpu.roll(end, SUB - s, 1), 0.0)
                end = end + dec[at, ms, :, lv] * moved
            ex = jnp.where(pm < SUB - 1, pltpu.roll(end, SUB - 1, 1), 0.0)
            ex8[ms, :, lv] = ex
            first = jnp.where(pm == 0, end, 0.0)
            r_own[ms, lv] = jnp.sum(first, axis=1)
            for at, value in ((0, gs), (1, mloc + ex * v8[ms, :, lv]), (3, first)):
                red[ms, pl.ds(at * lanes + k, 1), :] = jnp.sum(value, axis=1, keepdims=True)

        @pl.loop(m0, m0 + hm)
        def _(peer):
            @pl.when(peer != me)
            def _():
                p_copy(peer).start()

        if m0 == 0:
            take_x1()
            take_b_z1()

    sib_back = sib_copy(2, r_own, r_sib)
    sib_back.start()
    rr[me] = red[me]

    sib_back.wait_recv()
    mine_r, sib_r_half = r_own[:, my_half], r_sib[:, my_half]
    r_early = jnp.where(core == 0, mine_r, sib_r_half)
    r_late = jnp.where(core == 0, sib_r_half, mine_r)
    r_pair[...] = (r_early + far_half * r_late).astype(BF16)

    @pl.loop(0, pair)
    def _(peer):
        r_copy(peer, pair).start()


    take_x1()
    take_b_z1()
    take_b_z1()

    take_b_z2()

    take_z1()

    wait_all(rr.at[:, pl.ds(0, 5 * lanes)], p_rs)

    far_me = far4[me]

    def owner(j, carry):
        lam, gsum, msum, ksum = carry
        sender = n_ctx - 1 - j
        got = rr[sender]
        gsum = gsum + got[:lanes]
        msum = msum + got[lanes : 2 * lanes] + lam * got[2 * lanes : 3 * lanes]
        ksum = ksum + got[4 * lanes : 5 * lanes]
        return far_me * lam + got[3 * lanes : 4 * lanes], gsum, msum, ksum

    zl4 = jnp.zeros((lanes, LANE), F32)
    _, gsum, msum, ksum = lax.fori_loop(0, n_ctx, owner, (zl4, zl4, zl4, zl4))
    fin[me, pl.ds(0, lanes), :] = gsum
    fin[me, pl.ds(lanes, lanes), :] = msum
    others(lambda peer: q_copy(peer).start())
    scale = 1.0 / math.sqrt(seq)
    gskip_ref[...] = ksum * scale

    take_b_z2()

    take_z1()

    def join_back(j, total):
        sender = pairs - 1 - j
        r_copy(0, sender).wait_recv()
        return far_half * far_half * total + r_recv[sender].astype(F32)

    l_t[:, my_half] = lax.fori_loop(0, pairs - 1 - pair, join_back, none)
    sib_l = sib_copy(3, l_t.at[:, my_half], l_t.at[:, my_half])
    sib_l.start()

    take_b_z2()

    take_b_z2()

    sib_l.wait_recv()
    l_in = jnp.where(core == 1, l_t[...], far * l_t[...] + r_sib[...])
    for n in range(modes):
        in8[n] = jnp.broadcast_to(l_in[n : n + 1], (SUB, chans))

    for k in range(lanes):
        a, c = a8[:, :, lane(k)], c8[:, :, lane(k)]
        skip = skip_ref[:, lane(k)]
        start = ex8[:, :, lane(k)] + dec[3, :, :, lane(k)] * in8[:, :, lane(k)]

        def emit_back(j, h, a=a, c=c, skip=skip, k=k):
            i = steps - 1 - j
            now = at_step(g32, i, k)
            h = a * h + now[None]
            y32[k, pl.ds(i, SUB, stride=steps), :] = jnp.sum(c * h, axis=0) + skip * now
            return h

        lax.fori_loop(0, steps, emit_back, start, unroll=16)
        gi_ref[:, lane(k)] = y32[k].astype(BF16)

    wait_bytes(rs_r.at[at_az2], 2 * rows, split)
    out_ref[:, :split] = (
        total3(part.at[xl, z, :, pl.ds(0, split)], al2, ar2) + bx1[z].astype(F32)
    ).astype(BF16)

    wait_bytes(rs_r.at[at_x3], rows, dim - split)
    out_ref[:, split:] = (
        total3(part.at[xl, z, :, pl.ds(split, dim - split)], bl2.at[xl], br2.at[xl])
        + bx3[...].astype(F32)
    ).astype(BF16)


    wait_all(fin, q_rs)

    for k in range(lanes):
        rate = rate_t[:, lane(k)]
        gr = jnp.sum(fin[:, pl.ds(k, 1), :], axis=1)
        ml = jnp.sum(fin[:, pl.ds(lanes + k, 1), :], axis=1)
        gres_ref[:, lane(k)] = gr * (jnp.sqrt(2.0 * rate) * scale)
        glog_ref[:, lane(k)] = c_t[:, lane(k)] * ((0.5 + rate) * gr - rate * ml) * scale


    sent = w_v.at[pl.ds(0, tok - rows)]
    pltpu.make_async_copy(sent, sent, ag_s).wait()
    pltpu.make_async_copy(sent, sent, rs_s).wait()
    wait_bytes(sib_s, rows, 5 * chans)
    rest = s_recv.at[pl.ds(0, 2 * n_y - 1)]
    pltpu.make_async_copy(rest, rest, s_ss).wait()

    @pl.loop(0, pair)
    def _(peer):
        r_copy(peer, pair).wait_send()

    wait_all(rr.at[:, pl.ds(0, 5 * lanes)], p_ss)
    wait_all(fin, q_ss)


def store(*refs):
    n = len(refs) // 2
    copies = [pltpu.make_async_copy(refs[i], refs[n + i], refs[-1].at[i]) for i in range(n)]
    for copy in copies:
        copy.start()
    for copy in copies:
        copy.wait()


def per_device(inputs, residue, log_rate, skip, out_weight, out_grad):
    n_ctx = lax.axis_size("ctx")
    tok, chans = inputs.shape
    modes = residue.shape[1]
    dim = out_weight.shape[1]
    rows = tok // (NX * NZ)
    steps = tok // SUB
    lanes = chans // LANE
    split = dim // SHARES * sum(A_SHARES)
    b_cols = dim - split
    wide = (modes, SUB, chans)
    flat = (modes, chans)
    packed = -(-5 * lanes // SUB) * SUB
    anywhere = pl.BlockSpec(memory_space=pl.ANY)
    dma = pltpu.SemaphoreType.DMA
    results = (
        jax.ShapeDtypeStruct((rows, dim), BF16),
        jax.ShapeDtypeStruct((tok, chans), BF16),
        jax.ShapeDtypeStruct(flat, F32),
        jax.ShapeDtypeStruct(flat, F32),
        jax.ShapeDtypeStruct((lanes, LANE), F32),
    )
    vmem = pl.BlockSpec(memory_space=pltpu.VMEM)
    held = pl.pallas_call(
        functools.partial(kernel, tok * n_ctx, n_ctx),
        out_shape=tuple(pltpu.VMEM(r.shape, r.dtype) for r in results),
        in_specs=[anywhere] * 6,
        out_specs=(vmem,) * 5,
        scratch_shapes=[
            pltpu.VMEM((tok, chans), BF16),
            pltpu.VMEM(flat, F32),
            pltpu.VMEM(flat, F32),
            pltpu.VMEM((1, chans), F32),
            pltpu.VMEM((chans, dim), BF16),
            pltpu.VMEM((NX, NZ, rows, dim), BF16),
            pltpu.VMEM((NX, NZ, rows, dim), BF16),
            pltpu.VMEM((steps, *wide), F32),
            pltpu.VMEM((lanes, tok, LANE), F32),
            pltpu.VMEM((lanes, tok, LANE), F32),
            pltpu.VMEM((lanes, tok, LANE), F32),
            pltpu.VMEM((tok, chans), BF16),
            pltpu.VMEM(flat, F32),
            pltpu.VMEM(flat, F32),
            pltpu.VMEM((modes, lanes, LANE), F32),
            pltpu.VMEM(wide, F32),
            pltpu.VMEM(wide, F32),
            pltpu.VMEM(wide, F32),
            pltpu.VMEM(wide, F32),
            pltpu.VMEM(wide, F32),
            pltpu.VMEM(wide, F32),
            pltpu.VMEM(flat, F32),
            pltpu.VMEM(flat, F32),
            pltpu.VMEM((n_ctx // 2, modes, chans), BF16),
            pltpu.VMEM(flat, F32),
            pltpu.VMEM(flat, F32),
            pltpu.VMEM((modes, chans // 2), BF16),
            pltpu.VMEM((n_ctx // 2, modes, chans // 2), BF16),
            pltpu.VMEM(flat, F32),
            pltpu.VMEM((modes, packed, LANE), F32),
            pltpu.VMEM((n_ctx, packed, LANE), F32),
            pltpu.VMEM((5, *wide), F32),
            pltpu.VMEM((n_ctx, 2 * lanes, LANE), F32),
            pltpu.VMEM((NZ, rows, split), BF16),
            pltpu.VMEM((rows, split // 2), BF16),
            pltpu.VMEM((rows, split // 2), BF16),
            pltpu.VMEM((rows, split), BF16),
            pltpu.VMEM((rows, split), BF16),
            pltpu.VMEM((NX, rows, b_cols // 2), BF16),
            pltpu.VMEM((NX, rows, b_cols // 2), BF16),
            pltpu.VMEM((NX, rows, b_cols), BF16),
            pltpu.VMEM((NX, rows, b_cols), BF16),
            pltpu.VMEM((rows, b_cols), BF16),
            pltpu.SemaphoreType.REGULAR,
            dma((5,)),
            dma,
            dma,
            dma((15,)),
            dma,
            dma((2 * (A_PIECES + B_PIECES) + 2,)),
            dma,
            dma((2,)),
            dma((n_ctx // 2,)),
            dma((n_ctx // 2,)),
            dma,
            dma((4,)),
            *[dma] * 4,
        ],
        compiler_params=pltpu.CompilerParams(
            collective_id=0, has_side_effects=True, vmem_limit_bytes=56 * 1024 * 1024
        ),
    )(inputs, residue.T, log_rate.T, skip.reshape(1, chans), out_weight, out_grad)
    out, gi, gres, glog, gskip = pl.pallas_call(
        store,
        out_shape=results,
        in_specs=[vmem] * 5,
        out_specs=(anywhere,) * 5,
        scratch_shapes=[dma((5,))],
        compiler_params=pltpu.CompilerParams(vmem_limit_bytes=2 * 1024 * 1024),
    )(*held)
    return out, gi, gres.T, glog.T, gskip.reshape(chans)


def solution(mesh):
    return jax.shard_map(
        per_device,
        mesh=mesh,
        in_specs=(
            P("ctx", "tp"),
            P("tp", None),
            P("tp", None),
            P("tp"),
            P("tp", None),
            P(("ctx", "tp"), None),
        ),
        out_specs=(P(("ctx", "tp"), None), P("ctx", "tp"), P("tp", None), P("tp", None), P("tp")),
        check_vma=False,
    )
```

```python
import functools
import math

import jax
import jax.numpy as jnp
from jax import lax
from jax.experimental import pallas as pl
from jax.experimental.pallas import tpu as pltpu
from jax.sharding import PartitionSpec as P

MESH = pl.DeviceIdType.MESH
F32 = jnp.float32
BF16 = jnp.bfloat16
SUB = 8
LANE = 128
NX, NZ = 2, 4
SHARES, A_SHARES, B_SHARES = 32, (4, 4), (9, 8, 5, 2)
A_PIECES, B_PIECES = len(A_SHARES), len(B_SHARES)


def kernel(
    seq,
    n_ctx,
    x_hbm,
    res_hbm,
    lr_hbm,
    skip_hbm,
    w_hbm,
    og_hbm,
    out_ref,
    gi_ref,
    gres_ref,
    glog_ref,
    gskip_ref,
    x_ref,
    res_ref,
    lr_ref,
    skip_ref,
    w_v,
    og,
    part,
    hall,
    x32,
    y32,
    g32,
    mb,
    rate_t,
    c_t,
    far4,
    rate8,
    a8,
    c8,
    ex8,
    in8,
    v8,
    s_own,
    s_sib,
    s_recv,
    r_own,
    r_sib,
    r_pair,
    r_recv,
    l_t,
    red,
    rr,
    dec,
    fin,
    bx1,
    al1,
    ar1,
    al2,
    ar2,
    bl1,
    br1,
    bl2,
    br2,
    bx3,
    near,
    in_sem,
    w_sem,
    ag_s,
    ag_r,
    rs_s,
    rs_r,
    s_ss,
    s_rs,
    r_ss,
    r_rs,
    sib_s,
    sib_r,
    p_ss,
    p_rs,
    q_ss,
    q_rs,
):
    tok, chans = x_ref.shape
    modes = res_ref.shape[0]
    dim = w_v.shape[1]
    rows = tok // (NX * NZ)
    steps = tok // SUB
    lanes = chans // LANE
    half, quarter = dim // 2, dim // 4
    unit = dim // SHARES
    split = unit * sum(A_SHARES)

    me = lax.axis_index("ctx")
    tp = lax.axis_index("tp")
    xl, z = tp // NZ, lax.rem(tp, NZ)
    ox = 1 - xl
    zr, zl, zo = lax.rem(z + 1, NZ), lax.rem(z + 3, NZ), lax.rem(z + 2, NZ)
    to_x = {"tp": ox * NZ + z}
    to_r = {"tp": xl * NZ + zr}
    to_l = {"tp": xl * NZ + zl}
    pairs = n_ctx // 2
    pair, core = me // 2, lax.rem(me, 2)
    y, xh, n_y = me // 4, lax.rem(pair, 2), n_ctx // 4
    across = me + 2 - 4 * xh
    to_sib, to_xh = {"ctx": me + 1 - 2 * core}, {"ctx": across}
    to_x_other = {"ctx": across, "tp": ox * NZ + z}
    to_up, to_down = {"ctx": lax.rem(me + 4, n_ctx)}, {"ctx": lax.rem(me + n_ctx - 4, n_ctx)}
    my_half = pl.ds(pl.multiple_of(core * (chans // 2), chans // 2), chans // 2)

    w_copy = pltpu.make_async_copy(w_hbm, w_v, w_sem)

    barrier = pltpu.get_barrier_semaphore()
    for peer in (to_x, to_r, to_l, to_x_other, to_sib, to_up, to_down):
        pl.semaphore_signal(barrier, inc=1, device_id=peer, device_id_type=MESH)

    ins = [
        pltpu.make_async_copy(src, dst, in_sem.at[i])
        for i, (src, dst) in enumerate(
            (
                (lr_hbm, lr_ref),
                (res_hbm, res_ref),
                (x_hbm, x_ref),
                (skip_hbm, skip_ref),
                (og_hbm, og.at[xl, z]),
            )
        )
    ]
    for copy in ins:
        copy.start()
    w_copy.start()

    pl.semaphore_wait(barrier, 7)
    for peer in (to_x, to_up, to_down):
        pl.semaphore_signal(near, inc=1, device_id=peer, device_id_type=MESH)

    def ctx_copy(src, dst, send, recv, peer):
        return pltpu.make_async_remote_copy(
            src_ref=src,
            dst_ref=dst,
            send_sem=send,
            recv_sem=recv,
            device_id={"ctx": peer},
            device_id_type=MESH,
        )

    def ctx_s(src, dst, index, peer):
        return ctx_copy(src, dst, s_ss, s_rs.at[index], peer)

    def s_copy(other):
        both = s_recv.at[pl.ds(2 * y, 2)]
        return ctx_s(both, both, 1, 4 * other + 2 * xh + core)

    def r_copy(peer, sender):
        return ctx_copy(r_pair, r_recv.at[sender], r_ss.at[peer], r_rs.at[sender], 2 * peer + core)

    def sib_copy(index, src, dst):
        return pltpu.make_async_remote_copy(
            src_ref=src,
            dst_ref=dst,
            send_sem=sib_s,
            recv_sem=sib_r.at[index],
            device_id=to_sib,
            device_id_type=MESH,
        )

    def p_copy(peer):
        used = pl.ds(0, 5 * lanes)
        return ctx_copy(red.at[peer, used], rr.at[me, used], p_ss, p_rs, peer)

    def q_copy(peer):
        return ctx_copy(fin.at[me], fin.at[me], q_ss, q_rs, peer)

    def wait_all(ref, sem):
        rest = ref.at[pl.ds(0, n_ctx - 1)]
        pltpu.make_async_copy(rest, rest, sem).wait()

    def others(step):
        pl.loop(1, n_ctx)(lambda k: step(lax.rem(me + k, n_ctx)))

    tags = iter(range(2, 100))

    def ag(src, dst, peer, group):
        copy = pltpu.make_async_remote_copy(
            src_ref=src,
            dst_ref=dst,
            send_sem=ag_s,
            recv_sem=ag_r.at[next(tags) if group is None else group],
            device_id=peer,
            device_id_type=MESH,
        )
        copy.start()
        return copy

    def relay(shard_x, shard_z, columns, peer, group=None):
        piece = og.at[shard_x, shard_z, :, columns]
        return ag(piece, piece, peer, group)

    def mine(columns, peer, group=None):
        return ag(og_hbm.at[:, columns], og.at[xl, z, :, columns], peer, group)

    def wait_bytes(sem, depth, width):
        size = w_v.at[pl.ds(0, depth), pl.ds(0, width)]
        pltpu.make_async_copy(size, size, sem).wait()

    all_a, all_b = pl.ds(0, half), pl.ds(half, half)
    a1, a2 = pl.ds(0, quarter), pl.ds(quarter, quarter)
    b1, b2 = pl.ds(half, quarter), pl.ds(half + quarter, quarter)
    late_a, late_b = 0, 1

    x_a1, r_b1, l_b2 = mine(a1, to_x), mine(b1, to_r), mine(b2, to_l)
    x_a2, r_b2, l_b1 = mine(a2, to_x), mine(b2, to_r), mine(b1, to_l)

    for copy in ins[:4]:
        copy.wait()
    rate = jnp.exp(lr_ref[...]) / seq
    rate_t[...] = rate
    c_t[...] = res_ref[...] * jnp.sqrt(2.0 * rate)
    far = jnp.exp(-float(tok) * rate)
    for n in range(modes):
        row = pl.ds(n, 1)
        rate8[n] = jnp.broadcast_to(rate_t[row, :], (SUB, chans))
        c8[n] = jnp.broadcast_to(c_t[row, :], (SUB, chans))
    a8[...] = jnp.exp(-rate8[...])

    def lane(k):
        return pl.ds(k * LANE, LANE)

    for k in range(lanes):
        x32[k] = x_ref[:, lane(k)].astype(F32)
        far4[:, pl.ds(k, 1), :] = far[:, k * LANE : (k + 1) * LANE][:, None, :]

    place = lax.broadcasted_iota(jnp.int32, (modes, SUB, LANE), 1)
    place_f = place.astype(F32)
    span = float(steps)
    zero = jnp.zeros((modes, SUB, LANE), F32)

    def at_step(ref, i, k):
        return ref[k, pl.ds(i, SUB, stride=steps), :]

    for k in range(lanes):
        a = a8[:, :, lane(k)]

        def grow(i, h, a=a, k=k):
            return a * h + at_step(x32, i, k)[None]

        end = lax.fori_loop(0, steps, grow, zero, unroll=16)
        rk = rate8[:, :, lane(k)]
        for s in (1, 2, 4):
            moved = jnp.where(place >= s, pltpu.roll(end, s, 1), 0.0)
            end = end + jnp.exp(-(span * s) * rk) * moved
        ex8[:, :, lane(k)] = jnp.where(place >= 1, pltpu.roll(end, 1, 1), 0.0)
        s_own[:, lane(k)] = jnp.sum(jnp.where(place == SUB - 1, end, 0.0), axis=1)

    sib_first = sib_copy(0, s_own, s_sib)
    sib_first.start()

    r_a, l_a = mine(all_a, to_r), mine(all_a, to_l)

    far_half = jnp.exp(-float(tok) * rate_t[:, my_half])
    sib_first.wait_recv()
    s_early = jnp.where(core == 0, s_own[...], s_sib[...])
    s_late = jnp.where(core == 0, s_sib[...], s_own[...])
    far = jnp.exp(-float(tok) * rate_t[...])
    s_recv[pair] = (s_late + far * s_early).astype(BF16)
    pl.semaphore_wait(near, 3)
    s_across = ctx_s(s_recv.at[pair], s_recv.at[pair], 0, across)
    s_across.start()

    mine(all_b, to_x, late_b)

    for k in range(lanes):
        a = a8[:, :, lane(k)]
        rk = rate8[:, :, lane(k)]
        for at, s in enumerate((1, 2, 4)):
            dec[at, :, :, lane(k)] = jnp.exp(-(span * s) * rk)
        dec[3, :, :, lane(k)] = jnp.exp(-span * (SUB - 1.0 - place_f) * rk)
        dec[4, :, :, lane(k)] = jnp.exp(-span * place_f * rk)

        def lift(i, carry, a=a, k=k):
            h, v = carry
            h = a * h + at_step(x32, i, k)[None]
            return h, a * v + h

        _, v = lax.fori_loop(0, steps, lift, (zero, zero), unroll=16)
        v8[:, :, lane(k)] = a * v

    x_a1.wait_recv()
    r_xa1 = relay(ox, z, a1, to_r)
    r_b1.wait_recv()
    r_ob = relay(xl, zl, b1, to_r)
    relay(xl, zl, b1, to_x, late_b)
    l_b2.wait_recv()
    l_ob = relay(xl, zr, b2, to_l)
    relay(xl, zr, b2, to_x, late_b)
    s_across.wait_recv()

    @pl.loop(1, n_y)
    def _(step):
        s_copy(lax.rem(y + step, n_y)).start()

    x_a2.wait_recv()
    l_xa2 = relay(ox, z, a2, to_l)
    r_b2.wait_recv()
    relay(xl, zl, b2, to_x, late_b)
    l_b1.wait_recv()
    relay(xl, zr, b1, to_x, late_b)
    relay(ox, z, a2, to_r, late_a)
    relay(ox, z, a1, to_l, late_a)

    def join(sender, total):
        return far * far * total + s_recv[sender].astype(F32)

    got_y = s_recv.at[pl.ds(0, pairs - 2)]
    pltpu.make_async_copy(got_y, got_y, s_rs.at[1]).wait()
    none = jnp.zeros((modes, chans // 2), F32)
    h_in = lax.fori_loop(0, pair, join, jnp.zeros((modes, chans), F32))
    h_in = jnp.where(core == 0, h_in, far * h_in + s_sib[...])
    for n in range(modes):
        in8[n] = jnp.broadcast_to(h_in[n : n + 1], (SUB, chans))

    r_a.wait_recv()
    l_a.wait_recv()
    relay(xl, zl, a1, to_r, late_a)
    relay(xl, zr, a2, to_l, late_a)

    for k in range(lanes // 2):
        a, c = a8[:, :, lane(k)], c8[:, :, lane(k)]
        skip = skip_ref[:, lane(k)]
        start = ex8[:, :, lane(k)] + dec[4, :, :, lane(k)] * in8[:, :, lane(k)]
        v = v8[:, :, lane(k)] + span * a * dec[0, :, :, lane(k)] * start
        v8[:, :, lane(k)] = v
        u = jnp.sum(dec[3, :, :, lane(k)] * v, axis=1, keepdims=True)
        red[:, pl.ds(2 * lanes + k, 1), :] = u

        def emit(i, h, a=a, c=c, skip=skip, k=k):
            now = at_step(x32, i, k)
            h = a * h + now[None]
            hall[i, :, :, lane(k)] = h
            y32[k, pl.ds(i, SUB, stride=steps), :] = jnp.sum(c * h, axis=0) + skip * now
            return h

        lax.fori_loop(0, steps, emit, start, unroll=16)
        mb[:, lane(k)] = y32[k].astype(BF16)

    r_xa1.wait_recv()
    l_xa2.wait_recv()
    relay(ox, zl, a1, to_r, late_a)
    relay(ox, zr, a2, to_l, late_a)

    r_ob.wait_recv()
    relay(xl, zo, b1, to_x, late_b)
    l_ob.wait_recv()
    x_ob2 = relay(xl, zo, b2, to_x)

    for k in range(lanes // 2, lanes):
        a, c = a8[:, :, lane(k)], c8[:, :, lane(k)]
        skip = skip_ref[:, lane(k)]
        start = ex8[:, :, lane(k)] + dec[4, :, :, lane(k)] * in8[:, :, lane(k)]
        v = v8[:, :, lane(k)] + span * a * dec[0, :, :, lane(k)] * start
        v8[:, :, lane(k)] = v
        u = jnp.sum(dec[3, :, :, lane(k)] * v, axis=1, keepdims=True)
        red[:, pl.ds(2 * lanes + k, 1), :] = u

        def emit(i, h, a=a, c=c, skip=skip, k=k):
            now = at_step(x32, i, k)
            h = a * h + now[None]
            hall[i, :, :, lane(k)] = h
            y32[k, pl.ds(i, SUB, stride=steps), :] = jnp.sum(c * h, axis=0) + skip * now
            return h

        lax.fori_loop(0, steps, emit, start, unroll=16)
        mb[:, lane(k)] = y32[k].astype(BF16)

    def rs(src, dst, peer, index):
        copy = pltpu.make_async_remote_copy(
            src_ref=src,
            dst_ref=dst,
            send_sem=rs_s,
            recv_sem=rs_r.at[index],
            device_id=peer,
            device_id_type=MESH,
        )
        copy.start()

    at_x1, at_az1, at_az2 = 0, A_PIECES, 2 * A_PIECES
    at_bz1 = at_az2 + 1
    at_bz2 = at_bz1 + B_PIECES
    at_x3 = at_bz2 + B_PIECES
    done = {"x1": 0, "az1": 0, "bz1": 0, "bz2": 0}

    def following(name):
        done[name] += 1
        return done[name] - 1

    def a_place(i):
        return unit * sum(A_SHARES[:i]), unit * A_SHARES[i]

    def a_span(i):
        return pl.ds(*a_place(i))

    def a_halves(i):
        at, width = a_place(i)
        return pl.ds(at, width // 2), pl.ds(at + width // 2, width // 2)

    def a_half(i):
        at, width = a_place(i)
        return pl.ds(at // 2, width // 2)

    def b_place(i):
        return unit * sum(B_SHARES[:i]), unit * B_SHARES[i]

    def b_span(i, base=split):
        at, width = b_place(i)
        return pl.ds(base + at, width)

    def b_halves(i):
        at, width = b_place(i)
        return pl.ds(split + at, width // 2), pl.ds(split + at + width // 2, width // 2)

    def b_half(i):
        at, width = b_place(i)
        return pl.ds(at // 2, width // 2)

    w_copy.wait()

    def project(lo, hi):
        p = jnp.dot(mb[...], w_v[:, lo:hi], preferred_element_type=F32)
        part[:, :, :, lo:hi] = p.astype(BF16).reshape(NX, NZ, rows, hi - lo)

    def send_z1(i):
        h1, h2 = b_halves(i)
        rs(part.at[:, zo, :, h1], bl1.at[:, :, b_half(i)], to_r, at_bz1 + i)
        rs(part.at[:, zo, :, h2], br1.at[:, :, b_half(i)], to_l, at_bz1 + i)

    middle = split + b_place(2)[0]
    project(split, middle)
    send_z1(0)
    send_z1(1)
    project(middle, dim)
    for i in range(2, B_PIECES):
        send_z1(i)
    project(0, split)
    for i in range(A_PIECES):
        rs(part.at[ox, :, :, a_span(i)], bx1.at[:, :, a_span(i)], to_x, at_x1 + i)

    wait_bytes(ag_r.at[late_a], 6 * rows, quarter)
    ins[4].wait()

    def project_back(lo, hi, fresh=False):
        left = og[:, :, :, lo:hi].reshape(tok, hi - lo)
        for k in range(lanes):
            got = lax.dot_general(
                left,
                w_v[k * LANE : (k + 1) * LANE, lo:hi],
                (((1,), (1,)), ((), ())),
                preferred_element_type=F32,
            )
            g32[k] = got if fresh else g32[k] + got

    project_back(0, half, True)

    def merge(ref, got):
        ref[...] = (ref[...].astype(F32) + got[...].astype(F32)).astype(BF16)

    def take_b_z1():
        i = following("bz1")
        h1, h2 = b_halves(i)
        wait_bytes(rs_r.at[at_bz1 + i], 2 * NX * rows, b_place(i)[1] // 2)
        merge(part.at[:, zr, :, h1], bl1.at[:, :, b_half(i)])
        rs(part.at[:, zr, :, b_span(i)], bl2.at[:, :, b_span(i, 0)], to_r, at_bz2 + i)
        merge(part.at[:, zl, :, h2], br1.at[:, :, b_half(i)])
        rs(part.at[:, zl, :, b_span(i)], br2.at[:, :, b_span(i, 0)], to_l, at_bz2 + i)

    def take_x1():
        i = following("x1")
        here = bx1.at[:, :, a_span(i)]
        pltpu.make_async_copy(here, here, rs_r.at[at_x1 + i]).wait()
        h1, h2 = a_halves(i)
        merge(part.at[xl, zo, :, a_span(i)], here.at[zo])
        rs(part.at[xl, zo, :, h1], al1.at[:, a_half(i)], to_r, at_az1 + i)
        rs(part.at[xl, zo, :, h2], ar1.at[:, a_half(i)], to_l, at_az1 + i)
        merge(part.at[xl, zr, :, a_span(i)], here.at[zr])
        merge(part.at[xl, zl, :, a_span(i)], here.at[zl])

    def take_z1():
        i = following("az1")
        h1, h2 = a_halves(i)
        wait_bytes(rs_r.at[at_az1 + i], 2 * rows, a_place(i)[1] // 2)
        merge(part.at[xl, zr, :, h1], al1.at[:, a_half(i)])
        rs(part.at[xl, zr, :, a_span(i)], al2.at[:, a_span(i)], to_r, at_az2)
        merge(part.at[xl, zl, :, h2], ar1.at[:, a_half(i)])
        rs(part.at[xl, zl, :, a_span(i)], ar2.at[:, a_span(i)], to_l, at_az2)

    def total3(ref, left, right):
        return ref[...].astype(F32) + left[...].astype(F32) + right[...].astype(F32)

    def take_b_z2():
        i = following("bz2")
        wait_bytes(rs_r.at[at_bz2 + i], 2 * NX * rows, b_place(i)[1])
        far_part = part.at[ox, z, :, b_span(i)]
        here = b_span(i, 0)
        far_part[...] = total3(far_part, bl2.at[ox, :, here], br2.at[ox, :, here]).astype(BF16)
        rs(far_part, bx3.at[:, here], to_x, at_x3)

    take_b_z1()

    wait_bytes(ag_r.at[late_b], 7 * rows, quarter)

    project_back(half, half + quarter)
    x_ob2.wait_recv()
    project_back(half + quarter, dim)

    for k in range(lanes):
        g32[k] = g32[k].astype(BF16).astype(F32)
        sk = jnp.sum(g32[k] * x32[k], axis=0, keepdims=True)
        red[:, pl.ds(4 * lanes + k, 1), :] = jnp.broadcast_to(sk[None], (modes, 1, LANE))

    hm = modes // 2
    zh = jnp.zeros((hm, SUB, LANE), F32)
    pm = place[:hm]
    for m0 in (0, hm):
        ms = pl.ds(m0, hm)
        for k in range(lanes):
            lv = lane(k)
            a = a8[ms, :, lv]

            def back(j, carry, a=a, k=k, lv=lv, ms=ms):
                h, gs, mloc = carry
                i = steps - 1 - j
                now = at_step(g32, i, k)[None]
                held = hall[i, ms, :, lv]
                h = a * h + now
                return h, gs + now * held, mloc + h * held

            end, gs, mloc = lax.fori_loop(0, steps, back, (zh, zh, zh), unroll=16)
            for at, s in enumerate((1, 2, 4)):
                moved = jnp.where(pm < SUB - s, pltpu.roll(end, SUB - s, 1), 0.0)
                end = end + dec[at, ms, :, lv] * moved
            ex = jnp.where(pm < SUB - 1, pltpu.roll(end, SUB - 1, 1), 0.0)
            ex8[ms, :, lv] = ex
            first = jnp.where(pm == 0, end, 0.0)
            r_own[ms, lv] = jnp.sum(first, axis=1)
            for at, value in ((0, gs), (1, mloc + ex * v8[ms, :, lv]), (3, first)):
                red[ms, pl.ds(at * lanes + k, 1), :] = jnp.sum(value, axis=1, keepdims=True)

        @pl.loop(m0, m0 + hm)
        def _(peer):
            @pl.when(peer != me)
            def _():
                p_copy(peer).start()

        if m0 == 0:
            take_x1()
            take_b_z1()

    sib_back = sib_copy(2, r_own, r_sib)
    sib_back.start()
    rr[me] = red[me]

    sib_back.wait_recv()
    mine_r, sib_r_half = r_own[:, my_half], r_sib[:, my_half]
    r_early = jnp.where(core == 0, mine_r, sib_r_half)
    r_late = jnp.where(core == 0, sib_r_half, mine_r)
    r_pair[...] = (r_early + far_half * r_late).astype(BF16)

    @pl.loop(0, pair)
    def _(peer):
        r_copy(peer, pair).start()


    take_x1()
    take_b_z1()
    take_b_z1()

    take_b_z2()

    take_z1()

    wait_all(rr.at[:, pl.ds(0, 5 * lanes)], p_rs)

    far_me = far4[me]

    def owner(j, carry):
        lam, gsum, msum, ksum = carry
        sender = n_ctx - 1 - j
        got = rr[sender]
        gsum = gsum + got[:lanes]
        msum = msum + got[lanes : 2 * lanes] + lam * got[2 * lanes : 3 * lanes]
        ksum = ksum + got[4 * lanes : 5 * lanes]
        return far_me * lam + got[3 * lanes : 4 * lanes], gsum, msum, ksum

    zl4 = jnp.zeros((lanes, LANE), F32)
    _, gsum, msum, ksum = lax.fori_loop(0, n_ctx, owner, (zl4, zl4, zl4, zl4))
    fin[me, pl.ds(0, lanes), :] = gsum
    fin[me, pl.ds(lanes, lanes), :] = msum
    others(lambda peer: q_copy(peer).start())
    scale = 1.0 / math.sqrt(seq)
    gskip_ref[...] = ksum * scale

    take_b_z2()

    take_z1()

    def join_back(j, total):
        sender = pairs - 1 - j
        r_copy(0, sender).wait_recv()
        return far_half * far_half * total + r_recv[sender].astype(F32)

    l_t[:, my_half] = lax.fori_loop(0, pairs - 1 - pair, join_back, none)
    sib_l = sib_copy(3, l_t.at[:, my_half], l_t.at[:, my_half])
    sib_l.start()

    take_b_z2()

    take_b_z2()

    sib_l.wait_recv()
    l_in = jnp.where(core == 1, l_t[...], far * l_t[...] + r_sib[...])
    for n in range(modes):
        in8[n] = jnp.broadcast_to(l_in[n : n + 1], (SUB, chans))

    for k in range(lanes):
        a, c = a8[:, :, lane(k)], c8[:, :, lane(k)]
        skip = skip_ref[:, lane(k)]
        start = ex8[:, :, lane(k)] + dec[3, :, :, lane(k)] * in8[:, :, lane(k)]

        def emit_back(j, h, a=a, c=c, skip=skip, k=k):
            i = steps - 1 - j
            now = at_step(g32, i, k)
            h = a * h + now[None]
            y32[k, pl.ds(i, SUB, stride=steps), :] = jnp.sum(c * h, axis=0) + skip * now
            return h

        lax.fori_loop(0, steps, emit_back, start, unroll=16)
        gi_ref[:, lane(k)] = y32[k].astype(BF16)

    wait_bytes(rs_r.at[at_az2], 2 * rows, split)
    out_ref[:, :split] = (
        total3(part.at[xl, z, :, pl.ds(0, split)], al2, ar2) + bx1[z].astype(F32)
    ).astype(BF16)

    wait_bytes(rs_r.at[at_x3], rows, dim - split)
    out_ref[:, split:] = (
        total3(part.at[xl, z, :, pl.ds(split, dim - split)], bl2.at[xl], br2.at[xl])
        + bx3[...].astype(F32)
    ).astype(BF16)


    wait_all(fin, q_rs)

    for k in range(lanes):
        rate = rate_t[:, lane(k)]
        gr = jnp.sum(fin[:, pl.ds(k, 1), :], axis=1)
        ml = jnp.sum(fin[:, pl.ds(lanes + k, 1), :], axis=1)
        gres_ref[:, lane(k)] = gr * (jnp.sqrt(2.0 * rate) * scale)
        glog_ref[:, lane(k)] = c_t[:, lane(k)] * ((0.5 + rate) * gr - rate * ml) * scale


    sent = w_v.at[pl.ds(0, tok - rows)]
    pltpu.make_async_copy(sent, sent, ag_s).wait()
    pltpu.make_async_copy(sent, sent, rs_s).wait()
    wait_bytes(sib_s, rows, 5 * chans)
    rest = s_recv.at[pl.ds(0, 2 * n_y - 1)]
    pltpu.make_async_copy(rest, rest, s_ss).wait()

    @pl.loop(0, pair)
    def _(peer):
        r_copy(peer, pair).wait_send()

    wait_all(rr.at[:, pl.ds(0, 5 * lanes)], p_ss)
    wait_all(fin, q_ss)


def store(*refs):
    n = len(refs) // 2
    copies = [pltpu.make_async_copy(refs[i], refs[n + i], refs[-1].at[i]) for i in range(n)]
    for copy in copies:
        copy.start()
    for copy in copies:
        copy.wait()


def per_device(inputs, residue, log_rate, skip, out_weight, out_grad):
    n_ctx = lax.axis_size("ctx")
    tok, chans = inputs.shape
    modes = residue.shape[1]
    dim = out_weight.shape[1]
    rows = tok // (NX * NZ)
    steps = tok // SUB
    lanes = chans // LANE
    split = dim // SHARES * sum(A_SHARES)
    b_cols = dim - split
    wide = (modes, SUB, chans)
    flat = (modes, chans)
    packed = -(-5 * lanes // SUB) * SUB
    anywhere = pl.BlockSpec(memory_space=pl.ANY)
    dma = pltpu.SemaphoreType.DMA
    results = (
        jax.ShapeDtypeStruct((rows, dim), BF16),
        jax.ShapeDtypeStruct((tok, chans), BF16),
        jax.ShapeDtypeStruct(flat, F32),
        jax.ShapeDtypeStruct(flat, F32),
        jax.ShapeDtypeStruct((lanes, LANE), F32),
    )
    vmem = pl.BlockSpec(memory_space=pltpu.VMEM)
    held = pl.pallas_call(
        functools.partial(kernel, tok * n_ctx, n_ctx),
        out_shape=tuple(pltpu.VMEM(r.shape, r.dtype) for r in results),
        in_specs=[anywhere] * 6,
        out_specs=(vmem,) * 5,
        scratch_shapes=[
            pltpu.VMEM((tok, chans), BF16),
            pltpu.VMEM(flat, F32),
            pltpu.VMEM(flat, F32),
            pltpu.VMEM((1, chans), F32),
            pltpu.VMEM((chans, dim), BF16),
            pltpu.VMEM((NX, NZ, rows, dim), BF16),
            pltpu.VMEM((NX, NZ, rows, dim), BF16),
            pltpu.VMEM((steps, *wide), F32),
            pltpu.VMEM((lanes, tok, LANE), F32),
            pltpu.VMEM((lanes, tok, LANE), F32),
            pltpu.VMEM((lanes, tok, LANE), F32),
            pltpu.VMEM((tok, chans), BF16),
            pltpu.VMEM(flat, F32),
            pltpu.VMEM(flat, F32),
            pltpu.VMEM((modes, lanes, LANE), F32),
            pltpu.VMEM(wide, F32),
            pltpu.VMEM(wide, F32),
            pltpu.VMEM(wide, F32),
            pltpu.VMEM(wide, F32),
            pltpu.VMEM(wide, F32),
            pltpu.VMEM(wide, F32),
            pltpu.VMEM(flat, F32),
            pltpu.VMEM(flat, F32),
            pltpu.VMEM((n_ctx // 2, modes, chans), BF16),
            pltpu.VMEM(flat, F32),
            pltpu.VMEM(flat, F32),
            pltpu.VMEM((modes, chans // 2), BF16),
            pltpu.VMEM((n_ctx // 2, modes, chans // 2), BF16),
            pltpu.VMEM(flat, F32),
            pltpu.VMEM((modes, packed, LANE), F32),
            pltpu.VMEM((n_ctx, packed, LANE), F32),
            pltpu.VMEM((5, *wide), F32),
            pltpu.VMEM((n_ctx, 2 * lanes, LANE), F32),
            pltpu.VMEM((NZ, rows, split), BF16),
            pltpu.VMEM((rows, split // 2), BF16),
            pltpu.VMEM((rows, split // 2), BF16),
            pltpu.VMEM((rows, split), BF16),
            pltpu.VMEM((rows, split), BF16),
            pltpu.VMEM((NX, rows, b_cols // 2), BF16),
            pltpu.VMEM((NX, rows, b_cols // 2), BF16),
            pltpu.VMEM((NX, rows, b_cols), BF16),
            pltpu.VMEM((NX, rows, b_cols), BF16),
            pltpu.VMEM((rows, b_cols), BF16),
            pltpu.SemaphoreType.REGULAR,
            dma((5,)),
            dma,
            dma,
            dma((15,)),
            dma,
            dma((2 * (A_PIECES + B_PIECES) + 2,)),
            dma,
            dma((2,)),
            dma((n_ctx // 2,)),
            dma((n_ctx // 2,)),
            dma,
            dma((4,)),
            *[dma] * 4,
        ],
        compiler_params=pltpu.CompilerParams(
            collective_id=0, has_side_effects=True, vmem_limit_bytes=56 * 1024 * 1024
        ),
    )(inputs, residue.T, log_rate.T, skip.reshape(1, chans), out_weight, out_grad)
    out, gi, gres, glog, gskip = pl.pallas_call(
        store,
        out_shape=results,
        in_specs=[vmem] * 5,
        out_specs=(anywhere,) * 5,
        scratch_shapes=[dma((5,))],
        compiler_params=pltpu.CompilerParams(vmem_limit_bytes=2 * 1024 * 1024),
    )(*held)
    return out, gi, gres.T, glog.T, gskip.reshape(chans)


def solution(mesh):
    return jax.shard_map(
        per_device,
        mesh=mesh,
        in_specs=(
            P("ctx", "tp"),
            P("tp", None),
            P("tp", None),
            P("tp"),
            P("tp", None),
            P(("ctx", "tp"), None),
        ),
        out_specs=(P(("ctx", "tp"), None), P("ctx", "tp"), P("tp", None), P("tp", None), P("tp")),
        check_vma=False,
    )
```
